128 devices in a mesh: dp: 4 (over x), vocab: 32 (over z, y, core).
Axes of the slice: x: 4, y: 4, z: 4, core: 2. Of those that a mesh axis runs over, the one named last changes fastest.
Arguments:
- hidden: bfloat16 [1024, 2304], P('dp', 'vocab'), may hold values from -6 to 6
- embed: bfloat16 [128000, 2304], P('vocab')
- token_ids: int32 [1024], P('dp'), may hold values from 0 to 127999
- lookup_cot: bfloat16 [1024, 2304], P('dp', 'vocab'), may hold values from -0.15625 to 0.15625
- teacher_ids: int32 [1024, 64], P(('dp', 'vocab')), may hold values from 0 to 127999, as said below
- teacher_logits: float32 [1024, 64], P(('dp', 'vocab')), may hold values from -8 to 8
Outputs:
- hidden_grad: bfloat16 [1024, 2304], P('dp', 'vocab')
- embed_grad: bfloat16 [128000, 2304], P('vocab', 'dp')
- divergence: float32 [1024], P(('dp', 'vocab'))
The draws below stay inside these ranges and needn't reach their ends.
Inputs may be any that keep to these rules, and one draw needn't show every extreme that they name: `teacher_ids`: each token's 64 teacher ids are different.
All inputs are finite; a program needn't handle non-finite values.
Results may differ from the reference program's by a relative error of at most 0.0043.
The reference program's roundings to bfloat16 on the way count: a program that leaves them out, or rounds other values in their place, can miss the bound.
Values may be sent and summed in bfloat16 or wider, within the bound.
No kernel may reach another device: no remote copies, remote signals or barrier semaphores. Data moves between devices by JAX's collectives and lax.ppermute only.
A program may use at most 192 MiB of HBM per device.

```python
import math
import jax
import jax.numpy as jnp
import numpy as np
from jax import lax

D = 2304
VOCAB = 128000
TOP = 64
TOKENS = 1024
N_VOCAB = 32


def draw_embed(key, part):
    key = jax.random.fold_in(key, 7)
    rows = jnp.arange(VOCAB, dtype=jnp.float32)[:, None] / VOCAB
    base = jax.random.normal(key, (VOCAB, D), jnp.float32)
    scale = 0.03 * (1.0 + rows)
    return (base * scale).astype(jnp.bfloat16)


def draw_teacher_ids(key, part):
    key = jax.random.fold_in(key, 11)
    first_key, step_key = jax.random.split(key)
    start = jax.random.randint(first_key, (TOKENS, 1), 0, VOCAB, dtype=jnp.int32)
    stride_top = max(2, VOCAB // TOP)
    steps = jax.random.randint(step_key, (TOKENS, TOP), 1, stride_top, dtype=jnp.int32)
    offsets = jnp.cumsum(steps, axis=1) - steps[:, :1]
    return ((start + offsets) % VOCAB).astype(jnp.int32)


def place_ends(values, rng, least, largest):
    shape = values.shape
    place = [jax.random.randint(jax.random.fold_in(rng, axis), (), 0, shape[axis]) for axis in range(len(shape))]
    values = values.at[tuple(place)].set(least)
    longest = shape.index(max(shape))
    place[longest] = (place[longest] + 1) % shape[longest]
    return values.at[tuple(place)].set(largest)


def levels(own_key, shape, shards, low, high):
    factor_of = 1.0
    for dim, shards_of in shards:
        draws = jax.random.uniform(jax.random.fold_in(jax.random.fold_in(own_key, 6), dim), (shards_of,), jnp.float32, low / len(shards), high / len(shards))
        factor_of = factor_of * jnp.repeat(jnp.exp(draws), shape[dim] // shards_of).reshape((-1,) + (1,) * (len(shape) - 1 - dim))
    return factor_of


def wide_ids(key, dims, count, lean):
    weights = [min(1 << octave, count + 1 - (1 << octave)) * (1 << 20) // math.isqrt((1 << octave) ** lean) + 1 for octave in range((count + 1).bit_length()) if 1 << octave <= count]
    spread = 1 + sum(weights) // (1 << 30)
    listing = np.cumsum(np.array([max(1, weight // spread) for weight in weights]))
    ticket = jax.random.randint(jax.random.fold_in(key, 1), dims, 0, int(listing[len(weights) - 1]))
    start = jnp.left_shift(1, jnp.searchsorted(jnp.asarray(listing, jnp.int32), ticket, side="right").astype(jnp.int32))
    standing = start - 1 + jax.random.randint(jax.random.fold_in(key, 4), dims, 0, 1 << 30) % jnp.minimum(start, count + 1 - start)
    return jax.random.permutation(jax.random.fold_in(key, 2), count)[standing].astype(jnp.int32)


def gaussian(rng, dims, width, bound, cuts=(), held_as=jnp.bfloat16):
    values = width * jax.random.normal(rng, dims, jnp.float32)
    if cuts:
        values = values * levels(rng, dims, cuts, -0.22, 0.18)
    return jnp.clip(values, -bound, bound).astype(held_as)


def setup_inputs(seed: int = 0) -> dict:
    keys = jax.random.split(jax.random.key(seed), 7)
    hidden = gaussian(keys[0], (TOKENS, D), 1.0, 6.0, ((0, 4), (1, 32)))
    embed = draw_embed(jax.random.fold_in(keys[6], 71), 0)
    token_ids = place_ends(wide_ids(keys[2], (TOKENS,), VOCAB, 2), jax.random.fold_in(keys[2], 3), 0, VOCAB - 1).astype(jnp.int32)
    lookup_cot = gaussian(keys[3], (TOKENS, D), 0.01, 0.15625, ((0, 4), (1, 32)))
    teacher_ids = draw_teacher_ids(jax.random.fold_in(keys[6], 71), 0)
    teacher_logits = gaussian(keys[5], (TOKENS, TOP), 2.0, 8.0, ((0, 128),), jnp.float32)
    return {"hidden": hidden, "embed": embed, "token_ids": token_ids, "lookup_cot": lookup_cot, "teacher_ids": teacher_ids, "teacher_logits": teacher_logits}


soft_cap = 30.0
loss_scale = 16.0

def reference(hidden, embed, token_ids, lookup_cot, teacher_ids, teacher_logits):
    rows_block = VOCAB // N_VOCAB
    blocks = embed.reshape(N_VOCAB, rows_block, D)
    indices = jnp.arange(N_VOCAB, dtype=jnp.int32)
    teacher_prob = jax.nn.softmax(teacher_logits.astype(jnp.float32), axis=1)

    def capped_logits(weights):
        raw = lax.dot_general(hidden, weights, (((1,), (1,)), ((), ())), preferred_element_type=jnp.float32)
        return soft_cap * jnp.tanh(raw / soft_cap)

    def first_pass(carry, inputs):
        weights, block_index = inputs
        logits = capped_logits(weights)
        column = teacher_ids - block_index * rows_block
        inside = (column >= 0) & (column < rows_block)
        picked = jnp.take_along_axis(logits, jnp.clip(column, 0, rows_block - 1), axis=1)
        total, term = carry
        total = total + lax.optimization_barrier(jnp.sum(jnp.exp(logits), axis=1))
        term = term + lax.optimization_barrier(jnp.sum(jnp.where(inside, teacher_prob * picked, 0.0), axis=1))
        return ((total, term), None)
    zeros = jnp.zeros((TOKENS,), jnp.float32)
    (total, term), _ = lax.scan(first_pass, (zeros, zeros), (blocks, indices))
    divergence = lax.optimization_barrier(jnp.sum(teacher_prob * jnp.log(teacher_prob), axis=1)) - term + jnp.log(total)
    lookup_scale = math.sqrt(D)
    token_index = jnp.arange(TOKENS, dtype=jnp.int32)[:, None]

    def second_pass(carry, inputs):
        weights, block_index = inputs
        logits = capped_logits(weights)
        column = teacher_ids - block_index * rows_block
        inside = (column >= 0) & (column < rows_block)
        target = jnp.zeros((TOKENS, rows_block), jnp.float32).at[token_index, jnp.clip(column, 0, rows_block - 1)].add(jnp.where(inside, teacher_prob, 0.0))
        ratio = logits / soft_cap
        grads = (loss_scale * (jnp.exp(logits) / total[:, None] - target) * (1.0 - ratio * ratio)).astype(jnp.bfloat16)
        carry = carry + jnp.dot(grads, weights, preferred_element_type=jnp.float32)
        row_ids = block_index * rows_block + jnp.arange(rows_block, dtype=jnp.int32)
        onehot = (token_ids[:, None] == row_ids[None, :]).astype(jnp.bfloat16)
        first_term = lax.dot_general(grads, hidden, (((0,), (0,)), ((), ())), preferred_element_type=jnp.float32)
        second_term = lax.dot_general(onehot, lookup_cot, (((0,), (0,)), ((), ())), preferred_element_type=jnp.float32)
        return (carry, (first_term + lookup_scale * second_term).astype(jnp.bfloat16))
    hidden_sum, row_grads = lax.scan(second_pass, jnp.zeros((TOKENS, D), jnp.float32), (blocks, indices))
    return (hidden_sum.astype(jnp.bfloat16), row_grads.reshape(VOCAB, D), divergence)
```

```python
import functools
import math

import jax
import jax.numpy as jnp
from jax import lax
from jax.experimental import pallas as pl
from jax.experimental.pallas import tpu as pltpu
from jax.sharding import PartitionSpec as P

SOFT_CAP = 30.0
LOSS_SCALE = 16.0
TILE = 512
BLOCK = 256
FAST_SLOTS = 4
FAR = 1 << 30


def dot_nn(a, b):
    return lax.dot_general(a, b, (((1,), (0,)), ((), ())), preferred_element_type=jnp.float32)


def dot_nt(a, b):
    return lax.dot_general(a, b, (((1,), (1,)), ((), ())), preferred_element_type=jnp.float32)


def dot_tn(a, b):
    return lax.dot_general(a, b, (((0,), (0,)), ((), ())), preferred_element_type=jnp.float32)


def teacher_kernel(tiles, blocks, place, pack, ids, prob, counts):
    offset = place[0]
    flipped = pack[...].T
    top = flipped.shape[0] // 2
    scores = flipped[:top]
    local = flipped[top:].astype(jnp.int32) - offset
    raised = jnp.exp(scores - jnp.max(scores, axis=0, keepdims=True))
    ids[...] = local
    prob[...] = raised / jnp.sum(raised, axis=0, keepdims=True)
    for tile in range(tiles):
        low = tile * TILE
        inside = ((local >= low) & (local < low + TILE)).astype(jnp.int32)
        held = jnp.sum(inside, axis=0, keepdims=True)
        for block in range(blocks):
            counts[tile * blocks + block] = jnp.max(held[:, block * BLOCK : (block + 1) * BLOCK])


def lookup_kernel(rows, place, tokens, cot, packed_cot, packed_ids, chunks):
    offset = place[0]
    count = tokens.shape[1]
    blocks = count // BLOCK
    local = tokens[...] - offset
    inside = (local >= 0) & (local < rows)
    hit = jnp.broadcast_to(jnp.where(inside, 1.0, 0.0), (8, count))
    before = lax.broadcasted_iota(jnp.int32, (count, count), 0)
    after = lax.broadcasted_iota(jnp.int32, (count, count), 1)
    upto = jnp.where(before <= after, 1.0, 0.0).astype(jnp.bfloat16)
    running = dot_nn(hit.astype(jnp.bfloat16), upto)[0:1].astype(jnp.int32)
    rank = jnp.where(inside, running - 1, -1)
    total = jnp.max(running)
    chunks[0] = (total + BLOCK - 1) // BLOCK
    safe = jnp.where(inside, local, 0)
    high = jnp.broadcast_to((safe >> 6).astype(jnp.float32), (8, count)).astype(jnp.bfloat16)
    low = jnp.broadcast_to((safe & 63).astype(jnp.float32), (8, count)).astype(jnp.bfloat16)
    for chunk in range(blocks):

        @pl.when(chunk * BLOCK < total)
        def _():
            slot = lax.broadcasted_iota(jnp.int32, (BLOCK, count), 0) + chunk * BLOCK
            chosen = jnp.where(slot == rank, 1.0, 0.0).astype(jnp.bfloat16)
            taken = jnp.zeros((cot.shape[1], BLOCK), jnp.float32)
            for block in range(blocks):
                span = slice(block * BLOCK, (block + 1) * BLOCK)
                taken = taken + dot_nt(cot[block], chosen[:, span])
            packed_cot[chunk] = taken.astype(jnp.bfloat16)
            row = dot_nt(high, chosen)[0:1] * 64.0 + dot_nt(low, chosen)[0:1]
            used = dot_nt(hit.astype(jnp.bfloat16), chosen)[0:1] > 0.5
            packed_ids[chunk] = jnp.where(used, row.astype(jnp.int32), -1)


def next_slot(relative, prob, last):
    following = jnp.min(jnp.where(relative > last, relative, FAR), axis=0, keepdims=True)
    chance = jnp.sum(jnp.where(relative == following, prob, 0.0), axis=0, keepdims=True)
    return following, chance


def logit_kernel(blocks, rows, place, counts, embed, hidden, ids, prob, squashed, sums):
    step = pl.program_id(0)
    last_step = pl.num_programs(0) - 1
    mine = place[1]

    @pl.when(step == 0)
    def _():
        sums[...] = jnp.zeros_like(sums)

    def work(size):
        table = embed[0:size]
        for block in range(blocks):
            span = slice(block * BLOCK, (block + 1) * BLOCK)
            raw = dot_nn(table, hidden[block])
            ratio = jnp.tanh(raw * (1.0 / SOFT_CAP))
            squashed[0:size, span] = ratio
            raised = jnp.exp(ratio * SOFT_CAP)
            sums[0:8, span] += jnp.sum(raised.reshape(size // 8, 8, BLOCK), axis=0)
        own = pl.ds(pl.multiple_of(mine * BLOCK, BLOCK), BLOCK)
        row = lax.broadcasted_iota(jnp.int32, (size, BLOCK), 0)

        def pick(_, last):
            relative = ids[:, own] - step * TILE
            following, chance = next_slot(relative, prob[:, own], last)
            found = jnp.where(row == following, squashed[0:size, own], 0.0)
            sums[8:16, 0:BLOCK] += jnp.sum(found.reshape(size // 8, 8, BLOCK), axis=0) * (
                chance * SOFT_CAP
            )
            return following

        lax.fori_loop(0, counts[step * blocks + mine], pick, jnp.full((1, BLOCK), -1, jnp.int32))

    tail = rows - (rows - 1) // TILE * TILE

    @pl.when(step < last_step)
    def _():
        work(TILE)

    @pl.when(step == last_step)
    def _():
        work(tail)


def grad_kernel(
    blocks,
    rows,
    place,
    counts,
    chunks,
    embed,
    squashed,
    inverse,
    ids,
    prob,
    hidden,
    packed_cot,
    packed_ids,
    embed_grad,
    hidden_grad,
    grads,
    total_grad,
):
    step = pl.program_id(0)
    last_step = pl.num_programs(0) - 1
    mine = place[1]
    width = embed.shape[1]

    @pl.when(step == 0)
    def _():
        total_grad[...] = jnp.zeros_like(total_grad)

    def work(size):
        row = lax.broadcasted_iota(jnp.int32, (size, BLOCK), 0)
        for block in range(blocks):
            span = slice(block * BLOCK, (block + 1) * BLOCK)
            relative = ids[:, span] - step * TILE
            chances = prob[:, span]
            last = jnp.full((1, BLOCK), -1, jnp.int32)
            target = jnp.zeros((size, BLOCK), jnp.float32)
            for _ in range(FAST_SLOTS):
                last, chance = next_slot(relative, chances, last)
                target = jnp.where(row == last, chance * LOSS_SCALE, target)
            ratio = squashed[0:size, span]
            share = jnp.exp(ratio * SOFT_CAP) * inverse[:, span]
            grads[block, 0:size] = ((share - target) * (1.0 - ratio * ratio)).astype(jnp.bfloat16)

            def more(_, last):
                last, chance = next_slot(ids[:, span] - step * TILE, prob[:, span], last)
                ratio = squashed[0:size, span]
                share = jnp.exp(ratio * SOFT_CAP) * inverse[:, span]
                fresh = (share - chance * LOSS_SCALE) * (1.0 - ratio * ratio)
                held = grads[block, 0:size].astype(jnp.float32)
                grads[block, 0:size] = jnp.where(row == last, fresh, held).astype(jnp.bfloat16)
                return last

            lax.fori_loop(FAST_SLOTS, counts[step * blocks + block], more, last)

        spread = jnp.zeros((hidden.shape[1], size), jnp.float32)
        for block in range(blocks):
            spread = spread + dot_nt(hidden[block], grads[block, 0:size])
        embed_grad[:, 0:size] = spread.astype(jnp.bfloat16)

        def lookup(chunk, _):
            column = lax.broadcasted_iota(jnp.int32, (size, BLOCK), 0) + step * TILE
            onehot = jnp.where(column == packed_ids[chunk], math.sqrt(width), 0.0)
            return _ + dot_nt(packed_cot[chunk], onehot.astype(jnp.bfloat16))

        spread = lax.fori_loop(0, chunks[0], lookup, spread)
        embed_grad[:, 0:size] = spread.astype(jnp.bfloat16)
        total_grad[...] += dot_tn(grads[mine, 0:size], embed[0:size])

    tail = rows - (rows - 1) // TILE * TILE

    @pl.when(step < last_step)
    def _():
        work(TILE)

    @pl.when(step == last_step)
    def _():
        work(tail)
        hidden_grad[...] = total_grad[...].T


def smem():
    return pl.BlockSpec(memory_space=pltpu.SMEM)


def whole(shape):
    return pl.BlockSpec(shape, lambda *_: (0,) * len(shape))


def per_device(hidden, embed, token_ids, lookup_cot, teacher_ids, teacher_logits):
    rows, width = embed.shape
    dp = lax.axis_size("dp")
    vocab = lax.axis_size("vocab")
    dp_index = lax.axis_index("dp")
    vocab_index = lax.axis_index("vocab")
    here = hidden.shape[0]
    thin = hidden.shape[1]
    tokens = here * dp
    top = teacher_ids.shape[1]
    tiles = pl.cdiv(rows, TILE)
    share = here // vocab
    columns = width // dp
    both = ("dp", "vocab")
    place = jnp.stack([vocab_index * rows, dp_index]).astype(jnp.int32)

    pack = lax.all_gather(
        jnp.concatenate([teacher_logits, teacher_ids.astype(jnp.float32)], axis=1),
        both,
        axis=0,
        tiled=True,
    )
    hidden_all = lax.all_gather(hidden.T, both, axis=0, tiled=True).reshape(dp, width, here)
    token_all = lax.all_gather(token_ids, "dp", axis=0, tiled=True).reshape(1, tokens)
    per = vocab // dp
    route = [
        (i * vocab + j, (j // per) * vocab + i * per + j % per)
        for i in range(dp)
        for j in range(vocab)
    ]
    moved = lax.ppermute(lookup_cot.T, both, route)
    cot = lax.all_gather(moved, "vocab", axis=0, tiled=True).reshape(dp, columns, here)

    ids, prob, counts = pl.pallas_call(
        functools.partial(teacher_kernel, tiles, dp),
        out_shape=(
            jax.ShapeDtypeStruct((top, tokens), jnp.int32),
            jax.ShapeDtypeStruct((top, tokens), jnp.float32),
            jax.ShapeDtypeStruct((tiles * dp,), jnp.int32),
        ),
        in_specs=[smem(), pl.BlockSpec(memory_space=pltpu.VMEM)],
        out_specs=(
            pl.BlockSpec(memory_space=pltpu.VMEM),
            pl.BlockSpec(memory_space=pltpu.VMEM),
            smem(),
        ),
        name="teacher_prep",
    )(place, pack)

    squashed, sums = pl.pallas_call(
        functools.partial(logit_kernel, dp, rows),
        grid=(tiles,),
        in_specs=[
            smem(),
            smem(),
            pl.BlockSpec((TILE, width), lambda n: (n, 0)),
            whole((dp, width, here)),
            whole((top, tokens)),
            whole((top, tokens)),
        ],
        out_specs=(
            pl.BlockSpec((TILE, tokens), lambda n: (n, 0)),
            whole((16, tokens)),
        ),
        out_shape=(
            jax.ShapeDtypeStruct((rows, tokens), jnp.float32),
            jax.ShapeDtypeStruct((16, tokens), jnp.float32),
        ),
        compiler_params=pltpu.CompilerParams(vmem_limit_bytes=40 << 20),
        cost_estimate=pl.CostEstimate(
            flops=2 * rows * width * tokens,
            bytes_accessed=rows * width * 2 + rows * tokens * 4,
            transcendentals=2 * rows * tokens,
        ),
        name="logits",
    )(place, counts, embed, hidden_all, ids, prob)

    packed_cot, packed_ids, chunks = pl.pallas_call(
        functools.partial(lookup_kernel, rows),
        out_shape=(
            jax.ShapeDtypeStruct((dp, columns, here), jnp.bfloat16),
            jax.ShapeDtypeStruct((dp, 1, here), jnp.int32),
            jax.ShapeDtypeStruct((1,), jnp.int32),
        ),
        in_specs=[
            smem(),
            pl.BlockSpec(memory_space=pltpu.VMEM),
            pl.BlockSpec(memory_space=pltpu.VMEM),
        ],
        out_specs=(
            pl.BlockSpec(memory_space=pltpu.VMEM),
            pl.BlockSpec(memory_space=pltpu.VMEM),
            smem(),
        ),
        name="lookup_prep",
    )(place, token_all, cot)

    parts = jnp.concatenate(
        [jnp.sum(sums[0:8], axis=0), jnp.sum(sums[8:16, 0:here], axis=0)], axis=0
    )
    sums_all = lax.psum(parts, "vocab")
    total = sums_all[0:tokens]
    term = sums_all[tokens:]
    inverse = (LOSS_SCALE / total).reshape(1, tokens)

    embed_grad, hidden_part = pl.pallas_call(
        functools.partial(grad_kernel, dp, rows),
        grid_spec=pltpu.PrefetchScalarGridSpec(
            num_scalar_prefetch=3,
            grid=(tiles,),
            in_specs=[
                pl.BlockSpec((TILE, width), lambda n, *_: (n, 0)),
                pl.BlockSpec((TILE, tokens), lambda n, *_: (n, 0)),
                whole((1, tokens)),
                whole((top, tokens)),
                whole((top, tokens)),
                pl.BlockSpec((dp, columns, here), lambda n, place, *_: (0, place[1], 0)),
                whole((dp, columns, here)),
                whole((dp, 1, here)),
            ],
            out_specs=[
                pl.BlockSpec((columns, TILE), lambda n, *_: (0, n)),
                whole((width, here)),
            ],
            scratch_shapes=[
                pltpu.VMEM((dp, TILE, here), jnp.bfloat16),
                pltpu.VMEM((here, width), jnp.float32),
            ],
        ),
        out_shape=(
            jax.ShapeDtypeStruct((columns, rows), jnp.bfloat16),
            jax.ShapeDtypeStruct((width, here), jnp.float32),
        ),
        compiler_params=pltpu.CompilerParams(vmem_limit_bytes=48 << 20),
        cost_estimate=pl.CostEstimate(
            flops=4 * rows * width * here,
            bytes_accessed=rows * width * 2 + rows * tokens * 4 + rows * columns * 2,
            transcendentals=rows * tokens,
        ),
        name="grads",
    )(place, counts, chunks, embed, squashed, inverse, ids, prob, hidden_all, packed_cot, packed_ids)

    summed = lax.psum_scatter(hidden_part, "vocab", scatter_dimension=0, tiled=True)
    hidden_grad = summed.astype(jnp.bfloat16).T

    own_prob = jax.nn.softmax(teacher_logits, axis=1)
    first = vocab_index * share
    own_total = lax.dynamic_slice_in_dim(total, dp_index * here + first, share, 0)
    own_term = lax.dynamic_slice_in_dim(term, first, share, 0)
    divergence = (
        jnp.sum(own_prob * jnp.log(own_prob), axis=1) - own_term + jnp.log(own_total)
    )
    return (hidden_grad, embed_grad.T, divergence)


def solution(mesh):
    placed = (
        P("dp", "vocab"),
        P("vocab", None),
        P("dp"),
        P("dp", "vocab"),
        P(("dp", "vocab"), None),
        P(("dp", "vocab"), None),
    )
    return jax.shard_map(
        per_device,
        mesh=mesh,
        in_specs=placed,
        out_specs=(P("dp", "vocab"), P("vocab", "dp"), P(("dp", "vocab"))),
        check_vma=False,
    )
```

```python
import functools
import math

import jax
import jax.numpy as jnp
from jax import lax
from jax.experimental import pallas as pl
from jax.experimental.pallas import tpu as pltpu
from jax.sharding import Mesh, PartitionSpec as P

SOFT_CAP = 30.0
LOSS_SCALE = 16.0
BLOCK = 256
HALF = 128
ROW_TILE = 400
COLUMN_TILE = 512
FAST_SLOTS = 4
FAR = 1 << 30
SHIFTS = (0, 1, 3, 2)
RING = ("z", "y", "core")
PLANE = ("z", "y")


def dot_nn(a, b):
    return lax.dot_general(a, b, (((1,), (0,)), ((), ())), preferred_element_type=jnp.float32)


def dot_nt(a, b):
    return lax.dot_general(a, b, (((1,), (1,)), ((), ())), preferred_element_type=jnp.float32)


def dot_tn(a, b):
    return lax.dot_general(a, b, (((0,), (0,)), ((), ())), preferred_element_type=jnp.float32)


def teacher_kernel(rows, place, pack, ids, prob, row_counts, column_counts):
    offset = place[0]
    mine = place[1]
    blocks = pack.shape[1]
    top = pack.shape[3] // 2
    for block in range(blocks):
        source = lax.rem(mine + SHIFTS[block], blocks)
        flipped = pack[:, source].reshape(BLOCK, 2 * top).T
        scores = flipped[:top]
        local = flipped[top:].astype(jnp.int32) - offset
        raised = jnp.exp(scores - jnp.max(scores, axis=0, keepdims=True))
        ids[block] = local
        prob[block] = raised / jnp.sum(raised, axis=0, keepdims=True)
        size, held = (ROW_TILE, row_counts) if block == 0 else (COLUMN_TILE, column_counts)
        for tile in range(pl.cdiv(rows, size)):
            inside = (local >= tile * size) & (local < tile * size + size)
            most = jnp.max(jnp.sum(inside.astype(jnp.int32), axis=0))
            if block == 0:
                held[tile] = most
            else:
                held[tile * (blocks - 1) + block - 1] = most


def lookup_kernel(rows, place, tokens, cot, packed_cot, packed_ids, chunks):
    offset = place[0]
    count = tokens.shape[1]
    blocks = count // BLOCK
    local = tokens[...] - offset
    inside = (local >= 0) & (local < rows)
    hit = jnp.broadcast_to(jnp.where(inside, 1.0, 0.0), (8, count))
    before = lax.broadcasted_iota(jnp.int32, (count, count), 0)
    after = lax.broadcasted_iota(jnp.int32, (count, count), 1)
    upto = jnp.where(before <= after, 1.0, 0.0).astype(jnp.bfloat16)
    running = dot_nn(hit.astype(jnp.bfloat16), upto)[0:1].astype(jnp.int32)
    rank = jnp.where(inside, running - 1, -1)
    total = jnp.max(running)
    chunks[0] = (total + BLOCK - 1) // BLOCK
    safe = jnp.where(inside, local, 0)
    high = jnp.broadcast_to((safe >> 6).astype(jnp.float32), (8, count)).astype(jnp.bfloat16)
    low = jnp.broadcast_to((safe & 63).astype(jnp.float32), (8, count)).astype(jnp.bfloat16)
    for chunk in range(blocks):

        @pl.when(chunk * BLOCK < total)
        def _():
            slot = lax.broadcasted_iota(jnp.int32, (BLOCK, count), 0) + chunk * BLOCK
            chosen = jnp.where(slot == rank, 1.0, 0.0).astype(jnp.bfloat16)
            taken = jnp.zeros((cot.shape[1], BLOCK), jnp.float32)
            for block in range(blocks):
                span = slice(block * BLOCK, (block + 1) * BLOCK)
                taken = taken + dot_nt(cot[block], chosen[:, span])
            packed_cot[chunk] = taken.astype(jnp.bfloat16)
            row = dot_nt(high, chosen)[0:1] * 64.0 + dot_nt(low, chosen)[0:1]
            used = dot_nt(hit.astype(jnp.bfloat16), chosen)[0:1] > 0.5
            packed_ids[chunk] = jnp.where(used, row.astype(jnp.int32), -1)


def next_slot(relative, prob, last):
    following = jnp.min(jnp.where(relative > last, relative, FAR), axis=0, keepdims=True)
    chance = jnp.sum(jnp.where(relative == following, prob, 0.0), axis=0, keepdims=True)
    return following, chance


def join_halves(core, near, far, joined):
    joined[:, pl.ds(pl.multiple_of(core * HALF, HALF), HALF)] = near
    joined[:, pl.ds(pl.multiple_of((1 - core) * HALF, HALF), HALF)] = far


def logit_kernel(blocks, place, embed, *refs):
    near, far = refs[:blocks], refs[blocks : 2 * blocks]
    squashed, total, hidden, sums = refs[2 * blocks :]
    step = pl.program_id(0)
    size = embed.shape[0]

    @pl.when(step == 0)
    def _():
        sums[...] = jnp.zeros_like(sums)
        for block in range(blocks):
            join_halves(place[2], near[block][...], far[block][...], hidden.at[block])

    table = embed[...]
    for block in range(blocks):
        span = slice(block * BLOCK, (block + 1) * BLOCK)
        raw = dot_nn(table, hidden[block])
        ratio = jnp.tanh(raw * (1.0 / SOFT_CAP))
        squashed[:, span] = ratio
        raised = jnp.exp(ratio * SOFT_CAP)
        sums[:, span] += jnp.sum(raised.reshape(size // 8, 8, BLOCK), axis=0)

    @pl.when(step == pl.num_programs(0) - 1)
    def _():
        total[...] = jnp.sum(sums[...], axis=0, keepdims=True)


def place_targets(relative, chances, row):
    last = jnp.full((1, BLOCK), -1, jnp.int32)
    target = jnp.zeros(row.shape, jnp.float32)
    for _ in range(FAST_SLOTS):
        last, chance = next_slot(relative, chances, last)
        target = jnp.where(row == last, chance * LOSS_SCALE, target)
    return target, last


def hidden_grad_kernel(
    place, counts, embed, squashed, parts, ids, prob, grads, keep, give, rows_grad, flipped, term
):
    step = pl.program_id(0)
    size, width = embed.shape
    inverse = LOSS_SCALE / jnp.sum(parts[:, :, 0:BLOCK], axis=0)

    @pl.when(step == 0)
    def _():
        rows_grad[...] = jnp.zeros_like(rows_grad)
        term[...] = jnp.zeros_like(term)

    row = lax.broadcasted_iota(jnp.int32, (size, BLOCK), 0)
    target, last = place_targets(ids[0] - step * size, prob[0], row)
    ratio = squashed[...]
    share = jnp.exp(ratio * SOFT_CAP) * inverse
    grads[...] = ((share - target) * (1.0 - ratio * ratio)).astype(jnp.bfloat16)
    term[...] += jnp.sum((target * ratio).reshape(size // 8, 8, BLOCK), axis=0)

    def more(_, last):
        last, chance = next_slot(ids[0] - step * size, prob[0], last)
        ratio = squashed[...]
        share = jnp.exp(ratio * SOFT_CAP) * inverse
        target = jnp.where(row == last, chance * LOSS_SCALE, 0.0)
        fresh = (share - target) * (1.0 - ratio * ratio)
        held = grads[...].astype(jnp.float32)
        grads[...] = jnp.where(row == last, fresh, held).astype(jnp.bfloat16)
        term[...] += jnp.sum((target * ratio).reshape(size // 8, 8, BLOCK), axis=0)
        return last

    lax.fori_loop(FAST_SLOTS, counts[step], more, last)
    rows_grad[...] += dot_tn(grads[...], embed[...])

    @pl.when(step == pl.num_programs(0) - 1)
    def _():
        core = place[2]
        thin = keep.shape[1] - 8
        for part in range(width // BLOCK):
            span = slice(part * BLOCK, (part + 1) * BLOCK)
            flipped[span, :] = rows_grad[:, span].T
        total = jnp.sum(term[...], axis=0, keepdims=True) * (SOFT_CAP / LOSS_SCALE)
        for chip in range(keep.shape[0]):
            for ref, side in ((keep, core), (give, 1 - core)):
                start = pl.multiple_of((2 * chip + side) * thin, 8)
                ref[chip, 0:thin] = flipped[pl.ds(start, thin)]
                ref[chip, thin : thin + 8] = jnp.broadcast_to(total, (8, BLOCK))


def table_grad_kernel(
    rows,
    width,
    place,
    counts,
    chunks,
    own_grads,
    side_squashed,
    far_squashed,
    side_parts,
    far_parts,
    ids,
    prob,
    packed_cot,
    packed_ids,
    *refs,
):
    blocks = len(SHIFTS)
    near, far = refs[:blocks], refs[blocks : 2 * blocks]
    embed_grad, hidden, grads, inverse = refs[2 * blocks :]
    step = pl.program_id(0)
    last_step = pl.num_programs(0) - 1

    @pl.when(step == 0)
    def _():
        for block in range(blocks):
            join_halves(place[2], near[block][...], far[block][...], hidden.at[block])
        side = LOSS_SCALE / jnp.sum(side_parts[...], axis=0)
        inverse[0] = side[:, BLOCK : 2 * BLOCK]
        inverse[1] = side[:, 2 * BLOCK : 3 * BLOCK]
        inverse[2] = LOSS_SCALE / jnp.sum(far_parts[...], axis=0)

    def work(size):
        row = lax.broadcasted_iota(jnp.int32, (size, BLOCK), 0)

        def ratio_of(block):
            if block == 2:
                return far_squashed[0:size]
            return side_squashed[0:size, block * BLOCK : (block + 1) * BLOCK]

        for block in range(blocks - 1):
            relative = ids[block + 1] - step * COLUMN_TILE
            target, last = place_targets(relative, prob[block + 1], row)
            ratio = ratio_of(block)
            share = jnp.exp(ratio * SOFT_CAP) * inverse[block]
            grads[block, 0:size] = ((share - target) * (1.0 - ratio * ratio)).astype(jnp.bfloat16)

            def more(_, last):
                relative = ids[block + 1] - step * COLUMN_TILE
                last, chance = next_slot(relative, prob[block + 1], last)
                ratio = ratio_of(block)
                share = jnp.exp(ratio * SOFT_CAP) * inverse[block]
                fresh = (share - chance * LOSS_SCALE) * (1.0 - ratio * ratio)
                held = grads[block, 0:size].astype(jnp.float32)
                grads[block, 0:size] = jnp.where(row == last, fresh, held).astype(jnp.bfloat16)
                return last

            lax.fori_loop(FAST_SLOTS, counts[step * (blocks - 1) + block], more, last)

        spread = dot_nt(hidden[0], own_grads[0:size])
        for block in range(blocks - 1):
            spread = spread + dot_nt(hidden[block + 1], grads[block, 0:size])

        def lookup(chunk, held):
            column = lax.broadcasted_iota(jnp.int32, (size, BLOCK), 0) + step * COLUMN_TILE
            onehot = jnp.where(column == packed_ids[chunk], math.sqrt(width), 0.0)
            return held + dot_nt(packed_cot[chunk], onehot.astype(jnp.bfloat16))

        spread = lax.fori_loop(0, chunks[0], lookup, spread)
        embed_grad[:, 0:size] = spread.astype(jnp.bfloat16)

    @pl.when(step < last_step)
    def _():
        work(COLUMN_TILE)

    @pl.when(step == last_step)
    def _():
        work(rows - (rows - 1) // COLUMN_TILE * COLUMN_TILE)


def smem():
    return pl.BlockSpec(memory_space=pltpu.SMEM)


def vmem():
    return pl.BlockSpec(memory_space=pltpu.VMEM)


def whole(shape):
    return pl.BlockSpec(shape, lambda *_: (0,) * len(shape))


def shape_of(shape, dtype):
    return jax.ShapeDtypeStruct(shape, dtype)


def logits_call(place, embed, near, far):
    blocks = len(near)
    rows, width = embed.shape
    tokens = blocks * BLOCK
    return pl.pallas_call(
        functools.partial(logit_kernel, blocks),
        grid=(rows // ROW_TILE,),
        in_specs=[smem(), pl.BlockSpec((ROW_TILE, width), lambda n: (n, 0))]
        + [whole((width, HALF))] * (2 * blocks),
        out_specs=(pl.BlockSpec((ROW_TILE, tokens), lambda n: (n, 0)), whole((1, tokens))),
        out_shape=(shape_of((rows, tokens), jnp.float32), shape_of((1, tokens), jnp.float32)),
        scratch_shapes=[
            pltpu.VMEM((blocks, width, BLOCK), jnp.bfloat16),
            pltpu.VMEM((8, tokens), jnp.float32),
        ],
        compiler_params=pltpu.CompilerParams(vmem_limit_bytes=36 << 20),
        cost_estimate=pl.CostEstimate(
            flops=2 * rows * width * tokens,
            bytes_accessed=rows * width * 2 + rows * tokens * 4,
            transcendentals=2 * rows * tokens,
        ),
        name=f"logits_{blocks}",
    )(place, embed, *near, *far)


def spread_to(value, axes):
    count = lax.axis_size(axes)
    copies = jnp.broadcast_to(value[None], (count,) + value.shape)
    return lax.all_to_all(copies, axes, 0, 0, tiled=True)


def swap(value):
    return lax.ppermute(value, "core", [(0, 1), (1, 0)])


def shift(value, by):
    count = lax.axis_size("dp")
    return lax.ppermute(value, "dp", [(k, (k + by) % count) for k in range(count)])


def per_device(hidden, embed, token_ids, lookup_cot, teacher_ids, teacher_logits):
    rows, width = embed.shape
    dp = lax.axis_size("dp")
    vocab = lax.axis_size(RING)
    mine = lax.axis_index("dp")
    core = lax.axis_index("core")
    vocab_index = lax.axis_index(RING)
    here, thin = hidden.shape
    tokens = here * dp
    top = teacher_ids.shape[1]
    share = here // vocab
    columns = width // dp
    chips = vocab // 2
    blocks = len(SHIFTS)
    place = jnp.stack([vocab_index * rows, mine, core]).astype(jnp.int32)

    flat = hidden.T
    low, high = flat[:, :HALF], flat[:, HALF:]
    got = swap(jnp.where(core == 0, high, low))
    kept = jnp.where(core == 0, low, high)
    pair = jnp.where(
        core == 0, jnp.concatenate([kept, got], 0), jnp.concatenate([got, kept], 0)
    )
    own_near = spread_to(pair, PLANE).reshape(width, HALF)
    previous_near = shift(own_near, 1)
    next_near = shift(own_near, -1)
    own_far = swap(own_near)
    own_squashed, own_total = logits_call(place, embed, [own_near], [own_far])
    middle = width // 2
    far_upper = shift(previous_near[:middle], 1)
    far_lower = shift(next_near[middle:], -1)
    next_far = swap(next_near)
    previous_far = swap(previous_near)
    side_squashed, side_total = logits_call(
        place, embed, [next_near, previous_near], [next_far, previous_far]
    )
    opposite_near = jnp.concatenate([far_upper, far_lower], axis=0)
    opposite_far = swap(opposite_near)
    side_parts = spread_to(jnp.concatenate([own_total, side_total], axis=1), RING)
    far_squashed, far_total = logits_call(place, embed, [opposite_near], [opposite_far])
    far_parts = spread_to(far_total, RING)

    pack = jnp.concatenate(
        [
            jnp.concatenate([teacher_logits, teacher_ids.astype(jnp.float32)], axis=1),
            token_ids.astype(jnp.float32).reshape(here // HALF, HALF),
            jnp.zeros((8 - here // HALF, HALF), jnp.float32),
        ],
        axis=0,
    )
    pack = spread_to(pack, "dp")
    token_all = pack[:, share : share + here // HALF].reshape(1, tokens).astype(jnp.int32)
    pack = spread_to(pack[:, :share], RING)

    per = vocab // dp
    route = [
        (i * vocab + j, (j // per) * vocab + i * per + j % per)
        for i in range(dp)
        for j in range(vocab)
    ]
    moved = lax.ppermute(lookup_cot.T, ("dp",) + RING, route)
    cot = spread_to(moved, RING).reshape(dp, columns, here)

    row_tiles = rows // ROW_TILE
    column_tiles = pl.cdiv(rows, COLUMN_TILE)
    ids, prob, row_counts, column_counts = pl.pallas_call(
        functools.partial(teacher_kernel, rows),
        out_shape=(
            shape_of((blocks, top, BLOCK), jnp.int32),
            shape_of((blocks, top, BLOCK), jnp.float32),
            shape_of((row_tiles,), jnp.int32),
            shape_of((column_tiles * (blocks - 1),), jnp.int32),
        ),
        in_specs=[smem(), vmem()],
        out_specs=(vmem(), vmem(), smem(), smem()),
        name="teacher_prep",
    )(place, pack)

    packed_cot, packed_ids, chunks = pl.pallas_call(
        functools.partial(lookup_kernel, rows),
        out_shape=(
            shape_of((dp, columns, here), jnp.bfloat16),
            shape_of((dp, 1, here), jnp.int32),
            shape_of((1,), jnp.int32),
        ),
        in_specs=[smem(), vmem(), vmem()],
        out_specs=(vmem(), vmem(), smem()),
        name="lookup_prep",
    )(place, token_all, cot)

    own_grads, keep, give = pl.pallas_call(
        hidden_grad_kernel,
        grid=(row_tiles,),
        in_specs=[
            smem(),
            smem(),
            pl.BlockSpec((ROW_TILE, width), lambda n: (n, 0)),
            pl.BlockSpec((ROW_TILE, BLOCK), lambda n: (n, 0)),
            whole(side_parts.shape),
            whole(ids.shape),
            whole(prob.shape),
        ],
        out_specs=[
            pl.BlockSpec((ROW_TILE, BLOCK), lambda n: (n, 0)),
            whole((chips, thin + 8, BLOCK)),
            whole((chips, thin + 8, BLOCK)),
        ],
        out_shape=(
            shape_of((rows, BLOCK), jnp.bfloat16),
            shape_of((chips, thin + 8, BLOCK), jnp.float32),
            shape_of((chips, thin + 8, BLOCK), jnp.float32),
        ),
        scratch_shapes=[
            pltpu.VMEM((BLOCK, width), jnp.float32),
            pltpu.VMEM((width, BLOCK), jnp.float32),
            pltpu.VMEM((8, BLOCK), jnp.float32),
        ],
        compiler_params=pltpu.CompilerParams(vmem_limit_bytes=36 << 20),
        cost_estimate=pl.CostEstimate(
            flops=2 * rows * width * BLOCK,
            bytes_accessed=rows * width * 2 + rows * BLOCK * 6,
            transcendentals=rows * BLOCK,
        ),
        name="hidden_grads",
    )(place, row_counts, embed, own_squashed, side_parts, ids, prob)

    halved = keep + swap(give)

    near = [own_near, next_near, previous_near, opposite_near]
    far = [own_far, next_far, previous_far, opposite_far]
    half_spec = pl.BlockSpec((columns, HALF), lambda n, place, *_: (place[1], 0))
    embed_grad = pl.pallas_call(
        functools.partial(table_grad_kernel, rows, width),
        grid_spec=pltpu.PrefetchScalarGridSpec(
            num_scalar_prefetch=3,
            grid=(column_tiles,),
            in_specs=[
                pl.BlockSpec((COLUMN_TILE, BLOCK), lambda n, *_: (n, 0)),
                pl.BlockSpec((COLUMN_TILE, 2 * BLOCK), lambda n, *_: (n, 0)),
                pl.BlockSpec((COLUMN_TILE, BLOCK), lambda n, *_: (n, 0)),
                whole(side_parts.shape),
                whole(far_parts.shape),
                whole(ids.shape),
                whole(prob.shape),
                whole(packed_cot.shape),
                whole(packed_ids.shape),
            ]
            + [half_spec] * (2 * blocks),
            out_specs=pl.BlockSpec((columns, COLUMN_TILE), lambda n, *_: (0, n)),
            scratch_shapes=[
                pltpu.VMEM((blocks, columns, BLOCK), jnp.bfloat16),
                pltpu.VMEM((blocks - 1, COLUMN_TILE, BLOCK), jnp.bfloat16),
                pltpu.VMEM((blocks - 1, 1, BLOCK), jnp.float32),
            ],
        ),
        out_shape=shape_of((columns, rows), jnp.bfloat16),
        compiler_params=pltpu.CompilerParams(vmem_limit_bytes=36 << 20),
        cost_estimate=pl.CostEstimate(
            flops=2 * rows * columns * (tokens + BLOCK),
            bytes_accessed=rows * tokens * 4 + rows * columns * 2,
            transcendentals=rows * tokens,
        ),
        name="table_grads",
    )(
        place,
        column_counts,
        chunks,
        own_grads,
        side_squashed,
        far_squashed,
        side_parts,
        far_parts,
        ids,
        prob,
        packed_cot,
        packed_ids,
        *near,
        *far,
    )

    summed = jnp.sum(lax.all_to_all(halved, PLANE, 0, 0, tiled=True), axis=0)
    hidden_grad = summed[:thin].astype(jnp.bfloat16).T

    own_prob = jax.nn.softmax(teacher_logits, axis=1)
    first = vocab_index * share
    total = jnp.sum(side_parts[:, 0, :here], axis=0)
    own_total = lax.dynamic_slice_in_dim(total, first, share, 0)
    own_term = lax.dynamic_slice_in_dim(summed[thin], first, share, 0)
    divergence = (
        jnp.sum(own_prob * jnp.log(own_prob), axis=1) - own_term + jnp.log(own_total)
    )
    return (hidden_grad, embed_grad.T, divergence)


def solution(mesh):
    dp, vocab = (mesh.shape[name] for name in ("dp", "vocab"))
    side = math.isqrt(vocab // 2)
    fine = Mesh(mesh.devices.reshape(dp, side, side, 2), ("dp",) + RING)
    every = ("dp",) + RING
    return jax.shard_map(
        per_device,
        mesh=fine,
        in_specs=(
            P("dp", RING),
            P(RING, None),
            P("dp"),
            P("dp", RING),
            P(every, None),
            P(every, None),
        ),
        out_specs=(P("dp", RING), P(RING, "dp"), P(every)),
        check_vma=False,
    )
```

```python
import functools
import math

import jax
import jax.numpy as jnp
from jax import lax
from jax.experimental import pallas as pl
from jax.experimental.pallas import tpu as pltpu
from jax.sharding import Mesh, PartitionSpec as P

SOFT_CAP = 30.0
LOSS_SCALE = 16.0
BLOCK = 256
HALF = 128
ROW_TILE = 400
ROW_STEP = 800
COLUMN_TILE = 512
FAST_SLOTS = 4
FAR = 1 << 30
RING = ("z", "y", "core")
EVERY = ("dp",) + RING
SIDE = 4
OFFSETS = (0, 1, 3, 2)


def dot_nn(a, b):
    return lax.dot_general(a, b, (((1,), (0,)), ((), ())), preferred_element_type=jnp.float32)


def dot_nt(a, b):
    return lax.dot_general(a, b, (((1,), (1,)), ((), ())), preferred_element_type=jnp.float32)


def dot_tn(a, b):
    return lax.dot_general(a, b, (((0,), (0,)), ((), ())), preferred_element_type=jnp.float32)


def offset_of(index, core):
    return jnp.where(core == 0, OFFSETS[index], OFFSETS[(0, 2, 1, 3)[index]])


def chip_of(outer, inner, core, z, y):
    first, second = OFFSETS[inner], OFFSETS[outer]
    row = lax.rem(z + jnp.where(core == 0, second, first), SIDE)
    column = lax.rem(y + jnp.where(core == 0, first, second), SIDE)
    return row * SIDE + column


def here():
    return tuple(lax.axis_index(name) for name in EVERY)


def block_offset(rows, z, y, core):
    return ((z * SIDE + y) * 2 + core) * rows


def teacher_kernel(rows, thin, near, far, cot, ids, prob, row_counts, column_counts, joined):
    _, z, y, core = here()
    offset = block_offset(rows, z, y, core)
    top = ids.shape[1]
    share = 8
    group = thin + 2 * share
    for side, source in ((core, near), (1 - core, far)):
        lanes = pl.ds(pl.multiple_of(side * HALF, HALF), HALF)
        for outer in range(SIDE):
            for inner in range(SIDE):
                chip = chip_of(outer, inner, side, z, y)
                for other in range(2):
                    start = ((outer * SIDE + inner) * 2 + other) * group
                    rank = chip * 2 + other
                    into = pl.multiple_of(rank * thin, 8)
                    cot[pl.ds(into, thin), lanes] = source[start : start + thin]
                    for half in range(2):
                        held = source[start + thin + half * share : start + thin + (half + 1) * share]
                        joined[side * 2 + half, pl.ds(pl.multiple_of(rank * share, 8), share)] = held
    for block in range(SIDE):
        flipped = joined[offset_of(block, core)].T
        scores = flipped[:top]
        local = flipped[top:].astype(jnp.int32) - offset
        raised = jnp.exp(scores - jnp.max(scores, axis=0, keepdims=True))
        ids[block] = local
        prob[block] = raised / jnp.sum(raised, axis=0, keepdims=True)
        size, held = (ROW_TILE, row_counts) if block == 0 else (COLUMN_TILE, column_counts)
        for tile in range(pl.cdiv(rows, size)):
            inside = (local >= tile * size) & (local < tile * size + size)
            most = jnp.max(jnp.sum(inside.astype(jnp.int32), axis=0))
            if block == 0:
                held[tile] = most
            else:
                held[tile * (SIDE - 1) + block - 1] = most


def lookup_kernel(rows, share, packs, cot, packed_cot, packed_ids, chunks, tokens):
    mine, z, y, core = here()
    offset = block_offset(rows, z, y, core)
    count = tokens.shape[1]
    blocks = count // BLOCK
    for index in range(blocks):
        start = lax.rem(mine + OFFSETS[index], blocks) * BLOCK
        for half in range(BLOCK // HALF):
            lanes = pl.ds(pl.multiple_of(start + half * HALF, HALF), HALF)
            tokens[:, lanes] = packs[index, share + half : share + half + 1]
    local = tokens[...].astype(jnp.int32) - offset
    inside = (local >= 0) & (local < rows)
    hit = jnp.broadcast_to(jnp.where(inside, 1.0, 0.0), (8, count))
    before = lax.broadcasted_iota(jnp.int32, (count, count), 0)
    after = lax.broadcasted_iota(jnp.int32, (count, count), 1)
    upto = jnp.where(before <= after, 1.0, 0.0).astype(jnp.bfloat16)
    running = dot_nn(hit.astype(jnp.bfloat16), upto)[0:1].astype(jnp.int32)
    rank = jnp.where(inside, running - 1, -1)
    total = jnp.max(running)
    chunks[0] = (total + BLOCK - 1) // BLOCK
    safe = jnp.where(inside, local, 0)
    high = jnp.broadcast_to((safe >> 6).astype(jnp.float32), (8, count)).astype(jnp.bfloat16)
    low = jnp.broadcast_to((safe & 63).astype(jnp.float32), (8, count)).astype(jnp.bfloat16)
    for chunk in range(blocks):

        @pl.when(chunk * BLOCK < jnp.maximum(total, 1))
        def _():
            slot = lax.broadcasted_iota(jnp.int32, (BLOCK, count), 0) + chunk * BLOCK
            chosen = jnp.where(slot == rank, 1.0, 0.0).astype(jnp.bfloat16)
            columns = cot.shape[0] // blocks
            taken = jnp.zeros((columns, BLOCK), jnp.float32)
            for block in range(blocks):
                span = slice(block * BLOCK, (block + 1) * BLOCK)
                part = cot[block * columns : (block + 1) * columns].astype(jnp.bfloat16)
                taken = taken + dot_nt(part, chosen[:, span])
            packed_cot[chunk] = taken.astype(jnp.bfloat16)
            row = dot_nt(high, chosen)[0:1] * 64.0 + dot_nt(low, chosen)[0:1]
            used = dot_nt(hit.astype(jnp.bfloat16), chosen)[0:1] > 0.5
            packed_ids[chunk] = jnp.where(used, row.astype(jnp.int32), -1)


def next_slot(relative, prob, last):
    following = jnp.min(jnp.where(relative > last, relative, FAR), axis=0, keepdims=True)
    chance = jnp.sum(jnp.where(relative == following, prob, 0.0), axis=0, keepdims=True)
    return following, chance


def join_halves(near, far, joined):
    _, z, y, core = here()
    pair = near.shape[0] // (SIDE * SIDE)
    for side, source in ((core, near), (1 - core, far)):
        lanes = pl.ds(pl.multiple_of(side * HALF, HALF), HALF)
        for outer in range(SIDE):
            for inner in range(SIDE):
                start = (outer * SIDE + inner) * pair
                into = pl.multiple_of(chip_of(outer, inner, side, z, y) * pair, 16)
                joined[pl.ds(into, pair), lanes] = source[start : start + pair]


def table_copy(step, table, held, ready):
    rows = pl.ds(pl.multiple_of(step * ROW_STEP, 16), ROW_STEP)
    return pltpu.make_async_copy(table.at[rows], held.at[rows], ready.at[step])


def logit_kernel(blocks, fresh, embed, *refs):
    near, far = refs[:blocks], refs[blocks : 2 * blocks]
    squashed, total, columns = refs[2 * blocks : 2 * blocks + 3]
    rest = refs[2 * blocks + 3 :]
    step = pl.program_id(0)
    steps = pl.num_programs(0)
    if fresh:
        held, hidden, sums, ready = rest

        @pl.when(step == 0)
        def _():
            for index in range(held.shape[0] // ROW_STEP):
                table_copy(index, embed, held, ready).start()

    else:
        held, (hidden, sums) = embed, rest

    @pl.when(step == 0)
    def _():
        sums[...] = jnp.zeros_like(sums)
        size = columns.shape[1]
        start = pl.multiple_of(lax.axis_index("dp") * size, 16)
        for block in range(blocks):
            join_halves(near[block], far[block], hidden.at[block])
            columns[block] = hidden[block, pl.ds(start, size)]

    if fresh:
        table_copy(step, embed, held, ready).wait()

    for first in range(0, ROW_STEP, ROW_TILE):
        rows = slice(first, first + ROW_TILE)
        from_table = pl.ds(pl.multiple_of(step * ROW_STEP + first, 16), ROW_TILE)
        for block in range(blocks):
            span = slice(block * BLOCK, (block + 1) * BLOCK)
            raw = dot_nn(held[from_table], hidden[block])
            ratio = jnp.tanh(raw * (1.0 / SOFT_CAP))
            squashed[rows, span] = ratio
            raised = jnp.exp(ratio * SOFT_CAP)
            sums[:, span] += jnp.sum(raised.reshape(ROW_TILE // 8, 8, BLOCK), axis=0)

    @pl.when(step == steps - 1)
    def _():
        total[...] = jnp.sum(sums[...], axis=0, keepdims=True)


def logit_grad(ratio, inverse, relative, chances, count, term=None):
    row = lax.broadcasted_iota(jnp.int32, ratio.shape, 0)
    last = jnp.full((1, BLOCK), -1, jnp.int32)
    target = jnp.zeros(ratio.shape, jnp.float32)
    for _ in range(FAST_SLOTS):
        last, chance = next_slot(relative, chances, last)
        target = jnp.where(row == last, chance * LOSS_SCALE, target)

    if count is not None:

        def more(_, held):
            last, target = held
            last, chance = next_slot(relative, chances, last)
            return last, jnp.where(row == last, chance * LOSS_SCALE, target)

        _, target = lax.fori_loop(FAST_SLOTS, count, more, (last, target))
    if term is not None:
        term[...] += jnp.sum((target * ratio).reshape(ratio.shape[0] // 8, 8, BLOCK), axis=0)
    share = jnp.exp(ratio * SOFT_CAP) * inverse
    return ((share - target) * (1.0 - ratio * ratio)).astype(jnp.bfloat16)


def hidden_grad_kernel(
    counts, embed, squashed, total, ids, prob, grads, keep, give, rows_grad, flipped, term
):
    step = pl.program_id(0)
    width = embed.shape[1]
    inverse = LOSS_SCALE / total[:, 0:BLOCK]
    tiles = ROW_STEP // ROW_TILE

    @pl.when(step == 0)
    def _():
        rows_grad[...] = jnp.zeros_like(rows_grad)
        term[...] = jnp.zeros_like(term)

    def work(careful):
        gathered = None
        for tile in range(tiles):
            rows = slice(tile * ROW_TILE, (tile + 1) * ROW_TILE)
            relative = ids[0] - (step * ROW_STEP + tile * ROW_TILE)
            count = counts[step * tiles + tile] if careful else None
            fresh = logit_grad(squashed[rows], inverse, relative, prob[0], count, term)
            grads[rows] = fresh
            start = pl.multiple_of(step * ROW_STEP + tile * ROW_TILE, 16)
            product = dot_tn(fresh, embed[pl.ds(start, ROW_TILE)])
            gathered = product if gathered is None else gathered + product
        rows_grad[...] += gathered

    most = counts[step * tiles]
    for tile in range(1, tiles):
        most = jnp.maximum(most, counts[step * tiles + tile])

    @pl.when(most <= FAST_SLOTS)
    def _():
        work(False)

    @pl.when(most > FAST_SLOTS)
    def _():
        work(True)

    @pl.when(step == pl.num_programs(0) - 1)
    def _():
        _, z, y, core = here()
        thin = keep.shape[2] - 8
        for part in range(width // BLOCK):
            span = slice(part * BLOCK, (part + 1) * BLOCK)
            flipped[span, :] = rows_grad[:, span].T
        summed = jnp.sum(term[...], axis=0, keepdims=True) * (SOFT_CAP / LOSS_SCALE)
        for outer in range(SIDE):
            for inner in range(SIDE):
                for ref, side in ((keep, core), (give, 1 - core)):
                    rank = 2 * chip_of(outer, inner, side, z, y) + side
                    start = pl.multiple_of(rank * thin, 8)
                    ref[outer, inner, 0:thin] = flipped[pl.ds(start, thin)]
                    ref[outer, inner, thin : thin + 8] = jnp.broadcast_to(summed, (8, BLOCK))


def halve_kernel(keep, got, *outs):
    for index, out in enumerate(outs):
        out[...] = keep[index] + got[index]


def quarter_kernel(*refs):
    parts, outs = refs[:SIDE], refs[SIDE:]
    for index, out in enumerate(outs):
        out[...] = (parts[0][index] + parts[1][index]) + (parts[2][index] + parts[3][index])


def finish_kernel(total, teacher_logits, *refs):
    parts, (hidden_grad, divergence) = refs[:SIDE], refs[SIDE:]
    _, z, y, core = here()
    summed = (parts[0][...] + parts[1][...]) + (parts[2][...] + parts[3][...])
    thin = hidden_grad.shape[0]
    hidden_grad[...] = summed[:thin].astype(jnp.bfloat16)
    scores = teacher_logits[...]
    share = scores.shape[0]
    shifted = scores - jnp.max(scores, axis=1, keepdims=True)
    raised = jnp.exp(shifted)
    prob = raised / jnp.sum(raised, axis=1, keepdims=True)
    entropy = jnp.sum(prob * jnp.log(prob), axis=1, keepdims=True)
    rest = jnp.log(total[:, 0:BLOCK]) - summed[thin : thin + 1]
    first = ((z * SIDE + y) * 2 + core) * share
    lane = lax.broadcasted_iota(jnp.int32, (share, BLOCK), 1)
    token = lax.broadcasted_iota(jnp.int32, (share, BLOCK), 0) + first
    value = entropy + jnp.sum(jnp.where(lane == token, rest, 0.0), axis=1, keepdims=True)
    line = lax.broadcasted_iota(jnp.int32, (share, HALF), 0)
    column = lax.broadcasted_iota(jnp.int32, (share, HALF), 1)
    divergence[...] = jnp.sum(jnp.where(line == column, value, 0.0), axis=0, keepdims=True)


def table_grad_kernel(
    rows,
    width,
    first_step,
    counts,
    chunks,
    own_grads,
    side_squashed,
    far_squashed,
    total,
    ids,
    prob,
    packed_cot,
    packed_ids,
    own_columns,
    side_columns,
    far_columns,
    *refs,
):
    embed_grad = refs[-1]
    step = pl.program_id(0) + first_step
    last_step = pl.cdiv(rows, COLUMN_TILE) - 1
    blocks = SIDE - 1

    def work(size, careful):
        spread = dot_nt(own_columns[0], own_grads[0:size])
        for block in range(blocks):
            span = slice(block * BLOCK, (block + 1) * BLOCK)
            held = far_squashed[0:size] if block == 2 else side_squashed[0:size, span]
            inverse = LOSS_SCALE / total[:, (block + 1) * BLOCK : (block + 2) * BLOCK]
            relative = ids[block + 1] - step * COLUMN_TILE
            count = counts[step * blocks + block] if careful else None
            fresh = logit_grad(held, inverse, relative, prob[block + 1], count)
            columns = far_columns[0] if block == 2 else side_columns[block]
            spread = spread + dot_nt(columns, fresh)

        def lookup(chunk, held):
            column = lax.broadcasted_iota(jnp.int32, (size, BLOCK), 0) + step * COLUMN_TILE
            onehot = jnp.where(column == packed_ids[chunk], math.sqrt(width), 0.0)
            return held + dot_nt(packed_cot[chunk], onehot.astype(jnp.bfloat16))

        spread = lookup(0, spread)
        spread = lax.fori_loop(1, chunks[0], lookup, spread)
        embed_grad[:, 0:size] = spread.astype(jnp.bfloat16)

    most = counts[step * blocks]
    for block in range(1, blocks):
        most = jnp.maximum(most, counts[step * blocks + block])
    tail = rows - (rows - 1) // COLUMN_TILE * COLUMN_TILE
    for size, here_now in ((COLUMN_TILE, step < last_step), (tail, step == last_step)):
        for careful, chosen in ((False, most <= FAST_SLOTS), (True, most > FAST_SLOTS)):

            @pl.when(here_now & chosen)
            def _(size=size, careful=careful):
                work(size, careful)


def smem():
    return pl.BlockSpec(memory_space=pltpu.SMEM)


def vmem():
    return pl.BlockSpec(memory_space=pltpu.VMEM)


def whole(shape):
    return pl.BlockSpec(shape, lambda *_: (0,) * len(shape))


def shape_of(shape, dtype):
    return jax.ShapeDtypeStruct(shape, dtype)


def small_call(kernel, name, outs, *args, scratch=(), limit=4 << 20):
    return pl.pallas_call(
        kernel,
        out_shape=tuple(shape_of(shape, dtype) for shape, dtype, _ in outs),
        in_specs=[vmem()] * len(args),
        out_specs=tuple(space() for _, _, space in outs),
        scratch_shapes=scratch,
        compiler_params=pltpu.CompilerParams(vmem_limit_bytes=limit),
        name=name,
    )(*args)


def logits_call(embed, near, far, columns, fresh):
    blocks = len(near)
    rows, width = embed.shape
    tokens = blocks * BLOCK
    steps = rows // ROW_STEP
    table = whole((rows, width))
    out_specs = [
        pl.BlockSpec((ROW_STEP, tokens), lambda n: (n, 0)),
        whole((1, tokens)),
        whole((blocks, columns, BLOCK)),
    ]
    out_shape = [
        shape_of((rows, tokens), jnp.float32),
        shape_of((1, tokens), jnp.float32),
        shape_of((blocks, columns, BLOCK), jnp.bfloat16),
    ]
    scratch = [
        pltpu.VMEM((blocks, width, BLOCK), jnp.bfloat16),
        pltpu.VMEM((8, tokens), jnp.float32),
    ]
    if fresh:
        out_specs.append(table)
        out_shape.append(pltpu.VMEM((rows, width), embed.dtype))
        scratch.append(pltpu.SemaphoreType.DMA((steps,)))
    return pl.pallas_call(
        functools.partial(logit_kernel, blocks, fresh),
        grid=(steps,),
        in_specs=[pl.BlockSpec(memory_space=pltpu.HBM) if fresh else table]
        + [whole((width, HALF))] * (2 * blocks),
        out_specs=out_specs,
        out_shape=out_shape,
        scratch_shapes=scratch,
        compiler_params=pltpu.CompilerParams(vmem_limit_bytes=(4 + 3 * blocks) << 20),
        cost_estimate=pl.CostEstimate(
            flops=2 * rows * width * tokens,
            bytes_accessed=rows * tokens * 4 + (2 * rows * width if fresh else 0),
            transcendentals=2 * rows * tokens,
        ),
        name=f"logits_{blocks}",
    )(pltpu.with_memory_space_constraint(embed, pltpu.HBM) if fresh else embed, *near, *far)


def index_of(x, z, y, core):
    return ((x * SIDE + z) * SIDE + y) * 2 + core


def route_by(target):
    pairs = []
    for x in range(SIDE):
        for z in range(SIDE):
            for y in range(SIDE):
                for core in range(2):
                    pairs.append((index_of(x, z, y, core), index_of(*target(x, z, y, core))))
    return pairs


def along(axis, core, by, place):
    x, z, y = place
    if axis == 2:
        x = (x + (by if core == 0 else -by)) % SIDE
    elif axis == core:
        y = (y + by) % SIDE
    else:
        z = (z + by) % SIDE
    return x, z, y, core


def fetch(value, axis, by):
    return lax.ppermute(value, EVERY, route_by(lambda x, z, y, c: along(axis, c, -by, (x, z, y))))


def hand_on(value, axis, by):
    return lax.ppermute(value, EVERY, route_by(lambda x, z, y, c: along(axis, c, by, (x, z, y))))


def swap(value):
    return lax.ppermute(value, EVERY, route_by(lambda x, z, y, c: (x, z, y, 1 - c)))


def fetch_parts(value, axis):
    return [value] + [fetch(value, axis, by) for by in OFFSETS[1:]]


def fetch_all(value, axis):
    return jnp.concatenate(fetch_parts(value, axis), axis=0)


def halves(core_zero, low, high):
    return jnp.where(core_zero, low, high), jnp.where(core_zero, high, low)


def in_core_order(core_zero, kept, got):
    return jnp.where(
        core_zero, jnp.concatenate([kept, got], 0), jnp.concatenate([got, kept], 0)
    )


def side_values(core_zero, after, token_ids, lookup_cot, teacher_ids, teacher_logits):
    here_tokens, thin = lookup_cot.shape
    share = teacher_ids.shape[0]
    pack = jnp.concatenate(
        [
            jnp.concatenate([teacher_logits, teacher_ids.astype(jnp.float32)], axis=1),
            token_ids.astype(jnp.float32).reshape(here_tokens // HALF, HALF),
            jnp.zeros((8 - here_tokens // HALF, HALF), jnp.float32),
        ],
        axis=0,
    )
    pack, turned, _ = lax.optimization_barrier((pack, lookup_cot.T, after))
    moved = lax.ppermute(
        turned,
        EVERY,
        route_by(lambda x, z, y, c: (z, x, y, c)),
    ).astype(jnp.float32)
    packs = [pack] + [
        lax.ppermute(pack, "dp", [((k + by) % SIDE, k) for k in range(SIDE)])
        for by in OFFSETS[1:]
    ]
    far_away = [packs[0], packs[1], packs[3], packs[2]]
    sides = [
        jnp.concatenate(
            [
                moved[:, half * HALF : (half + 1) * HALF],
                far_away[2 * half][:share],
                far_away[2 * half + 1][:share],
            ],
            axis=0,
        )
        for half in range(2)
    ]
    kept, given = halves(core_zero, *sides)
    return in_core_order(core_zero, kept, swap(given)), jnp.stack(packs)


def per_device(hidden, embed, token_ids, lookup_cot, teacher_ids, teacher_logits):
    rows, width = embed.shape
    here_tokens, thin = hidden.shape
    dp = SIDE
    vocab = 2 * SIDE * SIDE
    tokens = here_tokens * dp
    top = teacher_ids.shape[1]
    share = here_tokens // vocab
    columns = width // dp
    core_zero = lax.axis_index("core") == 0

    flat = hidden.T
    kept, given = halves(core_zero, flat[:, :HALF], flat[:, HALF:])
    pair = in_core_order(core_zero, kept, swap(given))
    own_near = fetch_all(fetch_all(pair, 0), 1)
    side = side_values(core_zero, pair, token_ids, lookup_cot, teacher_ids, teacher_logits)
    own_near, side, packs = lax.optimization_barrier((own_near, *side))
    first_near = fetch(own_near, 2, 1)
    second_near = fetch(own_near, 2, -1)
    own_far = swap(own_near)
    own_squashed, own_total, own_columns, table = logits_call(
        embed, [own_near], [own_far], columns, True
    )
    first_near, second_near, own_total = lax.optimization_barrier(
        (first_near, second_near, own_total)
    )
    opposite_near = fetch(first_near, 2, 1)
    first_far = swap(second_near)
    second_far = swap(first_near)
    side = lax.optimization_barrier((side, first_near))[0]
    side_parts = fetch_parts(side, 0)
    side_squashed, side_total, side_columns = logits_call(
        table, [first_near, second_near], [first_far, second_far], columns, False
    )
    side_parts, opposite_near, side_total = lax.optimization_barrier(
        (side_parts, opposite_near, side_total)
    )
    opposite_far = swap(opposite_near)
    side_parts = fetch_parts(jnp.concatenate(side_parts, axis=0), 1)
    far_squashed, far_total, far_columns = logits_call(
        table, [opposite_near], [opposite_far], columns, False
    )
    side_parts, far_total = lax.optimization_barrier((side_parts, far_total))
    side_near = jnp.concatenate(side_parts, axis=0)
    side_far = swap(side_near)

    total = jnp.concatenate([own_total, side_total, far_total], axis=1)
    got = swap(total)
    total = total + jnp.concatenate(
        [
            got[:, :BLOCK],
            got[:, 2 * BLOCK : 3 * BLOCK],
            got[:, BLOCK : 2 * BLOCK],
            got[:, 3 * BLOCK :],
        ],
        axis=1,
    )
    for axis in (0, 1):
        one, two, three = (fetch(total, axis, by) for by in OFFSETS[1:])
        total = (total + one) + (two + three)

    row_tiles = rows // ROW_TILE
    column_tiles = pl.cdiv(rows, COLUMN_TILE)
    cot, ids, prob, row_counts, column_counts = small_call(
        functools.partial(teacher_kernel, rows, thin),
        "teacher_prep",
        [
            ((width, BLOCK), jnp.float32, vmem),
            ((dp, top, BLOCK), jnp.int32, vmem),
            ((dp, top, BLOCK), jnp.float32, vmem),
            ((row_tiles,), jnp.int32, smem),
            ((column_tiles * (dp - 1),), jnp.int32, smem),
        ],
        side_near,
        side_far,
        scratch=[pltpu.VMEM((dp, BLOCK, 2 * top), jnp.float32)],
    )
    packed_cot, packed_ids, chunks = small_call(
        functools.partial(lookup_kernel, rows, share),
        "lookup_prep",
        [
            ((dp, columns, BLOCK), jnp.bfloat16, vmem),
            ((dp, 1, BLOCK), jnp.int32, vmem),
            ((1,), jnp.int32, smem),
        ],
        packs,
        cot,
        scratch=[pltpu.VMEM((1, tokens), jnp.float32)],
    )

    scattered = (SIDE, SIDE, thin + 8, BLOCK)
    own_grads, keep, give = pl.pallas_call(
        hidden_grad_kernel,
        grid=(rows // ROW_STEP,),
        in_specs=[
            smem(),
            whole((rows, width)),
            pl.BlockSpec((ROW_STEP, BLOCK), lambda n: (n, 0)),
            whole((1, tokens)),
            whole(ids.shape),
            whole(prob.shape),
        ],
        out_specs=[
            pl.BlockSpec((ROW_STEP, BLOCK), lambda n: (n, 0)),
            whole(scattered),
            whole(scattered),
        ],
        out_shape=(
            shape_of((rows, BLOCK), jnp.bfloat16),
            shape_of(scattered, jnp.float32),
            shape_of(scattered, jnp.float32),
        ),
        scratch_shapes=[
            pltpu.VMEM((BLOCK, width), jnp.float32),
            pltpu.VMEM((width, BLOCK), jnp.float32),
            pltpu.VMEM((8, BLOCK), jnp.float32),
        ],
        compiler_params=pltpu.CompilerParams(vmem_limit_bytes=12 << 20),
        cost_estimate=pl.CostEstimate(
            flops=2 * rows * width * BLOCK,
            bytes_accessed=rows * BLOCK * 6,
            transcendentals=rows * BLOCK,
        ),
        name="hidden_grads",
    )(row_counts, table, own_squashed, total, ids, prob)

    def table_grads(first, steps, so_far):
        started = [] if so_far is None else [so_far]
        operands = [
            column_counts,
            chunks,
            own_grads,
            side_squashed,
            far_squashed,
            total,
            ids,
            prob,
            packed_cot,
            packed_ids,
            own_columns,
            side_columns,
            far_columns,
        ]
        return pl.pallas_call(
            functools.partial(table_grad_kernel, rows, width, first),
            grid=(steps,),
            in_specs=[
                smem(),
                smem(),
                pl.BlockSpec((COLUMN_TILE, BLOCK), lambda n: (n + first, 0)),
                pl.BlockSpec((COLUMN_TILE, 2 * BLOCK), lambda n: (n + first, 0)),
                pl.BlockSpec((COLUMN_TILE, BLOCK), lambda n: (n + first, 0)),
            ]
            + [whole(operand.shape) for operand in operands[5:]]
            + [pl.BlockSpec(memory_space=pltpu.HBM)] * len(started),
            out_specs=pl.BlockSpec((columns, COLUMN_TILE), lambda n: (0, n + first)),
            out_shape=shape_of((columns, rows), jnp.bfloat16),
            input_output_aliases={len(operands): 0} if started else {},
            compiler_params=pltpu.CompilerParams(vmem_limit_bytes=10 << 20),
            cost_estimate=pl.CostEstimate(
                flops=2 * steps * COLUMN_TILE * columns * (tokens + BLOCK),
                bytes_accessed=steps * COLUMN_TILE * columns * 2,
                transcendentals=steps * COLUMN_TILE * tokens,
            ),
            name=f"table_grads_{first}",
        )(*operands, *started)

    quarter = (SIDE, thin + 8, BLOCK)
    got, packed_cot, packed_ids = lax.optimization_barrier((swap(give), packed_cot, packed_ids))
    parts = small_call(halve_kernel, "halve", [(quarter, jnp.float32, vmem)] * SIDE, keep, got)
    travelling = [hand_on(part, 1, by) for part, by in zip(parts[1:], OFFSETS[1:])]
    half_steps = column_tiles // 2
    embed_grad = table_grads(0, half_steps, None)
    travelling, embed_grad = lax.optimization_barrier((travelling, embed_grad))
    parts = small_call(
        quarter_kernel,
        "quarter",
        [(quarter[1:], jnp.float32, vmem)] * SIDE,
        parts[0],
        *travelling,
    )
    travelling = [hand_on(part, 0, by) for part, by in zip(parts[1:], OFFSETS[1:])]
    embed_grad = table_grads(half_steps, column_tiles - half_steps, embed_grad)
    parts = [parts[0]] + travelling

    hidden_grad, divergence = small_call(
        finish_kernel,
        "finish",
        [((thin, BLOCK), jnp.bfloat16, vmem), ((1, HALF), jnp.float32, vmem)],
        total,
        teacher_logits,
        *parts,
    )
    return (hidden_grad.T, embed_grad.T, divergence[0, :share])


def solution(mesh):
    dp, vocab = (mesh.shape[name] for name in ("dp", "vocab"))
    fine = Mesh(mesh.devices.reshape(dp, SIDE, SIDE, vocab // (SIDE * SIDE)), EVERY)
    return jax.shard_map(
        per_device,
        mesh=fine,
        in_specs=(
            P("dp", RING),
            P(RING, None),
            P("dp"),
            P("dp", RING),
            P(EVERY, None),
            P(EVERY, None),
        ),
        out_specs=(P("dp", RING), P(RING, "dp"), P(EVERY)),
        check_vma=False,
    )
```

```python
import functools
import math

import jax
import jax.numpy as jnp
from jax import lax
from jax.experimental import pallas as pl
from jax.experimental.pallas import tpu as pltpu
from jax.sharding import Mesh, PartitionSpec as P

SOFT_CAP = 30.0
LOSS_SCALE = 16.0
BLOCK = 256
HALF = 128
ROW_TILE = 400
ROW_STEP = 800
LONG_STEP = 2000
GRAD_TILE = 1024
CHUNK = 16
COLUMN_TILE = 512
FAST_SLOTS = 4
HIDDEN_SLOTS = 5
FAR = 1 << 30
LOG2_E = math.log2(math.e)
RING = ("z", "y", "core")
EVERY = ("dp",) + RING
SIDE = 4
OFFSETS = (0, 1, 3, 2)


def dot_nn(a, b):
    return lax.dot_general(a, b, (((1,), (0,)), ((), ())), preferred_element_type=jnp.float32)


def dot_nt(a, b):
    return lax.dot_general(a, b, (((1,), (1,)), ((), ())), preferred_element_type=jnp.float32)


def dot_tn(a, b):
    return lax.dot_general(a, b, (((0,), (0,)), ((), ())), preferred_element_type=jnp.float32)


def offset_of(index, core):
    return jnp.where(core == 0, OFFSETS[index], OFFSETS[(0, 2, 1, 3)[index]])


def chip_of(outer, inner, core, z, y):
    first, second = OFFSETS[inner], OFFSETS[outer]
    row = lax.rem(z + jnp.where(core == 0, second, first), SIDE)
    column = lax.rem(y + jnp.where(core == 0, first, second), SIDE)
    return row * SIDE + column


def here():
    return tuple(lax.axis_index(name) for name in EVERY)


def block_offset(rows, z, y, core):
    return ((z * SIDE + y) * 2 + core) * rows


def teacher_kernel(rows, thin, near, far, cot, ids, prob, row_counts, column_counts, joined):
    _, z, y, core = here()
    offset = block_offset(rows, z, y, core)
    top = ids.shape[1]
    share = 8
    group = thin + 2 * share
    for side, source in ((core, near), (1 - core, far)):
        lanes = pl.ds(pl.multiple_of(side * HALF, HALF), HALF)
        for outer in range(SIDE):
            for inner in range(SIDE):
                chip = chip_of(outer, inner, side, z, y)
                for other in range(2):
                    start = ((outer * SIDE + inner) * 2 + other) * group
                    rank = chip * 2 + other
                    into = pl.multiple_of(rank * thin, 8)
                    cot[pl.ds(into, thin), lanes] = source[start : start + thin]
                    for half in range(2):
                        held = source[start + thin + half * share : start + thin + (half + 1) * share]
                        joined[side * 2 + half, pl.ds(pl.multiple_of(rank * share, 8), share)] = held
    for block in range(SIDE):
        flipped = joined[offset_of(block, core)].T
        scores = flipped[:top]
        local = flipped[top:].astype(jnp.int32) - offset
        raised = jnp.exp(scores - jnp.max(scores, axis=0, keepdims=True))
        ids[block] = local
        prob[block] = raised / jnp.sum(raised, axis=0, keepdims=True)
        for tile in range(pl.cdiv(rows, COLUMN_TILE)):
            first = tile * COLUMN_TILE
            inside = (local >= first) & (local < first + COLUMN_TILE)
            most = jnp.max(jnp.sum(inside.astype(jnp.int32), axis=0))
            if block == 0:
                row_counts[tile] = most
            else:
                column_counts[tile * (SIDE - 1) + block - 1] = most


def lookup_kernel(rows, share, packs, cot, packed_cot, packed_ids, chunks, tokens):
    mine, z, y, core = here()
    offset = block_offset(rows, z, y, core)
    count = tokens.shape[1]
    blocks = count // BLOCK
    for index in range(blocks):
        start = lax.rem(mine + OFFSETS[index], blocks) * BLOCK
        for half in range(BLOCK // HALF):
            lanes = pl.ds(pl.multiple_of(start + half * HALF, HALF), HALF)
            tokens[:, lanes] = packs[index, share + half : share + half + 1]
    local = tokens[...].astype(jnp.int32) - offset
    inside = (local >= 0) & (local < rows)
    hit = jnp.broadcast_to(jnp.where(inside, 1.0, 0.0), (8, count))
    before = lax.broadcasted_iota(jnp.int32, (count, count), 0)
    after = lax.broadcasted_iota(jnp.int32, (count, count), 1)
    upto = jnp.where(before <= after, 1.0, 0.0).astype(jnp.bfloat16)
    running = dot_nn(hit.astype(jnp.bfloat16), upto)[0:1].astype(jnp.int32)
    rank = jnp.where(inside, running - 1, -1)
    total = jnp.max(running)
    chunks[0] = (total + BLOCK - 1) // BLOCK
    safe = jnp.where(inside, local, 0)
    high = jnp.broadcast_to((safe >> 6).astype(jnp.float32), (8, count)).astype(jnp.bfloat16)
    low = jnp.broadcast_to((safe & 63).astype(jnp.float32), (8, count)).astype(jnp.bfloat16)
    for chunk in range(blocks):

        @pl.when(chunk * BLOCK < jnp.maximum(total, 1))
        def _():
            slot = lax.broadcasted_iota(jnp.int32, (BLOCK, count), 0) + chunk * BLOCK
            chosen = jnp.where(slot == rank, 1.0, 0.0).astype(jnp.bfloat16)
            columns = cot.shape[0] // blocks
            taken = jnp.zeros((columns, BLOCK), jnp.float32)
            for block in range(blocks):
                span = slice(block * BLOCK, (block + 1) * BLOCK)
                part = cot[block * columns : (block + 1) * columns].astype(jnp.bfloat16)
                taken = taken + dot_nt(part, chosen[:, span])
            packed_cot[chunk] = taken.astype(jnp.bfloat16)
            row = dot_nt(high, chosen)[0:1] * 64.0 + dot_nt(low, chosen)[0:1]
            used = dot_nt(hit.astype(jnp.bfloat16), chosen)[0:1] > 0.5
            packed_ids[chunk] = jnp.where(used, row.astype(jnp.int32), -1)


def next_slot(relative, prob, last):
    following = jnp.min(jnp.where(relative > last, relative, FAR), axis=0, keepdims=True)
    chance = jnp.sum(jnp.where(relative == following, prob, 0.0), axis=0, keepdims=True)
    return following, chance


def join_halves(near, far, joined):
    _, z, y, core = here()
    pair = near.shape[0] // (SIDE * SIDE)
    for side, source in ((core, near), (1 - core, far)):
        lanes = pl.ds(pl.multiple_of(side * HALF, HALF), HALF)
        for outer in range(SIDE):
            for inner in range(SIDE):
                start = (outer * SIDE + inner) * pair
                into = pl.multiple_of(chip_of(outer, inner, side, z, y) * pair, 16)
                joined[pl.ds(into, pair), lanes] = source[start : start + pair]


def table_copy(step, table, held, ready):
    rows = pl.ds(pl.multiple_of(step * ROW_STEP, CHUNK), ROW_STEP)
    return pltpu.make_async_copy(table.at[rows], held.at[rows], ready.at[step])


def logit_kernel(blocks, fresh, embed, *refs):
    near, far = refs[:blocks], refs[blocks : 2 * blocks]
    squashed, total, columns = refs[2 * blocks : 2 * blocks + 3]
    rest = refs[2 * blocks + 3 :]
    step = pl.program_id(0)
    steps = pl.num_programs(0)
    if fresh:
        held, hidden, sums, ready = rest

        @pl.when(step == 0)
        def _():
            for index in range(held.shape[0] // ROW_STEP):
                table_copy(index, embed, held, ready).start()

    else:
        held, (hidden, sums) = embed, rest

    @pl.when(step == 0)
    def _():
        sums[...] = jnp.zeros_like(sums)
        size = columns.shape[1]
        start = pl.multiple_of(lax.axis_index("dp") * size, 16)
        for block in range(blocks):
            join_halves(near[block], far[block], hidden.at[block])
            columns[block] = hidden[block, pl.ds(start, size)]

    if fresh:
        table_copy(step, embed, held, ready).wait()

    length = squashed.shape[0]
    for first in range(0, length, ROW_TILE):
        from_table = pl.ds(pl.multiple_of(step * length + first, CHUNK), ROW_TILE)
        for block in range(blocks):
            span = slice(block * BLOCK, (block + 1) * BLOCK)
            raw = dot_nn(held[from_table], hidden[block])
            raised = jnp.zeros((8, BLOCK), jnp.float32)
            for chunk in range(0, ROW_TILE, CHUNK):
                ratio = jnp.tanh(raw[chunk : chunk + CHUNK] * (1.0 / SOFT_CAP))
                squashed[first + chunk : first + chunk + CHUNK, span] = ratio
                power = jnp.exp2(ratio * (SOFT_CAP * LOG2_E))
                raised = raised + (power[:8] + power[8:])
            sums[:, span] += raised

    @pl.when(step == steps - 1)
    def _():
        total[...] = jnp.sum(sums[...], axis=0, keepdims=True)


def logit_grads(squashed, grads, log_share, relative, chances, fast, count, term=None):
    size = grads.shape[0]
    last = jnp.full((1, BLOCK), -1, jnp.int32)
    slots = []
    for _ in range(fast):
        last, chance = next_slot(relative, chances, last)
        slots.append((last, chance * LOSS_SCALE))

    def gradient(ratio, target):
        share = jnp.exp2(ratio * (SOFT_CAP * LOG2_E) + log_share)
        return ((share - target) * (1.0 - ratio * ratio)).astype(jnp.bfloat16)

    def place(row, target):
        for where, value in slots:
            target = jnp.where(row == where, value, target)
        return target

    if count is None:
        row = lax.broadcasted_iota(jnp.int32, (CHUNK, BLOCK), 0)
        added = jnp.zeros((8, BLOCK), jnp.float32)
        for chunk in range(0, size, CHUNK):
            ratio = squashed[chunk : chunk + CHUNK]
            target = place(row + chunk, jnp.zeros((CHUNK, BLOCK), jnp.float32))
            grads[chunk : chunk + CHUNK] = gradient(ratio, target)
            if term is not None:
                product = target * ratio
                added = added + (product[:8] + product[8:])
        if term is not None:
            term[...] += added
        return

    row = lax.broadcasted_iota(jnp.int32, (size, BLOCK), 0)
    target = place(row, jnp.zeros((size, BLOCK), jnp.float32))

    def more(_, held):
        last, target = held
        last, chance = next_slot(relative, chances, last)
        return last, jnp.where(row == last, chance * LOSS_SCALE, target)

    _, target = lax.fori_loop(fast, count, more, (last, target))
    ratio = squashed[...]
    grads[...] = gradient(ratio, target)
    if term is not None:
        term[...] += jnp.sum((target * ratio).reshape(size // 8, 8, BLOCK), axis=0)


def hidden_grad_kernel(
    counts, embed, squashed, total, ids, prob, grads, keep, give, rows_grad, flipped, term
):
    rows, width = embed.shape
    log_share = jnp.log2(LOSS_SCALE / total[:, 0:BLOCK])
    term[...] = jnp.zeros_like(term)
    tiles = pl.cdiv(rows, GRAD_TILE)

    def work(careful):
        for tile in range(tiles):
            first = tile * GRAD_TILE
            span = pl.ds(first, min(GRAD_TILE, rows - first))
            for start in range(first, min(first + GRAD_TILE, rows), COLUMN_TILE):
                part = pl.ds(start, min(COLUMN_TILE, rows - start))
                logit_grads(
                    squashed.at[part],
                    grads.at[part],
                    log_share,
                    ids[0] - start,
                    prob[0],
                    HIDDEN_SLOTS,
                    counts[start // COLUMN_TILE] if careful else None,
                    term,
                )
            product = dot_tn(grads[span], embed[span])
            if tile == 0:
                rows_grad[...] = product
            else:
                rows_grad[...] += product

    most = counts[0]
    for tile in range(1, pl.cdiv(rows, COLUMN_TILE)):
        most = jnp.maximum(most, counts[tile])

    @pl.when(most <= HIDDEN_SLOTS)
    def _():
        work(False)

    @pl.when(most > HIDDEN_SLOTS)
    def _():
        work(True)

    _, z, y, core = here()
    thin = keep.shape[2] - 8
    for part in range(width // BLOCK):
        span = slice(part * BLOCK, (part + 1) * BLOCK)
        flipped[span, :] = rows_grad[:, span].T
    summed = jnp.sum(term[...], axis=0, keepdims=True) * (SOFT_CAP / LOSS_SCALE)
    for outer in range(SIDE):
        for inner in range(SIDE):
            for ref, side in ((keep, core), (give, 1 - core)):
                rank = 2 * chip_of(outer, inner, side, z, y) + side
                start = pl.multiple_of(rank * thin, 8)
                ref[outer, inner, 0:thin] = flipped[pl.ds(start, thin)]
                ref[outer, inner, thin : thin + 8] = jnp.broadcast_to(summed, (8, BLOCK))


def halve_kernel(keep, got, *outs):
    for index, out in enumerate(outs):
        out[...] = keep[index] + got[index]


def quarter_kernel(*refs):
    parts, outs = refs[:SIDE], refs[SIDE:]
    for index, out in enumerate(outs):
        out[...] = (parts[0][index] + parts[1][index]) + (parts[2][index] + parts[3][index])


def finish_kernel(total, teacher_logits, *refs):
    parts, (hidden_grad, divergence) = refs[:SIDE], refs[SIDE:]
    _, z, y, core = here()
    summed = (parts[0][...] + parts[1][...]) + (parts[2][...] + parts[3][...])
    thin = hidden_grad.shape[0]
    hidden_grad[...] = summed[:thin].astype(jnp.bfloat16)
    scores = teacher_logits[...]
    share = scores.shape[0]
    shifted = scores - jnp.max(scores, axis=1, keepdims=True)
    raised = jnp.exp(shifted)
    prob = raised / jnp.sum(raised, axis=1, keepdims=True)
    entropy = jnp.sum(prob * jnp.log(prob), axis=1, keepdims=True)
    rest = jnp.log(total[:, 0:BLOCK]) - summed[thin : thin + 1]
    first = ((z * SIDE + y) * 2 + core) * share
    lane = lax.broadcasted_iota(jnp.int32, (share, BLOCK), 1)
    token = lax.broadcasted_iota(jnp.int32, (share, BLOCK), 0) + first
    value = entropy + jnp.sum(jnp.where(lane == token, rest, 0.0), axis=1, keepdims=True)
    line = lax.broadcasted_iota(jnp.int32, (share, HALF), 0)
    column = lax.broadcasted_iota(jnp.int32, (share, HALF), 1)
    divergence[...] = jnp.sum(jnp.where(line == column, value, 0.0), axis=0, keepdims=True)


def table_grad_kernel(
    rows,
    width,
    fresh,
    counts,
    chunks,
    own_grads,
    side_squashed,
    far_squashed,
    total,
    ids,
    prob,
    packed_cot,
    packed_ids,
    own_columns,
    side_columns,
    far_columns,
    *refs,
):
    blocks = SIDE - 1
    tiles = pl.cdiv(rows, COLUMN_TILE)
    half = tiles // 2
    tail = rows - (tiles - 1) * COLUMN_TILE
    embed_grad, grads = refs[-2:]

    def work(tile, base, size, out, careful):
        span = pl.ds(base, size)
        spread = dot_nt(own_columns[0], own_grads[span])
        for block in range(blocks):
            lanes = slice(block * BLOCK, (block + 1) * BLOCK)
            held = far_squashed.at[span] if block == 2 else side_squashed.at[span, lanes]
            log_share = jnp.log2(LOSS_SCALE / total[:, (block + 1) * BLOCK : (block + 2) * BLOCK])
            relative = ids[block + 1] - tile * COLUMN_TILE
            count = counts[tile * blocks + block] if careful else None
            fresh_grads = grads.at[block, pl.ds(0, size)]
            logit_grads(
                held, fresh_grads, log_share, relative, prob[block + 1], FAST_SLOTS, count
            )
            columns = far_columns[0] if block == 2 else side_columns[block]
            spread = spread + dot_nt(columns, fresh_grads[...])

        def lookup(chunk, held):
            column = lax.broadcasted_iota(jnp.int32, (size, BLOCK), 0) + tile * COLUMN_TILE
            onehot = jnp.where(column == packed_ids[chunk], math.sqrt(width), 0.0)
            return held + dot_nt(packed_cot[chunk], onehot.astype(jnp.bfloat16))

        spread = lookup(0, spread)
        spread = lax.fori_loop(1, chunks[0], lookup, spread)
        out[:, 0:size] = spread.astype(jnp.bfloat16)

    def choose(now, tile, base, size, out):
        most = counts[tile * blocks]
        for block in range(1, blocks):
            most = jnp.maximum(most, counts[tile * blocks + block])
        for careful, chosen in ((False, most <= FAST_SLOTS), (True, most > FAST_SLOTS)):

            @pl.when(now & chosen)
            def _(careful=careful):
                work(tile, base, size, out, careful)

    step = pl.program_id(0)
    if fresh:
        choose(step >= 0, step, 0, COLUMN_TILE, embed_grad)
        return

    @pl.when(step < half)
    def _():
        embed_grad[...] = refs[0][...]

    tile = jnp.maximum(step, half)
    choose((step >= half) & (step < tiles - 1), tile, 0, COLUMN_TILE, embed_grad)
    choose(step == tiles - 1, tile, 0, tail, embed_grad)


def smem():
    return pl.BlockSpec(memory_space=pltpu.SMEM)


def vmem():
    return pl.BlockSpec(memory_space=pltpu.VMEM)


def whole(shape):
    return pl.BlockSpec(shape, lambda *_: (0,) * len(shape))


def shape_of(shape, dtype):
    return jax.ShapeDtypeStruct(shape, dtype)


def small_call(kernel, name, outs, *args, scratch=(), limit=4 << 20):
    return pl.pallas_call(
        kernel,
        out_shape=tuple(shape_of(shape, dtype) for shape, dtype, _ in outs),
        in_specs=[vmem()] * len(args),
        out_specs=tuple(space() for _, _, space in outs),
        scratch_shapes=scratch,
        compiler_params=pltpu.CompilerParams(vmem_limit_bytes=limit),
        name=name,
    )(*args)


def logits_call(embed, near, far, columns, fresh):
    blocks = len(near)
    rows, width = embed.shape
    tokens = blocks * BLOCK
    length = ROW_STEP if fresh else LONG_STEP
    steps = rows // length
    table = whole((rows, width))
    out_specs = [
        pl.BlockSpec((length, tokens), lambda n: (n, 0)),
        whole((1, tokens)),
        whole((blocks, columns, BLOCK)),
    ]
    out_shape = [
        shape_of((rows, tokens), jnp.float32),
        shape_of((1, tokens), jnp.float32),
        shape_of((blocks, columns, BLOCK), jnp.bfloat16),
    ]
    scratch = [
        pltpu.VMEM((blocks, width, BLOCK), jnp.bfloat16),
        pltpu.VMEM((8, tokens), jnp.float32),
    ]
    if fresh:
        out_specs.append(table)
        out_shape.append(pltpu.VMEM((rows, width), embed.dtype))
        scratch.append(pltpu.SemaphoreType.DMA((steps,)))
    return pl.pallas_call(
        functools.partial(logit_kernel, blocks, fresh),
        grid=(steps,),
        in_specs=[pl.BlockSpec(memory_space=pltpu.HBM) if fresh else table]
        + [whole((width, HALF))] * (2 * blocks),
        out_specs=out_specs,
        out_shape=out_shape,
        scratch_shapes=scratch,
        compiler_params=pltpu.CompilerParams(vmem_limit_bytes=(4 + 3 * blocks) << 20),
        cost_estimate=pl.CostEstimate(
            flops=2 * rows * width * tokens,
            bytes_accessed=rows * tokens * 4 + (2 * rows * width if fresh else 0),
            transcendentals=2 * rows * tokens,
        ),
        name=f"logits_{blocks}",
    )(pltpu.with_memory_space_constraint(embed, pltpu.HBM) if fresh else embed, *near, *far)


def index_of(x, z, y, core):
    return ((x * SIDE + z) * SIDE + y) * 2 + core


def route_by(target):
    pairs = []
    for x in range(SIDE):
        for z in range(SIDE):
            for y in range(SIDE):
                for core in range(2):
                    pairs.append((index_of(x, z, y, core), index_of(*target(x, z, y, core))))
    return pairs


def along(axis, core, by, place):
    x, z, y = place
    if axis == 2:
        x = (x + (by if core == 0 else -by)) % SIDE
    elif axis == core:
        y = (y + by) % SIDE
    else:
        z = (z + by) % SIDE
    return x, z, y, core


def fetch(value, axis, by):
    return lax.ppermute(value, EVERY, route_by(lambda x, z, y, c: along(axis, c, -by, (x, z, y))))


def hand_on(value, axis, by):
    return lax.ppermute(value, EVERY, route_by(lambda x, z, y, c: along(axis, c, by, (x, z, y))))


def swap(value):
    return lax.ppermute(value, EVERY, route_by(lambda x, z, y, c: (x, z, y, 1 - c)))


def fetch_parts(value, axis):
    return [value] + [fetch(value, axis, by) for by in OFFSETS[1:]]


def fetch_all(value, axis):
    return jnp.concatenate(fetch_parts(value, axis), axis=0)


def halves(core_zero, low, high):
    return jnp.where(core_zero, low, high), jnp.where(core_zero, high, low)


def in_core_order(core_zero, kept, got):
    return jnp.where(
        core_zero, jnp.concatenate([kept, got], 0), jnp.concatenate([got, kept], 0)
    )


def side_values(core_zero, after, token_ids, lookup_cot, teacher_ids, teacher_logits):
    here_tokens, thin = lookup_cot.shape
    share = teacher_ids.shape[0]
    pack = jnp.concatenate(
        [
            jnp.concatenate([teacher_logits, teacher_ids.astype(jnp.float32)], axis=1),
            token_ids.astype(jnp.float32).reshape(here_tokens // HALF, HALF),
            jnp.zeros((8 - here_tokens // HALF, HALF), jnp.float32),
        ],
        axis=0,
    )
    pack, turned, _ = lax.optimization_barrier((pack, lookup_cot.T, after))
    moved = lax.ppermute(
        turned,
        EVERY,
        route_by(lambda x, z, y, c: (z, x, y, c)),
    ).astype(jnp.float32)
    packs = [pack] + [
        lax.ppermute(pack, "dp", [((k + by) % SIDE, k) for k in range(SIDE)])
        for by in OFFSETS[1:]
    ]
    far_away = [packs[0], packs[1], packs[3], packs[2]]
    sides = [
        jnp.concatenate(
            [
                moved[:, half * HALF : (half + 1) * HALF],
                far_away[2 * half][:share],
                far_away[2 * half + 1][:share],
            ],
            axis=0,
        )
        for half in range(2)
    ]
    kept, given = halves(core_zero, *sides)
    return in_core_order(core_zero, kept, swap(given)), jnp.stack(packs)


def per_device(hidden, embed, token_ids, lookup_cot, teacher_ids, teacher_logits):
    rows, width = embed.shape
    here_tokens, thin = hidden.shape
    dp = SIDE
    vocab = 2 * SIDE * SIDE
    tokens = here_tokens * dp
    top = teacher_ids.shape[1]
    share = here_tokens // vocab
    columns = width // dp
    core_zero = lax.axis_index("core") == 0

    flat = hidden.T
    kept, given = halves(core_zero, flat[:, :HALF], flat[:, HALF:])
    pair = in_core_order(core_zero, kept, swap(given))
    own_near = fetch_all(fetch_all(pair, 0), 1)
    first_near = fetch(own_near, 2, 1)
    second_near = fetch(own_near, 2, -1)
    own_far = swap(own_near)
    own_squashed, own_total, own_columns, table = logits_call(
        embed, [own_near], [own_far], columns, True
    )
    side, packs = side_values(
        core_zero, own_total, token_ids, lookup_cot, teacher_ids, teacher_logits
    )
    first_near, second_near, side, packs = lax.optimization_barrier(
        (first_near, second_near, side, packs)
    )
    opposite_near = fetch(first_near, 2, 1)
    first_far = swap(second_near)
    second_far = swap(first_near)
    side_parts = fetch_parts(side, 0)
    side_squashed, side_total, side_columns = logits_call(
        table, [first_near, second_near], [first_far, second_far], columns, False
    )
    side_parts, opposite_near, side_total = lax.optimization_barrier(
        (side_parts, opposite_near, side_total)
    )
    opposite_far = swap(opposite_near)
    side_parts = fetch_parts(jnp.concatenate(side_parts, axis=0), 1)
    far_squashed, far_total, far_columns = logits_call(
        table, [opposite_near], [opposite_far], columns, False
    )
    side_parts, far_total = lax.optimization_barrier((side_parts, far_total))
    side_near = jnp.concatenate(side_parts, axis=0)
    side_far = swap(side_near)

    total = jnp.concatenate([own_total, side_total, far_total], axis=1)
    got = swap(total)
    total = total + jnp.concatenate(
        [
            got[:, :BLOCK],
            got[:, 2 * BLOCK : 3 * BLOCK],
            got[:, BLOCK : 2 * BLOCK],
            got[:, 3 * BLOCK :],
        ],
        axis=1,
    )
    for axis in (0, 1):
        one, two, three = (fetch(total, axis, by) for by in OFFSETS[1:])
        total = (total + one) + (two + three)

    column_tiles = pl.cdiv(rows, COLUMN_TILE)
    cot, ids, prob, row_counts, column_counts = small_call(
        functools.partial(teacher_kernel, rows, thin),
        "teacher_prep",
        [
            ((width, BLOCK), jnp.float32, vmem),
            ((dp, top, BLOCK), jnp.int32, vmem),
            ((dp, top, BLOCK), jnp.float32, vmem),
            ((column_tiles,), jnp.int32, smem),
            ((column_tiles * (dp - 1),), jnp.int32, smem),
        ],
        side_near,
        side_far,
        scratch=[pltpu.VMEM((dp, BLOCK, 2 * top), jnp.float32)],
    )
    packed_cot, packed_ids, chunks = small_call(
        functools.partial(lookup_kernel, rows, share),
        "lookup_prep",
        [
            ((dp, columns, BLOCK), jnp.bfloat16, vmem),
            ((dp, 1, BLOCK), jnp.int32, vmem),
            ((1,), jnp.int32, smem),
        ],
        packs,
        cot,
        scratch=[pltpu.VMEM((1, tokens), jnp.float32)],
    )

    scattered = (SIDE, SIDE, thin + 8, BLOCK)
    own_grads, keep, give = pl.pallas_call(
        hidden_grad_kernel,
        in_specs=[smem()] + [vmem()] * 5,
        out_specs=[vmem()] * 3,
        out_shape=(
            shape_of((rows, BLOCK), jnp.bfloat16),
            shape_of(scattered, jnp.float32),
            shape_of(scattered, jnp.float32),
        ),
        scratch_shapes=[
            pltpu.VMEM((BLOCK, width), jnp.float32),
            pltpu.VMEM((width, BLOCK), jnp.float32),
            pltpu.VMEM((8, BLOCK), jnp.float32),
        ],
        compiler_params=pltpu.CompilerParams(vmem_limit_bytes=12 << 20),
        cost_estimate=pl.CostEstimate(
            flops=2 * rows * width * BLOCK,
            bytes_accessed=rows * BLOCK * 6,
            transcendentals=rows * BLOCK,
        ),
        name="hidden_grads",
    )(row_counts, table, own_squashed, total, ids, prob)

    half_tiles = column_tiles // 2

    def table_grads(so_far):
        fresh = so_far is None
        started = [] if fresh else [so_far]
        steps = half_tiles if fresh else column_tiles
        first = 0 if fresh else half_tiles
        operands = [
            column_counts,
            chunks,
            own_grads,
            side_squashed,
            far_squashed,
            total,
            ids,
            prob,
            packed_cot,
            packed_ids,
            own_columns,
            side_columns,
            far_columns,
        ]
        row_of = lambda n: (jnp.maximum(n, first), 0)
        made = (column_tiles - first if first else steps) * COLUMN_TILE
        return pl.pallas_call(
            functools.partial(table_grad_kernel, rows, width, fresh),
            grid=(steps,),
            in_specs=[
                smem(),
                smem(),
                pl.BlockSpec((COLUMN_TILE, BLOCK), row_of),
                pl.BlockSpec((COLUMN_TILE, 2 * BLOCK), row_of),
                pl.BlockSpec((COLUMN_TILE, BLOCK), row_of),
            ]
            + [whole(operand.shape) for operand in operands[5:]]
            + [
                pl.BlockSpec((columns, COLUMN_TILE), lambda n: (0, jnp.minimum(n, half_tiles - 1)))
                for _ in started
            ],
            out_specs=pl.BlockSpec((columns, COLUMN_TILE), lambda n: (0, n)),
            out_shape=pltpu.VMEM((columns, half_tiles * COLUMN_TILE), jnp.bfloat16)
            if fresh
            else shape_of((columns, rows), jnp.bfloat16),
            scratch_shapes=[pltpu.VMEM((dp - 1, COLUMN_TILE, BLOCK), jnp.bfloat16)],
            compiler_params=pltpu.CompilerParams(vmem_limit_bytes=10 << 20),
            cost_estimate=pl.CostEstimate(
                flops=2 * made * columns * (tokens + BLOCK),
                bytes_accessed=rows * columns * 2,
                transcendentals=made * tokens,
            ),
            name="table_grads_start" if fresh else "table_grads_rest",
        )(*operands, *started)

    quarter = (SIDE, thin + 8, BLOCK)
    got, packed_cot, packed_ids = lax.optimization_barrier((swap(give), packed_cot, packed_ids))
    parts = small_call(halve_kernel, "halve", [(quarter, jnp.float32, vmem)] * SIDE, keep, got)
    travelling = [hand_on(part, 1, by) for part, by in zip(parts[1:], OFFSETS[1:])]
    embed_grad = table_grads(None)
    travelling, embed_grad = lax.optimization_barrier((travelling, embed_grad))
    parts = small_call(
        quarter_kernel,
        "quarter",
        [(quarter[1:], jnp.float32, vmem)] * SIDE,
        parts[0],
        *travelling,
    )
    travelling = [hand_on(part, 0, by) for part, by in zip(parts[1:], OFFSETS[1:])]
    embed_grad = table_grads(embed_grad)
    parts = [parts[0]] + travelling

    hidden_grad, divergence = small_call(
        finish_kernel,
        "finish",
        [((thin, BLOCK), jnp.bfloat16, vmem), ((1, HALF), jnp.float32, vmem)],
        total,
        teacher_logits,
        *parts,
    )
    return (hidden_grad.T, embed_grad.T, divergence[0, :share])


def solution(mesh):
    dp, vocab = (mesh.shape[name] for name in ("dp", "vocab"))
    fine = Mesh(mesh.devices.reshape(dp, SIDE, SIDE, vocab // (SIDE * SIDE)), EVERY)
    return jax.shard_map(
        per_device,
        mesh=fine,
        in_specs=(
            P("dp", RING),
            P(RING, None),
            P("dp"),
            P("dp", RING),
            P(EVERY, None),
            P(EVERY, None),
        ),
        out_specs=(P("dp", RING), P(RING, "dp"), P(EVERY)),
        check_vma=False,
    )
```

```python
import functools
import math

import jax
import jax.numpy as jnp
from jax import lax
from jax.experimental import pallas as pl
from jax.experimental.pallas import tpu as pltpu
from jax.sharding import Mesh, PartitionSpec as P

SOFT_CAP = 30.0
LOSS_SCALE = 16.0
BLOCK = 256
HALF = 128
ROW_TILE = 400
ROW_STEP = 800
LONG_STEP = 2000
GRAD_TILE = 1024
CHUNK = 16
COLUMN_TILE = 512
FAST_SLOTS = 4
HIDDEN_SLOTS = 5
FAR = 1 << 30
LOG2_E = math.log2(math.e)
RING = ("z", "y", "core")
EVERY = ("dp",) + RING
SIDE = 4
OFFSETS = (0, 1, 3, 2)


def dot_nn(a, b):
    return lax.dot_general(a, b, (((1,), (0,)), ((), ())), preferred_element_type=jnp.float32)


def dot_nt(a, b):
    return lax.dot_general(a, b, (((1,), (1,)), ((), ())), preferred_element_type=jnp.float32)


def dot_tn(a, b):
    return lax.dot_general(a, b, (((0,), (0,)), ((), ())), preferred_element_type=jnp.float32)


def offset_of(index, core):
    return jnp.where(core == 0, OFFSETS[index], OFFSETS[(0, 2, 1, 3)[index]])


def chip_of(outer, inner, core, z, y):
    first, second = OFFSETS[inner], OFFSETS[outer]
    row = lax.rem(z + jnp.where(core == 0, second, first), SIDE)
    column = lax.rem(y + jnp.where(core == 0, first, second), SIDE)
    return row * SIDE + column


def here():
    return tuple(lax.axis_index(name) for name in EVERY)


def block_offset(rows, z, y, core):
    return ((z * SIDE + y) * 2 + core) * rows


def teacher_kernel(rows, thin, near, far, cot, ids, prob, row_counts, column_counts, joined):
    _, z, y, core = here()
    offset = block_offset(rows, z, y, core)
    top = ids.shape[1]
    share = 8
    group = thin + 2 * share
    for side, source in ((core, near), (1 - core, far)):
        lanes = pl.ds(pl.multiple_of(side * HALF, HALF), HALF)
        for outer in range(SIDE):
            for inner in range(SIDE):
                chip = chip_of(outer, inner, side, z, y)
                for other in range(2):
                    start = ((outer * SIDE + inner) * 2 + other) * group
                    rank = chip * 2 + other
                    into = pl.multiple_of(rank * thin, 8)
                    cot[pl.ds(into, thin), lanes] = source[start : start + thin]
                    for half in range(2):
                        held = source[start + thin + half * share : start + thin + (half + 1) * share]
                        joined[side * 2 + half, pl.ds(pl.multiple_of(rank * share, 8), share)] = held
    for block in range(SIDE):
        flipped = joined[offset_of(block, core)].T
        scores = flipped[:top]
        local = flipped[top:].astype(jnp.int32) - offset
        raised = jnp.exp(scores - jnp.max(scores, axis=0, keepdims=True))
        ids[block] = local
        prob[block] = raised / jnp.sum(raised, axis=0, keepdims=True)
        for tile in range(pl.cdiv(rows, COLUMN_TILE)):
            first = tile * COLUMN_TILE
            inside = (local >= first) & (local < first + COLUMN_TILE)
            most = jnp.max(jnp.sum(inside.astype(jnp.int32), axis=0))
            if block == 0:
                row_counts[tile] = most
            else:
                column_counts[tile * (SIDE - 1) + block - 1] = most


def lookup_kernel(rows, share, packs, cot, packed_cot, packed_ids, chunks, tokens):
    mine, z, y, core = here()
    offset = block_offset(rows, z, y, core)
    count = tokens.shape[1]
    blocks = count // BLOCK
    for index in range(blocks):
        start = lax.rem(mine + OFFSETS[index], blocks) * BLOCK
        for half in range(BLOCK // HALF):
            lanes = pl.ds(pl.multiple_of(start + half * HALF, HALF), HALF)
            tokens[:, lanes] = packs[index, share + half : share + half + 1]
    local = tokens[...].astype(jnp.int32) - offset
    inside = (local >= 0) & (local < rows)
    hit = jnp.broadcast_to(jnp.where(inside, 1.0, 0.0), (8, count))
    before = lax.broadcasted_iota(jnp.int32, (count, count), 0)
    after = lax.broadcasted_iota(jnp.int32, (count, count), 1)
    upto = jnp.where(before <= after, 1.0, 0.0).astype(jnp.bfloat16)
    running = dot_nn(hit.astype(jnp.bfloat16), upto)[0:1].astype(jnp.int32)
    rank = jnp.where(inside, running - 1, -1)
    total = jnp.max(running)
    chunks[0] = (total + BLOCK - 1) // BLOCK
    safe = jnp.where(inside, local, 0)
    high = jnp.broadcast_to((safe >> 6).astype(jnp.float32), (8, count)).astype(jnp.bfloat16)
    low = jnp.broadcast_to((safe & 63).astype(jnp.float32), (8, count)).astype(jnp.bfloat16)
    for chunk in range(blocks):

        @pl.when(chunk * BLOCK < jnp.maximum(total, 1))
        def _():
            slot = lax.broadcasted_iota(jnp.int32, (BLOCK, count), 0) + chunk * BLOCK
            chosen = jnp.where(slot == rank, 1.0, 0.0).astype(jnp.bfloat16)
            columns = cot.shape[0] // blocks
            taken = jnp.zeros((columns, BLOCK), jnp.float32)
            for block in range(blocks):
                span = slice(block * BLOCK, (block + 1) * BLOCK)
                part = cot[block * columns : (block + 1) * columns].astype(jnp.bfloat16)
                taken = taken + dot_nt(part, chosen[:, span])
            packed_cot[chunk] = taken.astype(jnp.bfloat16)
            row = dot_nt(high, chosen)[0:1] * 64.0 + dot_nt(low, chosen)[0:1]
            used = dot_nt(hit.astype(jnp.bfloat16), chosen)[0:1] > 0.5
            packed_ids[chunk] = jnp.where(used, row.astype(jnp.int32), -1)


def next_slot(relative, prob, last):
    following = jnp.min(jnp.where(relative > last, relative, FAR), axis=0, keepdims=True)
    chance = jnp.sum(jnp.where(relative == following, prob, 0.0), axis=0, keepdims=True)
    return following, chance


def join_halves(near, far, joined):
    _, z, y, core = here()
    pair = near.shape[0] // (SIDE * SIDE)
    for side, source in ((core, near), (1 - core, far)):
        lanes = pl.ds(pl.multiple_of(side * HALF, HALF), HALF)
        for outer in range(SIDE):
            for inner in range(SIDE):
                start = (outer * SIDE + inner) * pair
                into = pl.multiple_of(chip_of(outer, inner, side, z, y) * pair, 16)
                joined[pl.ds(into, pair), lanes] = source[start : start + pair]


def table_copy(step, table, held, ready):
    rows = pl.ds(pl.multiple_of(step * ROW_STEP, CHUNK), ROW_STEP)
    return pltpu.make_async_copy(table.at[rows], held.at[rows], ready.at[step])


def logit_kernel(blocks, fresh, embed, *refs):
    near, far = refs[:blocks], refs[blocks : 2 * blocks]
    squashed, total, columns = refs[2 * blocks : 2 * blocks + 3]
    rest = refs[2 * blocks + 3 :]
    step = pl.program_id(0)
    steps = pl.num_programs(0)
    if fresh:
        held, hidden, sums, ready = rest

        @pl.when(step == 0)
        def _():
            for index in range(held.shape[0] // ROW_STEP):
                table_copy(index, embed, held, ready).start()

    else:
        held, (hidden, sums) = embed, rest

    @pl.when(step == 0)
    def _():
        sums[...] = jnp.zeros_like(sums)
        size = columns.shape[1]
        start = pl.multiple_of(lax.axis_index("dp") * size, 16)
        for block in range(blocks):
            join_halves(near[block], far[block], hidden.at[block])
            columns[block] = hidden[block, pl.ds(start, size)]

    if fresh:
        table_copy(step, embed, held, ready).wait()

    length = squashed.shape[0]
    for first in range(0, length, ROW_TILE):
        from_table = pl.ds(pl.multiple_of(step * length + first, CHUNK), ROW_TILE)
        for block in range(blocks):
            span = slice(block * BLOCK, (block + 1) * BLOCK)
            raw = dot_nn(held[from_table], hidden[block])
            raised = jnp.zeros((8, BLOCK), jnp.float32)
            for chunk in range(0, ROW_TILE, CHUNK):
                ratio = jnp.tanh(raw[chunk : chunk + CHUNK] * (1.0 / SOFT_CAP))
                squashed[first + chunk : first + chunk + CHUNK, span] = ratio
                power = jnp.exp2(ratio * (SOFT_CAP * LOG2_E))
                raised = raised + (power[:8] + power[8:])
            sums[:, span] += raised

    @pl.when(step == steps - 1)
    def _():
        total[...] = jnp.sum(sums[...], axis=0, keepdims=True)


def logit_grads(squashed, grads, log_share, relative, chances, fast, count, term=None):
    size = grads.shape[0]
    last = jnp.full((1, BLOCK), -1, jnp.int32)
    slots = []
    for _ in range(fast):
        last, chance = next_slot(relative, chances, last)
        slots.append((last, chance * LOSS_SCALE))

    def gradient(ratio, target):
        share = jnp.exp2(ratio * (SOFT_CAP * LOG2_E) + log_share)
        return ((share - target) * (1.0 - ratio * ratio)).astype(jnp.bfloat16)

    def place(row, target):
        for where, value in slots:
            target = jnp.where(row == where, value, target)
        return target

    if count is None:
        row = lax.broadcasted_iota(jnp.int32, (CHUNK, BLOCK), 0)
        added = jnp.zeros((8, BLOCK), jnp.float32)
        for chunk in range(0, size, CHUNK):
            ratio = squashed[chunk : chunk + CHUNK]
            target = place(row + chunk, jnp.zeros((CHUNK, BLOCK), jnp.float32))
            grads[chunk : chunk + CHUNK] = gradient(ratio, target)
            if term is not None:
                product = target * ratio
                added = added + (product[:8] + product[8:])
        if term is not None:
            term[...] += added
        return

    row = lax.broadcasted_iota(jnp.int32, (size, BLOCK), 0)
    target = place(row, jnp.zeros((size, BLOCK), jnp.float32))

    def more(_, held):
        last, target = held
        last, chance = next_slot(relative, chances, last)
        return last, jnp.where(row == last, chance * LOSS_SCALE, target)

    _, target = lax.fori_loop(fast, count, more, (last, target))
    ratio = squashed[...]
    grads[...] = gradient(ratio, target)
    if term is not None:
        term[...] += jnp.sum((target * ratio).reshape(size // 8, 8, BLOCK), axis=0)


def hidden_grad_kernel(
    counts, embed, squashed, total, ids, prob, grads, keep, give, rows_grad, flipped, term
):
    rows, width = embed.shape
    log_share = jnp.log2(LOSS_SCALE / total[:, 0:BLOCK])
    term[...] = jnp.zeros_like(term)
    tiles = pl.cdiv(rows, GRAD_TILE)

    def work(careful):
        for tile in range(tiles):
            first = tile * GRAD_TILE
            span = pl.ds(first, min(GRAD_TILE, rows - first))
            for start in range(first, min(first + GRAD_TILE, rows), COLUMN_TILE):
                part = pl.ds(start, min(COLUMN_TILE, rows - start))
                logit_grads(
                    squashed.at[part],
                    grads.at[part],
                    log_share,
                    ids[0] - start,
                    prob[0],
                    HIDDEN_SLOTS,
                    counts[start // COLUMN_TILE] if careful else None,
                    term,
                )
            product = dot_tn(grads[span], embed[span])
            if tile == 0:
                rows_grad[...] = product
            else:
                rows_grad[...] += product

    most = counts[0]
    for tile in range(1, pl.cdiv(rows, COLUMN_TILE)):
        most = jnp.maximum(most, counts[tile])

    @pl.when(most <= HIDDEN_SLOTS)
    def _():
        work(False)

    @pl.when(most > HIDDEN_SLOTS)
    def _():
        work(True)

    _, z, y, core = here()
    thin = keep.shape[2] - 8
    for part in range(width // BLOCK):
        span = slice(part * BLOCK, (part + 1) * BLOCK)
        flipped[span, :] = rows_grad[:, span].T
    summed = jnp.sum(term[...], axis=0, keepdims=True) * (SOFT_CAP / LOSS_SCALE)
    for outer in range(SIDE):
        for inner in range(SIDE):
            for ref, side in ((keep, core), (give, 1 - core)):
                rank = 2 * chip_of(outer, inner, side, z, y) + side
                start = pl.multiple_of(rank * thin, 8)
                ref[outer, inner, 0:thin] = flipped[pl.ds(start, thin)]
                ref[outer, inner, thin : thin + 8] = jnp.broadcast_to(summed, (8, BLOCK))


def halve_kernel(keep, got, *outs):
    for index, out in enumerate(outs):
        out[...] = keep[index] + got[index]


def quarter_kernel(*refs):
    parts, outs = refs[:SIDE], refs[SIDE:]
    for index, out in enumerate(outs):
        out[...] = (parts[0][index] + parts[1][index]) + (parts[2][index] + parts[3][index])


def finish_kernel(total, teacher_logits, *refs):
    parts, (hidden_grad, divergence) = refs[:SIDE], refs[SIDE:]
    _, z, y, core = here()
    summed = (parts[0][...] + parts[1][...]) + (parts[2][...] + parts[3][...])
    thin = hidden_grad.shape[0]
    hidden_grad[...] = summed[:thin].astype(jnp.bfloat16)
    scores = teacher_logits[...]
    share = scores.shape[0]
    shifted = scores - jnp.max(scores, axis=1, keepdims=True)
    raised = jnp.exp(shifted)
    prob = raised / jnp.sum(raised, axis=1, keepdims=True)
    entropy = jnp.sum(prob * jnp.log(prob), axis=1, keepdims=True)
    rest = jnp.log(total[:, 0:BLOCK]) - summed[thin : thin + 1]
    first = ((z * SIDE + y) * 2 + core) * share
    lane = lax.broadcasted_iota(jnp.int32, (share, BLOCK), 1)
    token = lax.broadcasted_iota(jnp.int32, (share, BLOCK), 0) + first
    value = entropy + jnp.sum(jnp.where(lane == token, rest, 0.0), axis=1, keepdims=True)
    line = lax.broadcasted_iota(jnp.int32, (share, HALF), 0)
    column = lax.broadcasted_iota(jnp.int32, (share, HALF), 1)
    divergence[...] = jnp.sum(jnp.where(line == column, value, 0.0), axis=0, keepdims=True)


def table_grad_kernel(
    rows,
    width,
    fresh,
    counts,
    chunks,
    own_grads,
    side_squashed,
    far_squashed,
    total,
    ids,
    prob,
    packed_cot,
    packed_ids,
    own_columns,
    side_columns,
    far_columns,
    *refs,
):
    blocks = SIDE - 1
    tiles = pl.cdiv(rows, COLUMN_TILE)
    half = tiles // 2
    out, left, grads = refs[-3:]
    first = 0 if fresh else half
    mine = range(first, half if fresh else tiles)
    now = pl.program_id(0) == pl.num_programs(0) - 1

    if not fresh:

        @pl.when(jnp.logical_not(now))
        def _():
            out[...] = refs[0][...]

    log_share = jnp.log2(LOSS_SCALE / total[...])

    def onehot(tile, size, chunk):
        column = lax.broadcasted_iota(jnp.int32, (size, BLOCK), 0) + tile * COLUMN_TILE
        chosen = jnp.where(column == packed_ids[chunk], math.sqrt(width), 0.0)
        return chosen.astype(jnp.bfloat16)

    def fill(index, tile, size, careful):
        span = pl.ds(tile * COLUMN_TILE, size)
        for block in range(blocks):
            lanes = pl.ds(block * BLOCK, BLOCK)
            held = far_squashed.at[span] if block == 2 else side_squashed.at[span, lanes]
            logit_grads(
                held,
                grads.at[index, pl.ds(0, size), pl.ds((block + 1) * BLOCK, BLOCK)],
                log_share[:, (block + 1) * BLOCK : (block + 2) * BLOCK],
                ids[block + 1] - tile * COLUMN_TILE,
                prob[block + 1],
                FAST_SLOTS,
                counts[tile * blocks + block] if careful else None,
            )

    def keep(tile, size, value):
        start = (tile - first) * COLUMN_TILE
        out[:, start : start + size] = value.astype(jnp.bfloat16)

    sizes = [min(COLUMN_TILE, rows - tile * COLUMN_TILE) for tile in mine]

    @pl.when(now)
    def _():
        left[:, 0:BLOCK] = own_columns[0]
        left[:, BLOCK : 2 * BLOCK] = side_columns[0]
        left[:, 2 * BLOCK : 3 * BLOCK] = side_columns[1]
        left[:, 3 * BLOCK : 4 * BLOCK] = far_columns[0]
        left[:, 4 * BLOCK :] = packed_cot[0]
        for index, (tile, size) in enumerate(zip(mine, sizes)):
            grads[index, 0:size, 0:BLOCK] = own_grads[pl.ds(tile * COLUMN_TILE, size)]
            grads[index, 0:size, 4 * BLOCK :] = onehot(tile, size, 0)
            fill(index, tile, size, False)
            keep(tile, size, dot_nt(left[...], grads[index, 0:size]))

    for index, (tile, size) in enumerate(zip(mine, sizes)):
        most = counts[tile * blocks]
        for block in range(1, blocks):
            most = jnp.maximum(most, counts[tile * blocks + block])

        @pl.when(now & ((most > FAST_SLOTS) | (chunks[0] > 1)))
        def _(index=index, tile=tile, size=size):
            fill(index, tile, size, True)
            spread = lax.fori_loop(
                1,
                chunks[0],
                lambda chunk, held: held + dot_nt(packed_cot[chunk], onehot(tile, size, chunk)),
                dot_nt(left[...], grads[index, 0:size]),
            )
            keep(tile, size, spread)


def smem():
    return pl.BlockSpec(memory_space=pltpu.SMEM)


def vmem():
    return pl.BlockSpec(memory_space=pltpu.VMEM)


def whole(shape):
    return pl.BlockSpec(shape, lambda *_: (0,) * len(shape))


def shape_of(shape, dtype):
    return jax.ShapeDtypeStruct(shape, dtype)


def small_call(kernel, name, outs, *args, scratch=(), limit=4 << 20):
    return pl.pallas_call(
        kernel,
        out_shape=tuple(shape_of(shape, dtype) for shape, dtype, _ in outs),
        in_specs=[vmem()] * len(args),
        out_specs=tuple(space() for _, _, space in outs),
        scratch_shapes=scratch,
        compiler_params=pltpu.CompilerParams(vmem_limit_bytes=limit),
        name=name,
    )(*args)


def logits_call(embed, near, far, columns, fresh):
    blocks = len(near)
    rows, width = embed.shape
    tokens = blocks * BLOCK
    length = ROW_STEP if fresh else LONG_STEP
    steps = rows // length
    table = whole((rows, width))
    out_specs = [
        pl.BlockSpec((length, tokens), lambda n: (n, 0)),
        whole((1, tokens)),
        whole((blocks, columns, BLOCK)),
    ]
    out_shape = [
        shape_of((rows, tokens), jnp.float32),
        shape_of((1, tokens), jnp.float32),
        shape_of((blocks, columns, BLOCK), jnp.bfloat16),
    ]
    scratch = [
        pltpu.VMEM((blocks, width, BLOCK), jnp.bfloat16),
        pltpu.VMEM((8, tokens), jnp.float32),
    ]
    if fresh:
        out_specs.append(table)
        out_shape.append(pltpu.VMEM((rows, width), embed.dtype))
        scratch.append(pltpu.SemaphoreType.DMA((steps,)))
    return pl.pallas_call(
        functools.partial(logit_kernel, blocks, fresh),
        grid=(steps,),
        in_specs=[pl.BlockSpec(memory_space=pltpu.HBM) if fresh else table]
        + [whole((width, HALF))] * (2 * blocks),
        out_specs=out_specs,
        out_shape=out_shape,
        scratch_shapes=scratch,
        compiler_params=pltpu.CompilerParams(vmem_limit_bytes=(4 + 3 * blocks) << 20),
        cost_estimate=pl.CostEstimate(
            flops=2 * rows * width * tokens,
            bytes_accessed=rows * tokens * 4 + (2 * rows * width if fresh else 0),
            transcendentals=2 * rows * tokens,
        ),
        name=f"logits_{blocks}",
    )(pltpu.with_memory_space_constraint(embed, pltpu.HBM) if fresh else embed, *near, *far)


def index_of(x, z, y, core):
    return ((x * SIDE + z) * SIDE + y) * 2 + core


def route_by(target):
    pairs = []
    for x in range(SIDE):
        for z in range(SIDE):
            for y in range(SIDE):
                for core in range(2):
                    pairs.append((index_of(x, z, y, core), index_of(*target(x, z, y, core))))
    return pairs


def along(axis, core, by, place):
    x, z, y = place
    if axis == 2:
        x = (x + (by if core == 0 else -by)) % SIDE
    elif axis == core:
        y = (y + by) % SIDE
    else:
        z = (z + by) % SIDE
    return x, z, y, core


def fetch(value, axis, by):
    return lax.ppermute(value, EVERY, route_by(lambda x, z, y, c: along(axis, c, -by, (x, z, y))))


def hand_on(value, axis, by):
    return lax.ppermute(value, EVERY, route_by(lambda x, z, y, c: along(axis, c, by, (x, z, y))))


def exchange(value, axis, bit):
    def other(x, z, y, core):
        return along(axis, core, ((y if axis == core else z) ^ bit) - (y if axis == core else z), (x, z, y))

    return lax.ppermute(value, EVERY, route_by(other))


def swap(value):
    return lax.ppermute(value, EVERY, route_by(lambda x, z, y, c: (x, z, y, 1 - c)))


def fetch_parts(value, axis):
    return [value] + [fetch(value, axis, by) for by in OFFSETS[1:]]


def fetch_all(value, axis):
    return jnp.concatenate(fetch_parts(value, axis), axis=0)


def halves(core_zero, low, high):
    return jnp.where(core_zero, low, high), jnp.where(core_zero, high, low)


def in_core_order(core_zero, kept, got):
    return jnp.where(
        core_zero, jnp.concatenate([kept, got], 0), jnp.concatenate([got, kept], 0)
    )


def side_values(core_zero, after, token_ids, lookup_cot, teacher_ids, teacher_logits):
    here_tokens, thin = lookup_cot.shape
    share = teacher_ids.shape[0]
    pack = jnp.concatenate(
        [
            jnp.concatenate([teacher_logits, teacher_ids.astype(jnp.float32)], axis=1),
            token_ids.astype(jnp.float32).reshape(here_tokens // HALF, HALF),
            jnp.zeros((8 - here_tokens // HALF, HALF), jnp.float32),
        ],
        axis=0,
    )
    pack, turned, _ = lax.optimization_barrier((pack, lookup_cot.T, after))
    moved = lax.ppermute(
        turned,
        EVERY,
        route_by(lambda x, z, y, c: (z, x, y, c)),
    ).astype(jnp.float32)
    packs = [pack] + [
        lax.ppermute(pack, "dp", [((k + by) % SIDE, k) for k in range(SIDE)])
        for by in OFFSETS[1:]
    ]
    far_away = [packs[0], packs[1], packs[3], packs[2]]
    sides = [
        jnp.concatenate(
            [
                moved[:, half * HALF : (half + 1) * HALF],
                far_away[2 * half][:share],
                far_away[2 * half + 1][:share],
            ],
            axis=0,
        )
        for half in range(2)
    ]
    return *halves(core_zero, *sides), jnp.stack(packs)


def per_device(hidden, embed, token_ids, lookup_cot, teacher_ids, teacher_logits):
    rows, width = embed.shape
    here_tokens, thin = hidden.shape
    dp = SIDE
    vocab = 2 * SIDE * SIDE
    tokens = here_tokens * dp
    top = teacher_ids.shape[1]
    share = here_tokens // vocab
    columns = width // dp
    core_zero = lax.axis_index("core") == 0

    flat = hidden.T
    kept, given = halves(core_zero, flat[:, :HALF], flat[:, HALF:])
    pair = in_core_order(core_zero, kept, swap(given))
    row = fetch_all(pair, 0)
    own_near = fetch_all(row, 1)
    side = side_values(core_zero, row, token_ids, lookup_cot, teacher_ids, teacher_logits)
    own_near, kept, given, packs = lax.optimization_barrier((own_near, *side))
    first_near = fetch(own_near, 2, 1)
    second_near = fetch(own_near, 2, -1)
    own_far = swap(own_near)
    own_squashed, own_total, own_columns, table = logits_call(
        embed, [own_near], [own_far], columns, True
    )
    given = lax.optimization_barrier((given, own_total))[0]
    side = in_core_order(core_zero, kept, swap(given))
    first_near, second_near, side = lax.optimization_barrier((first_near, second_near, side))
    opposite_near = fetch(first_near, 2, 1)
    first_far = swap(second_near)
    second_far = swap(first_near)
    side_parts = fetch_parts(side, 0)
    side_squashed, side_total, side_columns = logits_call(
        table, [first_near, second_near], [first_far, second_far], columns, False
    )
    side_parts, opposite_near, side_total = lax.optimization_barrier(
        (side_parts, opposite_near, side_total)
    )
    opposite_far = swap(opposite_near)
    side_parts = fetch_parts(jnp.concatenate(side_parts, axis=0), 1)
    far_squashed, far_total, far_columns = logits_call(
        table, [opposite_near], [opposite_far], columns, False
    )
    side_parts, far_total = lax.optimization_barrier((side_parts, far_total))
    side_near = jnp.concatenate(side_parts, axis=0)
    side_far = swap(side_near)

    total = jnp.concatenate([own_total, side_total, far_total], axis=1)
    got = swap(total)
    total = total + jnp.concatenate(
        [
            got[:, :BLOCK],
            got[:, 2 * BLOCK : 3 * BLOCK],
            got[:, BLOCK : 2 * BLOCK],
            got[:, 3 * BLOCK :],
        ],
        axis=1,
    )
    for axis in (0, 1):
        for bit in (1, 2):
            total = total + exchange(total, axis, bit)

    column_tiles = pl.cdiv(rows, COLUMN_TILE)
    cot, ids, prob, row_counts, column_counts = small_call(
        functools.partial(teacher_kernel, rows, thin),
        "teacher_prep",
        [
            ((width, BLOCK), jnp.float32, vmem),
            ((dp, top, BLOCK), jnp.int32, vmem),
            ((dp, top, BLOCK), jnp.float32, vmem),
            ((column_tiles,), jnp.int32, smem),
            ((column_tiles * (dp - 1),), jnp.int32, smem),
        ],
        side_near,
        side_far,
        scratch=[pltpu.VMEM((dp, BLOCK, 2 * top), jnp.float32)],
    )
    packed_cot, packed_ids, chunks = small_call(
        functools.partial(lookup_kernel, rows, share),
        "lookup_prep",
        [
            ((dp, columns, BLOCK), jnp.bfloat16, vmem),
            ((dp, 1, BLOCK), jnp.int32, vmem),
            ((1,), jnp.int32, smem),
        ],
        packs,
        cot,
        scratch=[pltpu.VMEM((1, tokens), jnp.float32)],
    )

    scattered = (SIDE, SIDE, thin + 8, BLOCK)
    own_grads, keep, give = pl.pallas_call(
        hidden_grad_kernel,
        in_specs=[smem()] + [vmem()] * 5,
        out_specs=[vmem()] * 3,
        out_shape=(
            shape_of((rows, BLOCK), jnp.bfloat16),
            shape_of(scattered, jnp.float32),
            shape_of(scattered, jnp.float32),
        ),
        scratch_shapes=[
            pltpu.VMEM((BLOCK, width), jnp.float32),
            pltpu.VMEM((width, BLOCK), jnp.float32),
            pltpu.VMEM((8, BLOCK), jnp.float32),
        ],
        compiler_params=pltpu.CompilerParams(vmem_limit_bytes=12 << 20),
        cost_estimate=pl.CostEstimate(
            flops=2 * rows * width * BLOCK,
            bytes_accessed=rows * BLOCK * 6,
            transcendentals=rows * BLOCK,
        ),
        name="hidden_grads",
    )(row_counts, table, own_squashed, total, ids, prob)

    half_tiles = column_tiles // 2

    def table_grads(so_far):
        fresh = so_far is None
        started = [] if fresh else [so_far]
        operands = [
            column_counts,
            chunks,
            own_grads,
            side_squashed,
            far_squashed,
            total,
            ids,
            prob,
            packed_cot,
            packed_ids,
            own_columns,
            side_columns,
            far_columns,
        ]
        made = half_tiles if fresh else column_tiles - half_tiles
        half = (columns, half_tiles * COLUMN_TILE)
        return pl.pallas_call(
            functools.partial(table_grad_kernel, rows, width, fresh),
            grid=(1 if fresh else 2,),
            in_specs=[smem()] * 2
            + [whole(operand.shape) for operand in operands[2:]]
            + [whole(half) for _ in started],
            out_specs=pl.BlockSpec(half, lambda n: (0, n)),
            out_shape=pltpu.VMEM(half, jnp.bfloat16)
            if fresh
            else shape_of((columns, rows), jnp.bfloat16),
            scratch_shapes=[
                pltpu.VMEM((columns, (dp + 1) * BLOCK), jnp.bfloat16),
                pltpu.VMEM((made, COLUMN_TILE, (dp + 1) * BLOCK), jnp.bfloat16),
            ],
            compiler_params=pltpu.CompilerParams(vmem_limit_bytes=20 << 20),
            cost_estimate=pl.CostEstimate(
                flops=2 * made * COLUMN_TILE * columns * (tokens + BLOCK),
                bytes_accessed=rows * columns * 2,
                transcendentals=made * COLUMN_TILE * tokens,
            ),
            name="table_grads_start" if fresh else "table_grads_rest",
        )(*operands, *started)

    quarter = (SIDE, thin + 8, BLOCK)
    got, packed_cot, packed_ids = lax.optimization_barrier((swap(give), packed_cot, packed_ids))
    parts = small_call(halve_kernel, "halve", [(quarter, jnp.float32, vmem)] * SIDE, keep, got)
    travelling = [hand_on(part, 1, by) for part, by in zip(parts[1:], OFFSETS[1:])]
    embed_grad = table_grads(None)
    travelling, embed_grad = lax.optimization_barrier((travelling, embed_grad))
    parts = small_call(
        quarter_kernel,
        "quarter",
        [(quarter[1:], jnp.float32, vmem)] * SIDE,
        parts[0],
        *travelling,
    )
    travelling = [hand_on(part, 0, by) for part, by in zip(parts[1:], OFFSETS[1:])]
    embed_grad = table_grads(embed_grad)
    parts = [parts[0]] + travelling

    hidden_grad, divergence = small_call(
        finish_kernel,
        "finish",
        [((thin, BLOCK), jnp.bfloat16, vmem), ((1, HALF), jnp.float32, vmem)],
        total,
        teacher_logits,
        *parts,
    )
    return (hidden_grad.T, embed_grad.T, divergence[0, :share])


def solution(mesh):
    dp, vocab = (mesh.shape[name] for name in ("dp", "vocab"))
    fine = Mesh(mesh.devices.reshape(dp, SIDE, SIDE, vocab // (SIDE * SIDE)), EVERY)
    return jax.shard_map(
        per_device,
        mesh=fine,
        in_specs=(
            P("dp", RING),
            P(RING, None),
            P("dp"),
            P("dp", RING),
            P(EVERY, None),
            P(EVERY, None),
        ),
        out_specs=(P("dp", RING), P(RING, "dp"), P(EVERY)),
        check_vma=False,
    )
```

```python
import functools
import math

import jax
import jax.numpy as jnp
from jax import lax
from jax.experimental import pallas as pl
from jax.experimental.pallas import tpu as pltpu
from jax.sharding import Mesh, PartitionSpec as P

SOFT_CAP = 30.0
LOSS_SCALE = 16.0
BLOCK = 256
HALF = 128
ROW_TILE = 400
ROW_STEP = 800
LONG_STEP = 2000
PADDED = 4096
STRIP = 16
GRAD_TILE = 512
TABLE_TILE = 256
FAST_SLOTS = 4
HIDDEN_SLOTS = 5
FAR = 1 << 30
LOG2_E = math.log2(math.e)
RING = ("z", "y", "core")
EVERY = ("dp",) + RING
SIDE = 4
OFFSETS = (0, 1, 3, 2)


def dot_nn(a, b):
    return lax.dot_general(a, b, (((1,), (0,)), ((), ())), preferred_element_type=jnp.float32)


def dot_nt(a, b):
    return lax.dot_general(a, b, (((1,), (1,)), ((), ())), preferred_element_type=jnp.float32)


def dot_tn(a, b):
    return lax.dot_general(a, b, (((0,), (0,)), ((), ())), preferred_element_type=jnp.float32)


def offset_of(index, core):
    return jnp.where(core == 0, OFFSETS[index], OFFSETS[(0, 2, 1, 3)[index]])


def chip_of(outer, inner, core, z, y):
    first, second = OFFSETS[inner], OFFSETS[outer]
    row = lax.rem(z + jnp.where(core == 0, second, first), SIDE)
    column = lax.rem(y + jnp.where(core == 0, first, second), SIDE)
    return row * SIDE + column


def here():
    return tuple(lax.axis_index(name) for name in EVERY)


def block_offset(rows, z, y, core):
    return ((z * SIDE + y) * 2 + core) * rows


def teacher_kernel(rows, thin, near, far, cot, ids, prob, row_counts, column_counts, joined):
    _, z, y, core = here()
    offset = block_offset(rows, z, y, core)
    top = ids.shape[1]
    share = 8
    group = thin + 2 * share
    for side, source in ((core, near), (1 - core, far)):
        lanes = pl.ds(pl.multiple_of(side * HALF, HALF), HALF)
        for outer in range(SIDE):
            for inner in range(SIDE):
                chip = chip_of(outer, inner, side, z, y)
                for other in range(2):
                    start = ((outer * SIDE + inner) * 2 + other) * group
                    rank = chip * 2 + other
                    into = pl.multiple_of(rank * thin, 8)
                    cot[pl.ds(into, thin), lanes] = source[start : start + thin]
                    for half in range(2):
                        held = source[start + thin + half * share : start + thin + (half + 1) * share]
                        joined[side * 2 + half, pl.ds(pl.multiple_of(rank * share, 8), share)] = held
    for block in range(SIDE):
        flipped = joined[offset_of(block, core)].T
        scores = flipped[:top]
        local = flipped[top:].astype(jnp.int32) - offset
        raised = jnp.exp(scores - jnp.max(scores, axis=0, keepdims=True))
        ids[block] = local
        prob[block] = raised / jnp.sum(raised, axis=0, keepdims=True)
        size = GRAD_TILE if block == 0 else TABLE_TILE
        for tile in range(PADDED // size):
            first = tile * size
            inside = (local >= first) & (local < min(first + size, rows))
            most = jnp.max(jnp.sum(inside.astype(jnp.int32), axis=0))
            if block == 0:
                row_counts[tile] = most
            else:
                column_counts[tile * (SIDE - 1) + block - 1] = most


def lookup_kernel(rows, share, packs, cot, packed_cot, packed_ids, chunks, tokens):
    mine, z, y, core = here()
    offset = block_offset(rows, z, y, core)
    count = tokens.shape[1]
    blocks = count // BLOCK
    for index in range(blocks):
        start = lax.rem(mine + OFFSETS[index], blocks) * BLOCK
        for half in range(BLOCK // HALF):
            lanes = pl.ds(pl.multiple_of(start + half * HALF, HALF), HALF)
            tokens[:, lanes] = packs[index, share + half : share + half + 1]
    local = tokens[...].astype(jnp.int32) - offset
    inside = (local >= 0) & (local < rows)
    hit = jnp.broadcast_to(jnp.where(inside, 1.0, 0.0), (8, count))
    before = lax.broadcasted_iota(jnp.int32, (count, count), 0)
    after = lax.broadcasted_iota(jnp.int32, (count, count), 1)
    upto = jnp.where(before <= after, 1.0, 0.0).astype(jnp.bfloat16)
    running = dot_nn(hit.astype(jnp.bfloat16), upto)[0:1].astype(jnp.int32)
    rank = jnp.where(inside, running - 1, -1)
    total = jnp.max(running)
    chunks[0] = (total + BLOCK - 1) // BLOCK
    safe = jnp.where(inside, local, 0)
    high = jnp.broadcast_to((safe >> 6).astype(jnp.float32), (8, count)).astype(jnp.bfloat16)
    low = jnp.broadcast_to((safe & 63).astype(jnp.float32), (8, count)).astype(jnp.bfloat16)
    for chunk in range(blocks):

        @pl.when(chunk * BLOCK < jnp.maximum(total, 1))
        def _():
            slot = lax.broadcasted_iota(jnp.int32, (BLOCK, count), 0) + chunk * BLOCK
            chosen = jnp.where(slot == rank, 1.0, 0.0).astype(jnp.bfloat16)
            columns = cot.shape[0] // blocks
            taken = jnp.zeros((columns, BLOCK), jnp.float32)
            for block in range(blocks):
                span = slice(block * BLOCK, (block + 1) * BLOCK)
                part = cot[block * columns : (block + 1) * columns].astype(jnp.bfloat16)
                taken = taken + dot_nt(part, chosen[:, span])
            packed_cot[chunk] = taken.astype(jnp.bfloat16)
            row = dot_nt(high, chosen)[0:1] * 64.0 + dot_nt(low, chosen)[0:1]
            used = dot_nt(hit.astype(jnp.bfloat16), chosen)[0:1] > 0.5
            packed_ids[chunk] = jnp.where(used, row.astype(jnp.int32), -1)


def next_slot(relative, prob, last):
    following = jnp.min(jnp.where(relative > last, relative, FAR), axis=0, keepdims=True)
    chance = jnp.sum(jnp.where(relative == following, prob, 0.0), axis=0, keepdims=True)
    return following, chance


def join_halves(near, far, joined):
    _, z, y, core = here()
    pair = near.shape[0] // (SIDE * SIDE)
    for side, source in ((core, near), (1 - core, far)):
        lanes = pl.ds(pl.multiple_of(side * HALF, HALF), HALF)
        for outer in range(SIDE):
            for inner in range(SIDE):
                start = (outer * SIDE + inner) * pair
                into = pl.multiple_of(chip_of(outer, inner, side, z, y) * pair, 16)
                joined[pl.ds(into, pair), lanes] = source[start : start + pair]


def table_copy(step, table, held, ready):
    rows = pl.ds(pl.multiple_of(step * ROW_STEP, STRIP), ROW_STEP)
    return pltpu.make_async_copy(table.at[rows], held.at[rows], ready.at[step])


def logit_kernel(blocks, fresh, embed, *refs):
    near, far = refs[:blocks], refs[blocks : 2 * blocks]
    squashed, total, columns = refs[2 * blocks : 2 * blocks + 3]
    rest = refs[2 * blocks + 3 :]
    step = pl.program_id(0)
    steps = pl.num_programs(0)
    length = ROW_STEP if fresh else LONG_STEP
    if fresh:
        held, hidden, sums, ready = rest

        @pl.when(step == 0)
        def _():
            for index in range(embed.shape[0] // ROW_STEP):
                table_copy(index, embed, held, ready).start()
            rows = embed.shape[0]
            held[rows:] = jnp.zeros((PADDED - rows, held.shape[1]), held.dtype)

    else:
        held, (hidden, sums) = embed, rest

    @pl.when(step == 0)
    def _():
        sums[...] = jnp.zeros_like(sums)
        used = ROW_STEP * (PADDED // ROW_STEP)
        squashed[used:] = jnp.zeros((PADDED - used, squashed.shape[1]), jnp.float32)
        size = columns.shape[1]
        start = pl.multiple_of(lax.axis_index("dp") * size, 16)
        for block in range(blocks):
            join_halves(near[block], far[block], hidden.at[block])
            columns[block] = hidden[block, pl.ds(start, size)]

    if fresh:
        table_copy(step, embed, held, ready).wait()

    for first in range(0, length, ROW_TILE):
        from_table = pl.ds(pl.multiple_of(step * length + first, STRIP), ROW_TILE)
        for block in range(blocks):
            span = slice(block * BLOCK, (block + 1) * BLOCK)
            raw = dot_nn(held[from_table], hidden[block])
            raised = jnp.zeros((8, BLOCK), jnp.float32)
            for chunk in range(0, ROW_TILE, STRIP):
                ratio = jnp.tanh(raw[chunk : chunk + STRIP] * (1.0 / SOFT_CAP))
                into = pl.multiple_of(step * length + first + chunk, STRIP)
                squashed[pl.ds(into, STRIP), span] = ratio
                power = jnp.exp2(ratio * (SOFT_CAP * LOG2_E))
                raised = raised + (power[:8] + power[8:])
            sums[:, span] += raised

    @pl.when(step == steps - 1)
    def _():
        total[...] = jnp.sum(sums[...], axis=0, keepdims=True)


def gradient(ratio, target, log_share):
    share = jnp.exp2(ratio * (SOFT_CAP * LOG2_E) + log_share)
    return (share - target) * (1.0 - ratio * ratio)


def logit_grads(squashed, grads, log_share, relative, chances, fast, term=None):
    last = jnp.full((1, BLOCK), -1, jnp.int32)
    slots = []
    for _ in range(fast):
        last, chance = next_slot(relative, chances, last)
        slots.append((last, chance * LOSS_SCALE))
    row = lax.broadcasted_iota(jnp.int32, (STRIP, BLOCK), 0)
    added = jnp.zeros((8, BLOCK), jnp.float32)
    for start in range(0, grads.shape[0], STRIP):
        strip = slice(start, start + STRIP)
        ratio = squashed[strip]
        target = jnp.zeros((STRIP, BLOCK), jnp.float32)
        for where, value in slots:
            target = jnp.where(row + start == where, value, target)
        grads[strip] = gradient(ratio, target, log_share).astype(jnp.bfloat16)
        if term is not None:
            product = target * ratio
            added = added + (product[:8] + product[8:])
    if term is not None:
        term[...] += added
    return last


def more_targets(
    squashed, grads, log_share, relative, chances, last, fast, count, term=None
):
    row = lax.broadcasted_iota(jnp.int32, (STRIP, BLOCK), 0)

    def slot(_, last):
        last, chance = next_slot(relative, chances, last)
        value = chance * LOSS_SCALE

        def strip(index, _):
            start = pl.multiple_of(index * STRIP, STRIP)
            rows = pl.ds(start, STRIP)
            ratio = squashed[rows]
            hit = row + start == last
            fresh = gradient(ratio, jnp.broadcast_to(value, ratio.shape), log_share)
            held = grads[rows].astype(jnp.float32)
            grads[rows] = jnp.where(hit, fresh, held).astype(jnp.bfloat16)
            if term is not None:
                product = jnp.where(hit, value * ratio, 0.0)
                term[...] += product[:8] + product[8:]
            return 0

        lax.fori_loop(0, grads.shape[0] // STRIP, strip, 0)
        return last

    lax.fori_loop(fast, count, slot, last)


def hidden_grad_kernel(
    counts,
    embed,
    squashed,
    total,
    ids,
    prob,
    grads,
    keep,
    give,
    rows_grad,
    flipped,
    term,
    ready,
    made,
):
    width = embed.shape[1]
    log_share = jnp.log2(LOSS_SCALE / total[:, 0:BLOCK])
    term[...] = jnp.zeros_like(term)
    ready[...] = jnp.zeros_like(ready)
    rows_grad[...] = jnp.zeros_like(rows_grad)
    tiles = PADDED // GRAD_TILE

    def rows_of(tile):
        return pl.ds(pl.multiple_of(tile * GRAD_TILE, GRAD_TILE), GRAD_TILE)

    def step(tile, _):
        rows = rows_of(tile)
        rows_grad[...] += dot_tn(ready[...], embed[rows_of(jnp.maximum(tile - 1, 0))])
        held = squashed.at[rows]
        relative = ids[0] - tile * GRAD_TILE
        last = logit_grads(held, made, log_share, relative, prob[0], HIDDEN_SLOTS, term)

        @pl.when(counts[tile] > HIDDEN_SLOTS)
        def _():
            more_targets(
                held,
                made,
                log_share,
                ids[0] - tile * GRAD_TILE,
                prob[0],
                last,
                HIDDEN_SLOTS,
                counts[tile],
                term,
            )

        ready[...] = made[...]
        grads[rows] = made[...]
        return 0

    lax.fori_loop(0, tiles, step, 0)
    rows_grad[...] += dot_tn(ready[...], embed[rows_of(tiles - 1)])

    _, z, y, core = here()
    thin = keep.shape[2] - 8
    for part in range(width // BLOCK):
        span = slice(part * BLOCK, (part + 1) * BLOCK)
        flipped[span, :] = rows_grad[:, span].T
    summed = jnp.sum(term[...], axis=0, keepdims=True) * (SOFT_CAP / LOSS_SCALE)
    for outer in range(SIDE):
        for inner in range(SIDE):
            for ref, side in ((keep, core), (give, 1 - core)):
                rank = 2 * chip_of(outer, inner, side, z, y) + side
                start = pl.multiple_of(rank * thin, 8)
                ref[outer, inner, 0:thin] = flipped[pl.ds(start, thin)]
                ref[outer, inner, thin : thin + 8] = jnp.broadcast_to(summed, (8, BLOCK))


def halve_kernel(keep, got, *outs):
    for index, out in enumerate(outs):
        out[...] = keep[index] + got[index]


def quarter_kernel(*refs):
    parts, outs = refs[:SIDE], refs[SIDE:]
    for index, out in enumerate(outs):
        out[...] = (parts[0][index] + parts[1][index]) + (parts[2][index] + parts[3][index])


def finish_kernel(total, teacher_logits, *refs):
    parts, (hidden_grad, divergence) = refs[:SIDE], refs[SIDE:]
    _, z, y, core = here()
    summed = (parts[0][...] + parts[1][...]) + (parts[2][...] + parts[3][...])
    thin = hidden_grad.shape[0]
    hidden_grad[...] = summed[:thin].astype(jnp.bfloat16)
    scores = teacher_logits[...]
    share = scores.shape[0]
    shifted = scores - jnp.max(scores, axis=1, keepdims=True)
    raised = jnp.exp(shifted)
    prob = raised / jnp.sum(raised, axis=1, keepdims=True)
    entropy = jnp.sum(prob * jnp.log(prob), axis=1, keepdims=True)
    rest = jnp.log(total[:, 0:BLOCK]) - summed[thin : thin + 1]
    first = ((z * SIDE + y) * 2 + core) * share
    lane = lax.broadcasted_iota(jnp.int32, (share, BLOCK), 1)
    token = lax.broadcasted_iota(jnp.int32, (share, BLOCK), 0) + first
    value = entropy + jnp.sum(jnp.where(lane == token, rest, 0.0), axis=1, keepdims=True)
    line = lax.broadcasted_iota(jnp.int32, (share, HALF), 0)
    column = lax.broadcasted_iota(jnp.int32, (share, HALF), 1)
    divergence[...] = jnp.sum(jnp.where(line == column, value, 0.0), axis=0, keepdims=True)


def table_grad_kernel(
    width,
    fresh,
    counts,
    chunks,
    own_grads,
    side_squashed,
    far_squashed,
    total,
    ids,
    prob,
    packed_cot,
    packed_ids,
    own_columns,
    side_columns,
    far_columns,
    *refs,
):
    blocks = SIDE - 1
    tiles = PADDED // TABLE_TILE // 2
    first = 0 if fresh else tiles
    out, left, ready, made = refs[-4:]
    now = pl.program_id(0) == pl.num_programs(0) - 1

    if not fresh:

        @pl.when(jnp.logical_not(now))
        def _():
            out[...] = refs[0][...]

    def rows_of(tile):
        return pl.ds(pl.multiple_of(tile * TABLE_TILE, TABLE_TILE), TABLE_TILE)

    def onehot(tile, chunk):
        column = lax.broadcasted_iota(jnp.int32, (TABLE_TILE, BLOCK), 0) + tile * TABLE_TILE
        chosen = jnp.where(column == packed_ids[chunk], math.sqrt(width), 0.0)
        return chosen.astype(jnp.bfloat16)

    def product():
        return dot_nt(left[...], ready[...])

    def put(index, value):
        out[:, rows_of(index)] = value.astype(jnp.bfloat16)

    def more_lookups(index):
        spread = lax.fori_loop(
            1,
            chunks[0],
            lambda chunk, held: held + dot_nt(packed_cot[chunk], onehot(first + index, chunk)),
            product(),
        )
        put(index, spread)

    def step(index, _):
        tile = first + index
        rows = rows_of(tile)
        before = jnp.maximum(index - 1, 0)
        put(before, product())
        made[:, 0:BLOCK] = own_grads[rows]
        made[:, 4 * BLOCK :] = onehot(tile, 0)

        def of(block):
            lanes = pl.ds(block * BLOCK, BLOCK)
            held = far_squashed.at[rows] if block == 2 else side_squashed.at[rows, lanes]
            into = pl.ds((block + 1) * BLOCK, BLOCK)
            log_share = jnp.log2(LOSS_SCALE / total[:, into])
            relative = ids[block + 1] - tile * TABLE_TILE
            return held, made.at[:, into], log_share, relative, prob[block + 1]

        lasts = [logit_grads(*of(block), FAST_SLOTS) for block in range(blocks)]
        for block in range(blocks):
            count = counts[tile * blocks + block]

            @pl.when(count > FAST_SLOTS)
            def _(block=block, count=count):
                more_targets(*of(block), lasts[block], FAST_SLOTS, count)

        @pl.when((chunks[0] > 1) & (index > 0))
        def _():
            more_lookups(before)

        ready[...] = made[...]
        return 0

    @pl.when(now)
    def _():
        left[:, 0:BLOCK] = own_columns[0]
        left[:, BLOCK : 2 * BLOCK] = side_columns[0]
        left[:, 2 * BLOCK : 3 * BLOCK] = side_columns[1]
        left[:, 3 * BLOCK : 4 * BLOCK] = far_columns[0]
        left[:, 4 * BLOCK :] = packed_cot[0]
        ready[...] = jnp.zeros_like(ready)
        lax.fori_loop(0, tiles, step, 0)
        put(tiles - 1, product())

        @pl.when(chunks[0] > 1)
        def _():
            more_lookups(tiles - 1)


def smem():
    return pl.BlockSpec(memory_space=pltpu.SMEM)


def vmem():
    return pl.BlockSpec(memory_space=pltpu.VMEM)


def whole(shape):
    return pl.BlockSpec(shape, lambda *_: (0,) * len(shape))


def shape_of(shape, dtype):
    return jax.ShapeDtypeStruct(shape, dtype)


def small_call(kernel, name, outs, *args, scratch=(), limit=4 << 20):
    return pl.pallas_call(
        kernel,
        out_shape=tuple(shape_of(shape, dtype) for shape, dtype, _ in outs),
        in_specs=[vmem()] * len(args),
        out_specs=tuple(space() for _, _, space in outs),
        scratch_shapes=scratch,
        compiler_params=pltpu.CompilerParams(vmem_limit_bytes=limit),
        name=name,
    )(*args)


def logits_call(embed, near, far, columns, fresh):
    blocks = len(near)
    rows, width = embed.shape
    tokens = blocks * BLOCK
    length = ROW_STEP if fresh else LONG_STEP
    steps = ROW_STEP * (PADDED // ROW_STEP) // length
    table = whole((PADDED, width))
    out_specs = [
        whole((PADDED, tokens)),
        whole((1, tokens)),
        whole((blocks, columns, BLOCK)),
    ]
    out_shape = [
        pltpu.VMEM((PADDED, tokens), jnp.float32),
        shape_of((1, tokens), jnp.float32),
        shape_of((blocks, columns, BLOCK), jnp.bfloat16),
    ]
    scratch = [
        pltpu.VMEM((blocks, width, BLOCK), jnp.bfloat16),
        pltpu.VMEM((8, tokens), jnp.float32),
    ]
    if fresh:
        out_specs.append(table)
        out_shape.append(pltpu.VMEM((PADDED, width), embed.dtype))
        scratch.append(pltpu.SemaphoreType.DMA((steps,)))
    return pl.pallas_call(
        functools.partial(logit_kernel, blocks, fresh),
        grid=(steps,),
        in_specs=[pl.BlockSpec(memory_space=pltpu.HBM) if fresh else table]
        + [whole((width, HALF))] * (2 * blocks),
        out_specs=out_specs,
        out_shape=out_shape,
        scratch_shapes=scratch,
        compiler_params=pltpu.CompilerParams(vmem_limit_bytes=(3 + 2 * blocks) << 20),
        cost_estimate=pl.CostEstimate(
            flops=2 * rows * width * tokens,
            bytes_accessed=rows * tokens * 4 + (2 * rows * width if fresh else 0),
            transcendentals=2 * rows * tokens,
        ),
        name=f"logits_{blocks}",
    )(pltpu.with_memory_space_constraint(embed, pltpu.HBM) if fresh else embed, *near, *far)


def index_of(x, z, y, core):
    return ((x * SIDE + z) * SIDE + y) * 2 + core


def route_by(target):
    pairs = []
    for x in range(SIDE):
        for z in range(SIDE):
            for y in range(SIDE):
                for core in range(2):
                    pairs.append((index_of(x, z, y, core), index_of(*target(x, z, y, core))))
    return pairs


def along(axis, core, by, place):
    x, z, y = place
    if axis == 2:
        x = (x + (by if core == 0 else -by)) % SIDE
    elif axis == core:
        y = (y + by) % SIDE
    else:
        z = (z + by) % SIDE
    return x, z, y, core


def fetch(value, axis, by):
    return lax.ppermute(value, EVERY, route_by(lambda x, z, y, c: along(axis, c, -by, (x, z, y))))


def hand_on(value, axis, by):
    return lax.ppermute(value, EVERY, route_by(lambda x, z, y, c: along(axis, c, by, (x, z, y))))


def exchange(value, axis, bit):
    def other(x, z, y, core):
        return along(axis, core, ((y if axis == core else z) ^ bit) - (y if axis == core else z), (x, z, y))

    return lax.ppermute(value, EVERY, route_by(other))


def swap(value):
    return lax.ppermute(value, EVERY, route_by(lambda x, z, y, c: (x, z, y, 1 - c)))


def fetch_parts(value, axis):
    return [value] + [fetch(value, axis, by) for by in OFFSETS[1:]]


def fetch_all(value, axis):
    return jnp.concatenate(fetch_parts(value, axis), axis=0)


def halves(core_zero, low, high):
    return jnp.where(core_zero, low, high), jnp.where(core_zero, high, low)


def in_core_order(core_zero, kept, got):
    return jnp.where(
        core_zero, jnp.concatenate([kept, got], 0), jnp.concatenate([got, kept], 0)
    )


def side_values(core_zero, after, token_ids, lookup_cot, teacher_ids, teacher_logits):
    here_tokens, thin = lookup_cot.shape
    share = teacher_ids.shape[0]
    pack = jnp.concatenate(
        [
            jnp.concatenate([teacher_logits, teacher_ids.astype(jnp.float32)], axis=1),
            token_ids.astype(jnp.float32).reshape(here_tokens // HALF, HALF),
            jnp.zeros((8 - here_tokens // HALF, HALF), jnp.float32),
        ],
        axis=0,
    )
    pack, turned, _ = lax.optimization_barrier((pack, lookup_cot.T, after))
    moved = lax.ppermute(
        turned,
        EVERY,
        route_by(lambda x, z, y, c: (z, x, y, c)),
    ).astype(jnp.float32)
    packs = [pack] + [
        lax.ppermute(pack, "dp", [((k + by) % SIDE, k) for k in range(SIDE)])
        for by in OFFSETS[1:]
    ]
    far_away = [packs[0], packs[1], packs[3], packs[2]]
    sides = [
        jnp.concatenate(
            [
                moved[:, half * HALF : (half + 1) * HALF],
                far_away[2 * half][:share],
                far_away[2 * half + 1][:share],
            ],
            axis=0,
        )
        for half in range(2)
    ]
    return *halves(core_zero, *sides), jnp.stack(packs)


def per_device(hidden, embed, token_ids, lookup_cot, teacher_ids, teacher_logits):
    rows, width = embed.shape
    here_tokens, thin = hidden.shape
    dp = SIDE
    vocab = 2 * SIDE * SIDE
    tokens = here_tokens * dp
    top = teacher_ids.shape[1]
    share = here_tokens // vocab
    columns = width // dp
    core_zero = lax.axis_index("core") == 0

    flat = hidden.T
    kept, given = halves(core_zero, flat[:, :HALF], flat[:, HALF:])
    pair = in_core_order(core_zero, kept, swap(given))
    row = fetch_all(pair, 0)
    own_near = fetch_all(row, 1)
    side = side_values(core_zero, row, token_ids, lookup_cot, teacher_ids, teacher_logits)
    own_near, kept, given, packs = lax.optimization_barrier((own_near, *side))
    first_near = fetch(own_near, 2, 1)
    second_near = fetch(own_near, 2, -1)
    own_far = swap(own_near)
    own_squashed, own_total, own_columns, table = logits_call(
        embed, [own_near], [own_far], columns, True
    )
    given = lax.optimization_barrier((given, own_total))[0]
    side = in_core_order(core_zero, kept, swap(given))
    first_near, second_near, side = lax.optimization_barrier((first_near, second_near, side))
    opposite_near = fetch(first_near, 2, 1)
    first_far = swap(second_near)
    second_far = swap(first_near)
    side_parts = fetch_parts(side, 0)
    side_squashed, side_total, side_columns = logits_call(
        table, [first_near, second_near], [first_far, second_far], columns, False
    )
    side_parts, opposite_near, side_total = lax.optimization_barrier(
        (side_parts, opposite_near, side_total)
    )
    opposite_far = swap(opposite_near)
    side_parts = fetch_parts(jnp.concatenate(side_parts, axis=0), 1)
    far_squashed, far_total, far_columns = logits_call(
        table, [opposite_near], [opposite_far], columns, False
    )
    side_parts, far_total = lax.optimization_barrier((side_parts, far_total))
    side_near = jnp.concatenate(side_parts, axis=0)
    side_far = swap(side_near)

    total = jnp.concatenate([own_total, side_total, far_total], axis=1)
    got = swap(total)
    total = total + jnp.concatenate(
        [
            got[:, :BLOCK],
            got[:, 2 * BLOCK : 3 * BLOCK],
            got[:, BLOCK : 2 * BLOCK],
            got[:, 3 * BLOCK :],
        ],
        axis=1,
    )
    for axis in (0, 1):
        for bit in (1, 2):
            total = total + exchange(total, axis, bit)

    cot, ids, prob, row_counts, column_counts = small_call(
        functools.partial(teacher_kernel, rows, thin),
        "teacher_prep",
        [
            ((width, BLOCK), jnp.float32, vmem),
            ((dp, top, BLOCK), jnp.int32, vmem),
            ((dp, top, BLOCK), jnp.float32, vmem),
            ((PADDED // GRAD_TILE,), jnp.int32, smem),
            ((PADDED // TABLE_TILE * (dp - 1),), jnp.int32, smem),
        ],
        side_near,
        side_far,
        scratch=[pltpu.VMEM((dp, BLOCK, 2 * top), jnp.float32)],
    )
    packed_cot, packed_ids, chunks = small_call(
        functools.partial(lookup_kernel, rows, share),
        "lookup_prep",
        [
            ((dp, columns, BLOCK), jnp.bfloat16, vmem),
            ((dp, 1, BLOCK), jnp.int32, vmem),
            ((1,), jnp.int32, smem),
        ],
        packs,
        cot,
        scratch=[pltpu.VMEM((1, tokens), jnp.float32)],
    )

    scattered = (SIDE, SIDE, thin + 8, BLOCK)
    own_grads, keep, give = pl.pallas_call(
        hidden_grad_kernel,
        in_specs=[smem()] + [vmem()] * 5,
        out_specs=[vmem()] * 3,
        out_shape=(
            pltpu.VMEM((PADDED, BLOCK), jnp.bfloat16),
            shape_of(scattered, jnp.float32),
            shape_of(scattered, jnp.float32),
        ),
        scratch_shapes=[
            pltpu.VMEM((BLOCK, width), jnp.float32),
            pltpu.VMEM((width, BLOCK), jnp.float32),
            pltpu.VMEM((8, BLOCK), jnp.float32),
            pltpu.VMEM((GRAD_TILE, BLOCK), jnp.bfloat16),
            pltpu.VMEM((GRAD_TILE, BLOCK), jnp.bfloat16),
        ],
        compiler_params=pltpu.CompilerParams(vmem_limit_bytes=10 << 20),
        cost_estimate=pl.CostEstimate(
            flops=2 * rows * width * BLOCK,
            bytes_accessed=rows * BLOCK * 6,
            transcendentals=rows * BLOCK,
        ),
        name="hidden_grads",
    )(row_counts, table, own_squashed, total, ids, prob)

    def table_grads(so_far):
        fresh = so_far is None
        started = [] if fresh else [so_far]
        operands = [
            column_counts,
            chunks,
            own_grads,
            side_squashed,
            far_squashed,
            total,
            ids,
            prob,
            packed_cot,
            packed_ids,
            own_columns,
            side_columns,
            far_columns,
        ]
        made = PADDED // 2
        half = (columns, PADDED // 2)
        return pl.pallas_call(
            functools.partial(table_grad_kernel, width, fresh),
            grid=(1 if fresh else 2,),
            in_specs=[smem()] * 2
            + [whole(operand.shape) for operand in operands[2:]]
            + [whole(half) for _ in started],
            out_specs=pl.BlockSpec(half, lambda n: (0, n)),
            out_shape=pltpu.VMEM(half, jnp.bfloat16)
            if fresh
            else shape_of((columns, rows), jnp.bfloat16),
            scratch_shapes=[
                pltpu.VMEM((columns, (dp + 1) * BLOCK), jnp.bfloat16),
                pltpu.VMEM((TABLE_TILE, (dp + 1) * BLOCK), jnp.bfloat16),
                pltpu.VMEM((TABLE_TILE, (dp + 1) * BLOCK), jnp.bfloat16),
            ],
            compiler_params=pltpu.CompilerParams(vmem_limit_bytes=12 << 20),
            cost_estimate=pl.CostEstimate(
                flops=2 * made * columns * (tokens + BLOCK),
                bytes_accessed=rows * columns * 2,
                transcendentals=made * tokens,
            ),
            name="table_grads_start" if fresh else "table_grads_rest",
        )(*operands, *started)

    quarter = (SIDE, thin + 8, BLOCK)
    got, packed_cot, packed_ids = lax.optimization_barrier((swap(give), packed_cot, packed_ids))
    parts = small_call(halve_kernel, "halve", [(quarter, jnp.float32, vmem)] * SIDE, keep, got)
    travelling = [hand_on(part, 1, by) for part, by in zip(parts[1:], OFFSETS[1:])]
    embed_grad = table_grads(None)
    travelling, embed_grad = lax.optimization_barrier((travelling, embed_grad))
    parts = small_call(
        quarter_kernel,
        "quarter",
        [(quarter[1:], jnp.float32, vmem)] * SIDE,
        parts[0],
        *travelling,
    )
    travelling = [hand_on(part, 0, by) for part, by in zip(parts[1:], OFFSETS[1:])]
    embed_grad = table_grads(embed_grad)
    parts = [parts[0]] + travelling

    hidden_grad, divergence = small_call(
        finish_kernel,
        "finish",
        [((thin, BLOCK), jnp.bfloat16, vmem), ((1, HALF), jnp.float32, vmem)],
        total,
        teacher_logits,
        *parts,
    )
    return (hidden_grad.T, embed_grad.T, divergence[0, :share])


def solution(mesh):
    dp, vocab = (mesh.shape[name] for name in ("dp", "vocab"))
    fine = Mesh(mesh.devices.reshape(dp, SIDE, SIDE, vocab // (SIDE * SIDE)), EVERY)
    return jax.shard_map(
        per_device,
        mesh=fine,
        in_specs=(
            P("dp", RING),
            P(RING, None),
            P("dp"),
            P("dp", RING),
            P(EVERY, None),
            P(EVERY, None),
        ),
        out_specs=(P("dp", RING), P(RING, "dp"), P(EVERY)),
        check_vma=False,
    )
```

```python
import functools
import math

import jax
import jax.numpy as jnp
from jax import lax
from jax.experimental import pallas as pl
from jax.experimental.pallas import tpu as pltpu
from jax.sharding import Mesh, PartitionSpec as P

SOFT_CAP = 30.0
LOSS_SCALE = 16.0
BLOCK = 256
HALF = 128
ROW_TILE = 400
ROW_STEP = 800
LONG_STEP = 2000
PADDED = 4096
STRIP = 16
WIDE_STRIP = 32
GRAD_TILE = 512
TABLE_TILE = 256
FAST_SLOTS = 4
HIDDEN_SLOTS = 5
FAR = 1 << 30
LOG2_E = math.log2(math.e)
RING = ("z", "y", "core")
EVERY = ("dp",) + RING
SIDE = 4
OFFSETS = (0, 1, 3, 2)


def dot_nn(a, b):
    return lax.dot_general(a, b, (((1,), (0,)), ((), ())), preferred_element_type=jnp.float32)


def dot_nt(a, b):
    return lax.dot_general(a, b, (((1,), (1,)), ((), ())), preferred_element_type=jnp.float32)


def dot_tn(a, b):
    return lax.dot_general(a, b, (((0,), (0,)), ((), ())), preferred_element_type=jnp.float32)


def offset_of(index, core):
    return jnp.where(core == 0, OFFSETS[index], OFFSETS[(0, 2, 1, 3)[index]])


def chip_of(outer, inner, core, z, y):
    first, second = OFFSETS[inner], OFFSETS[outer]
    row = lax.rem(z + jnp.where(core == 0, second, first), SIDE)
    column = lax.rem(y + jnp.where(core == 0, first, second), SIDE)
    return row * SIDE + column


def here():
    return tuple(lax.axis_index(name) for name in EVERY)


def block_offset(rows, z, y, core):
    return ((z * SIDE + y) * 2 + core) * rows


def teacher_kernel(rows, thin, near, far, cot, ids, prob, row_counts, column_counts, joined):
    _, z, y, core = here()
    offset = block_offset(rows, z, y, core)
    top = ids.shape[0]
    share = 8
    group = thin + 2 * share
    for side, source in ((core, near), (1 - core, far)):
        lanes = pl.ds(pl.multiple_of(side * HALF, HALF), HALF)
        for outer in range(SIDE):
            for inner in range(SIDE):
                chip = chip_of(outer, inner, side, z, y)
                for other in range(2):
                    start = ((outer * SIDE + inner) * 2 + other) * group
                    rank = chip * 2 + other
                    into = pl.multiple_of(rank * thin, 8)
                    cot[pl.ds(into, thin), lanes] = source[start : start + thin]
                    for half in range(2):
                        held = source[start + thin + half * share : start + thin + (half + 1) * share]
                        joined[side * 2 + half, pl.ds(pl.multiple_of(rank * share, 8), share)] = held
    for block in range(SIDE):
        flipped = joined[offset_of(block, core)].T
        scores = flipped[:top]
        local = flipped[top:].astype(jnp.int32) - offset
        raised = jnp.exp(scores - jnp.max(scores, axis=0, keepdims=True))
        lanes = slice(block * BLOCK, (block + 1) * BLOCK)
        ids[:, lanes] = local
        prob[:, lanes] = raised / jnp.sum(raised, axis=0, keepdims=True)
        size = GRAD_TILE if block == 0 else TABLE_TILE
        for tile in range(PADDED // size):
            first = tile * size
            inside = (local >= first) & (local < min(first + size, rows))
            most = jnp.max(jnp.sum(inside.astype(jnp.int32), axis=0))
            if block == 0:
                row_counts[tile] = most
            else:
                column_counts[tile * (SIDE - 1) + block - 1] = most


def lookup_kernel(rows, share, packs, cot, packed_cot, packed_ids, chunks, tokens):
    mine, z, y, core = here()
    offset = block_offset(rows, z, y, core)
    count = tokens.shape[1]
    blocks = count // BLOCK
    for index in range(blocks):
        start = lax.rem(mine + OFFSETS[index], blocks) * BLOCK
        for half in range(BLOCK // HALF):
            lanes = pl.ds(pl.multiple_of(start + half * HALF, HALF), HALF)
            tokens[:, lanes] = packs[index, share + half : share + half + 1]
    local = tokens[...].astype(jnp.int32) - offset
    inside = (local >= 0) & (local < rows)
    hit = jnp.broadcast_to(jnp.where(inside, 1.0, 0.0), (8, count))
    before = lax.broadcasted_iota(jnp.int32, (count, count), 0)
    after = lax.broadcasted_iota(jnp.int32, (count, count), 1)
    upto = jnp.where(before <= after, 1.0, 0.0).astype(jnp.bfloat16)
    running = dot_nn(hit.astype(jnp.bfloat16), upto)[0:1].astype(jnp.int32)
    rank = jnp.where(inside, running - 1, -1)
    total = jnp.max(running)
    chunks[0] = (total + BLOCK - 1) // BLOCK
    safe = jnp.where(inside, local, 0)
    high = jnp.broadcast_to((safe >> 6).astype(jnp.float32), (8, count)).astype(jnp.bfloat16)
    low = jnp.broadcast_to((safe & 63).astype(jnp.float32), (8, count)).astype(jnp.bfloat16)
    for chunk in range(blocks):

        @pl.when(chunk * BLOCK < jnp.maximum(total, 1))
        def _():
            slot = lax.broadcasted_iota(jnp.int32, (BLOCK, count), 0) + chunk * BLOCK
            chosen = jnp.where(slot == rank, 1.0, 0.0).astype(jnp.bfloat16)
            columns = cot.shape[0] // blocks
            taken = jnp.zeros((columns, BLOCK), jnp.float32)
            for block in range(blocks):
                span = slice(block * BLOCK, (block + 1) * BLOCK)
                part = cot[block * columns : (block + 1) * columns].astype(jnp.bfloat16)
                taken = taken + dot_nt(part, chosen[:, span])
            packed_cot[chunk] = taken.astype(jnp.bfloat16)
            row = dot_nt(high, chosen)[0:1] * 64.0 + dot_nt(low, chosen)[0:1]
            used = dot_nt(hit.astype(jnp.bfloat16), chosen)[0:1] > 0.5
            packed_ids[chunk] = jnp.where(used, row.astype(jnp.int32), -1)


def next_slot(relative, prob, last):
    following = jnp.min(jnp.where(relative > last, relative, FAR), axis=0, keepdims=True)
    chance = jnp.sum(jnp.where(relative == following, prob, 0.0), axis=0, keepdims=True)
    return following, chance


def join_halves(near, far, joined):
    _, z, y, core = here()
    pair = near.shape[0] // (SIDE * SIDE)
    for side, source in ((core, near), (1 - core, far)):
        lanes = pl.ds(pl.multiple_of(side * HALF, HALF), HALF)
        for outer in range(SIDE):
            for inner in range(SIDE):
                start = (outer * SIDE + inner) * pair
                into = pl.multiple_of(chip_of(outer, inner, side, z, y) * pair, 16)
                joined[pl.ds(into, pair), lanes] = source[start : start + pair]


def table_copy(step, table, held, ready):
    rows = pl.ds(pl.multiple_of(step * ROW_STEP, STRIP), ROW_STEP)
    return pltpu.make_async_copy(table.at[rows], held.at[rows], ready.at[step])


def logit_kernel(blocks, fresh, embed, *refs):
    near, far = refs[:blocks], refs[blocks : 2 * blocks]
    squashed, total, columns = refs[2 * blocks : 2 * blocks + 3]
    rest = refs[2 * blocks + 3 :]
    step = pl.program_id(0)
    steps = pl.num_programs(0)
    length = ROW_STEP if fresh else LONG_STEP
    if fresh:
        held, hidden, sums, ready = rest

        @pl.when(step == 0)
        def _():
            for index in range(embed.shape[0] // ROW_STEP):
                table_copy(index, embed, held, ready).start()
            rows = embed.shape[0]
            held[rows:] = jnp.zeros((PADDED - rows, held.shape[1]), held.dtype)

    else:
        held, (hidden, sums) = embed, rest

    @pl.when(step == 0)
    def _():
        sums[...] = jnp.zeros_like(sums)
        used = ROW_STEP * (PADDED // ROW_STEP)
        squashed[used:] = jnp.zeros((PADDED - used, squashed.shape[1]), jnp.float32)
        size = columns.shape[1]
        start = pl.multiple_of(lax.axis_index("dp") * size, 16)
        for block in range(blocks):
            join_halves(near[block], far[block], hidden.at[block])
            columns[block] = hidden[block, pl.ds(start, size)]

    if fresh:
        table_copy(step, embed, held, ready).wait()

    for first in range(0, length, ROW_TILE):
        from_table = pl.ds(pl.multiple_of(step * length + first, STRIP), ROW_TILE)
        for block in range(blocks):
            span = slice(block * BLOCK, (block + 1) * BLOCK)
            raw = dot_nn(held[from_table], hidden[block])
            raised = jnp.zeros((8, BLOCK), jnp.float32)
            for chunk in range(0, ROW_TILE, STRIP):
                ratio = jnp.tanh(raw[chunk : chunk + STRIP] * (1.0 / SOFT_CAP))
                into = pl.multiple_of(step * length + first + chunk, STRIP)
                squashed[pl.ds(into, STRIP), span] = ratio
                power = jnp.exp2(ratio * (SOFT_CAP * LOG2_E))
                raised = raised + (power[:8] + power[8:])
            sums[:, span] += raised

    @pl.when(step == steps - 1)
    def _():
        total[...] = jnp.sum(sums[...], axis=0, keepdims=True)


def gradient(ratio, target, log_share):
    share = jnp.exp2(ratio * (SOFT_CAP * LOG2_E) + log_share)
    return (share - target) * (1.0 - ratio * ratio)


def first_slots(relative, chances, fast):
    last = jnp.full((1, relative.shape[1]), -1, jnp.int32)
    slots = []
    for _ in range(fast):
        last, chance = next_slot(relative, chances, last)
        slots.append((last, chance * LOSS_SCALE))
    return slots


def logit_grads(squashed, grads, log_share, slots, lanes, term=None):
    row = lax.broadcasted_iota(jnp.int32, (WIDE_STRIP, BLOCK), 0)
    added = jnp.zeros((8, BLOCK), jnp.float32)
    for start in range(0, grads.shape[0], WIDE_STRIP):
        strip = slice(start, start + WIDE_STRIP)
        ratio = squashed[strip]
        target = jnp.zeros((WIDE_STRIP, BLOCK), jnp.float32)
        for where, value in slots:
            target = jnp.where(row + start == where[:, lanes], value[:, lanes], target)
        grads[strip] = gradient(ratio, target, log_share).astype(jnp.bfloat16)
        if term is not None:
            product = target * ratio
            added = added + jnp.sum(product.reshape(WIDE_STRIP // 8, 8, BLOCK), axis=0)
    if term is not None:
        term[...] += added


def more_targets(
    squashed, grads, log_share, relative, chances, last, fast, count, term=None
):
    row = lax.broadcasted_iota(jnp.int32, (STRIP, BLOCK), 0)

    def slot(_, last):
        last, chance = next_slot(relative, chances, last)
        value = chance * LOSS_SCALE

        def strip(index, _):
            start = pl.multiple_of(index * STRIP, STRIP)
            rows = pl.ds(start, STRIP)
            ratio = squashed[rows]
            hit = row + start == last
            fresh = gradient(ratio, jnp.broadcast_to(value, ratio.shape), log_share)
            held = grads[rows].astype(jnp.float32)
            grads[rows] = jnp.where(hit, fresh, held).astype(jnp.bfloat16)
            if term is not None:
                product = jnp.where(hit, value * ratio, 0.0)
                term[...] += product[:8] + product[8:]
            return 0

        lax.fori_loop(0, grads.shape[0] // STRIP, strip, 0)
        return last

    lax.fori_loop(fast, count, slot, last)


def hidden_grad_kernel(
    counts,
    embed,
    squashed,
    total,
    ids,
    prob,
    grads,
    keep,
    give,
    rows_grad,
    flipped,
    term,
    ready,
    made,
):
    width = embed.shape[1]
    log_share = jnp.log2(LOSS_SCALE / total[:, 0:BLOCK])
    term[...] = jnp.zeros_like(term)
    ready[...] = jnp.zeros_like(ready)
    rows_grad[...] = jnp.zeros_like(rows_grad)
    tiles = PADDED // GRAD_TILE

    def rows_of(tile):
        return pl.ds(pl.multiple_of(tile * GRAD_TILE, GRAD_TILE), GRAD_TILE)

    def step(tile, _):
        rows = rows_of(tile)
        rows_grad[...] += dot_tn(ready[...], embed[rows_of(jnp.maximum(tile - 1, 0))])
        held = squashed.at[rows]
        slots = first_slots(ids[:, 0:BLOCK] - tile * GRAD_TILE, prob[:, 0:BLOCK], HIDDEN_SLOTS)
        logit_grads(held, made, log_share, slots, slice(0, BLOCK), term)

        @pl.when(counts[tile] > HIDDEN_SLOTS)
        def _():
            more_targets(
                held,
                made,
                log_share,
                ids[:, 0:BLOCK] - tile * GRAD_TILE,
                prob[:, 0:BLOCK],
                slots[-1][0],
                HIDDEN_SLOTS,
                counts[tile],
                term,
            )

        ready[...] = made[...]
        grads[rows] = made[...]
        return 0

    lax.fori_loop(0, tiles, step, 0)
    rows_grad[...] += dot_tn(ready[...], embed[rows_of(tiles - 1)])

    _, z, y, core = here()
    thin = keep.shape[2] - 8
    for part in range(width // BLOCK):
        span = slice(part * BLOCK, (part + 1) * BLOCK)
        flipped[span, :] = rows_grad[:, span].T
    summed = jnp.sum(term[...], axis=0, keepdims=True) * (SOFT_CAP / LOSS_SCALE)
    for outer in range(SIDE):
        for inner in range(SIDE):
            for ref, side in ((keep, core), (give, 1 - core)):
                rank = 2 * chip_of(outer, inner, side, z, y) + side
                start = pl.multiple_of(rank * thin, 8)
                ref[outer, inner, 0:thin] = flipped[pl.ds(start, thin)]
                ref[outer, inner, thin : thin + 8] = jnp.broadcast_to(summed, (8, BLOCK))


def halve_kernel(keep, got, *outs):
    for index, out in enumerate(outs):
        out[...] = keep[index] + got[index]


def quarter_kernel(*refs):
    parts, outs = refs[:SIDE], refs[SIDE:]
    for index, out in enumerate(outs):
        out[...] = (parts[0][index] + parts[1][index]) + (parts[2][index] + parts[3][index])


def finish_kernel(total, teacher_logits, *refs):
    parts, (hidden_grad, divergence) = refs[:SIDE], refs[SIDE:]
    _, z, y, core = here()
    summed = (parts[0][...] + parts[1][...]) + (parts[2][...] + parts[3][...])
    thin = hidden_grad.shape[0]
    hidden_grad[...] = summed[:thin].astype(jnp.bfloat16)
    scores = teacher_logits[...]
    share = scores.shape[0]
    shifted = scores - jnp.max(scores, axis=1, keepdims=True)
    raised = jnp.exp(shifted)
    prob = raised / jnp.sum(raised, axis=1, keepdims=True)
    entropy = jnp.sum(prob * jnp.log(prob), axis=1, keepdims=True)
    rest = jnp.log(total[:, 0:BLOCK]) - summed[thin : thin + 1]
    first = ((z * SIDE + y) * 2 + core) * share
    lane = lax.broadcasted_iota(jnp.int32, (share, BLOCK), 1)
    token = lax.broadcasted_iota(jnp.int32, (share, BLOCK), 0) + first
    value = entropy + jnp.sum(jnp.where(lane == token, rest, 0.0), axis=1, keepdims=True)
    line = lax.broadcasted_iota(jnp.int32, (share, HALF), 0)
    column = lax.broadcasted_iota(jnp.int32, (share, HALF), 1)
    divergence[...] = jnp.sum(jnp.where(line == column, value, 0.0), axis=0, keepdims=True)


def table_grad_kernel(
    width,
    fresh,
    counts,
    chunks,
    own_grads,
    side_squashed,
    far_squashed,
    total,
    ids,
    prob,
    packed_cot,
    packed_ids,
    own_columns,
    side_columns,
    far_columns,
    *refs,
):
    blocks = SIDE - 1
    tiles = PADDED // TABLE_TILE // 2
    first = 0 if fresh else tiles
    out, left, ready, made = refs[-4:]
    now = pl.program_id(0) == pl.num_programs(0) - 1

    if not fresh:

        @pl.when(jnp.logical_not(now))
        def _():
            out[...] = refs[0][...]

    def rows_of(tile):
        return pl.ds(pl.multiple_of(tile * TABLE_TILE, TABLE_TILE), TABLE_TILE)

    def onehot(tile, chunk):
        column = lax.broadcasted_iota(jnp.int32, (TABLE_TILE, BLOCK), 0) + tile * TABLE_TILE
        chosen = jnp.where(column == packed_ids[chunk], math.sqrt(width), 0.0)
        return chosen.astype(jnp.bfloat16)

    def product():
        return dot_nt(left[...], ready[...])

    def put(index, value):
        out[:, rows_of(index)] = value.astype(jnp.bfloat16)

    def more_lookups(index):
        spread = lax.fori_loop(
            1,
            chunks[0],
            lambda chunk, held: held + dot_nt(packed_cot[chunk], onehot(first + index, chunk)),
            product(),
        )
        put(index, spread)

    def step(index, _):
        tile = first + index
        rows = rows_of(tile)
        before = jnp.maximum(index - 1, 0)
        put(before, product())
        made[:, 0:BLOCK] = own_grads[rows]
        made[:, 4 * BLOCK :] = onehot(tile, 0)

        relative = ids[:, BLOCK:] - tile * TABLE_TILE
        chances = prob[:, BLOCK:]
        slots = first_slots(relative, chances, FAST_SLOTS)

        def of(block):
            lanes = pl.ds(block * BLOCK, BLOCK)
            held = far_squashed.at[rows] if block == 2 else side_squashed.at[rows, lanes]
            into = pl.ds((block + 1) * BLOCK, BLOCK)
            return held, made.at[:, into], jnp.log2(LOSS_SCALE / total[:, into])

        for block in range(blocks):
            logit_grads(*of(block), slots, slice(block * BLOCK, (block + 1) * BLOCK))
        for block in range(blocks):
            count = counts[tile * blocks + block]

            @pl.when(count > FAST_SLOTS)
            def _(block=block, count=count):
                own = pl.ds((block + 1) * BLOCK, BLOCK)
                more_targets(
                    *of(block),
                    ids[:, own] - tile * TABLE_TILE,
                    prob[:, own],
                    slots[-1][0][:, block * BLOCK : (block + 1) * BLOCK],
                    FAST_SLOTS,
                    count,
                )

        @pl.when((chunks[0] > 1) & (index > 0))
        def _():
            more_lookups(before)

        ready[...] = made[...]
        return 0

    @pl.when(now)
    def _():
        left[:, 0:BLOCK] = own_columns[0]
        left[:, BLOCK : 2 * BLOCK] = side_columns[0]
        left[:, 2 * BLOCK : 3 * BLOCK] = side_columns[1]
        left[:, 3 * BLOCK : 4 * BLOCK] = far_columns[0]
        left[:, 4 * BLOCK :] = packed_cot[0]
        ready[...] = jnp.zeros_like(ready)
        lax.fori_loop(0, tiles, step, 0)
        put(tiles - 1, product())

        @pl.when(chunks[0] > 1)
        def _():
            more_lookups(tiles - 1)


def smem():
    return pl.BlockSpec(memory_space=pltpu.SMEM)


def vmem():
    return pl.BlockSpec(memory_space=pltpu.VMEM)


def whole(shape):
    return pl.BlockSpec(shape, lambda *_: (0,) * len(shape))


def shape_of(shape, dtype):
    return jax.ShapeDtypeStruct(shape, dtype)


def small_call(kernel, name, outs, *args, scratch=(), limit=4 << 20):
    return pl.pallas_call(
        kernel,
        out_shape=tuple(shape_of(shape, dtype) for shape, dtype, _ in outs),
        in_specs=[vmem()] * len(args),
        out_specs=tuple(space() for _, _, space in outs),
        scratch_shapes=scratch,
        compiler_params=pltpu.CompilerParams(vmem_limit_bytes=limit),
        name=name,
    )(*args)


def logits_call(embed, near, far, columns, fresh):
    blocks = len(near)
    rows, width = embed.shape
    tokens = blocks * BLOCK
    length = ROW_STEP if fresh else LONG_STEP
    steps = ROW_STEP * (PADDED // ROW_STEP) // length
    table = whole((PADDED, width))
    out_specs = [
        whole((PADDED, tokens)),
        whole((1, tokens)),
        whole((blocks, columns, BLOCK)),
    ]
    out_shape = [
        pltpu.VMEM((PADDED, tokens), jnp.float32),
        shape_of((1, tokens), jnp.float32),
        shape_of((blocks, columns, BLOCK), jnp.bfloat16),
    ]
    scratch = [
        pltpu.VMEM((blocks, width, BLOCK), jnp.bfloat16),
        pltpu.VMEM((8, tokens), jnp.float32),
    ]
    if fresh:
        out_specs.append(table)
        out_shape.append(pltpu.VMEM((PADDED, width), embed.dtype))
        scratch.append(pltpu.SemaphoreType.DMA((steps,)))
    return pl.pallas_call(
        functools.partial(logit_kernel, blocks, fresh),
        grid=(steps,),
        in_specs=[pl.BlockSpec(memory_space=pltpu.HBM) if fresh else table]
        + [whole((width, HALF))] * (2 * blocks),
        out_specs=out_specs,
        out_shape=out_shape,
        scratch_shapes=scratch,
        compiler_params=pltpu.CompilerParams(vmem_limit_bytes=(3 + 2 * blocks) << 20),
        cost_estimate=pl.CostEstimate(
            flops=2 * rows * width * tokens,
            bytes_accessed=rows * tokens * 4 + (2 * rows * width if fresh else 0),
            transcendentals=2 * rows * tokens,
        ),
        name=f"logits_{blocks}",
    )(pltpu.with_memory_space_constraint(embed, pltpu.HBM) if fresh else embed, *near, *far)


def index_of(x, z, y, core):
    return ((x * SIDE + z) * SIDE + y) * 2 + core


def route_by(target):
    pairs = []
    for x in range(SIDE):
        for z in range(SIDE):
            for y in range(SIDE):
                for core in range(2):
                    pairs.append((index_of(x, z, y, core), index_of(*target(x, z, y, core))))
    return pairs


def along(axis, core, by, place):
    x, z, y = place
    if axis == 2:
        x = (x + (by if core == 0 else -by)) % SIDE
    elif axis == core:
        y = (y + by) % SIDE
    else:
        z = (z + by) % SIDE
    return x, z, y, core


def fetch(value, axis, by):
    return lax.ppermute(value, EVERY, route_by(lambda x, z, y, c: along(axis, c, -by, (x, z, y))))


def hand_on(value, axis, by):
    return lax.ppermute(value, EVERY, route_by(lambda x, z, y, c: along(axis, c, by, (x, z, y))))


def exchange(value, axis, bit):
    def other(x, z, y, core):
        return along(axis, core, ((y if axis == core else z) ^ bit) - (y if axis == core else z), (x, z, y))

    return lax.ppermute(value, EVERY, route_by(other))


def swap(value):
    return lax.ppermute(value, EVERY, route_by(lambda x, z, y, c: (x, z, y, 1 - c)))


def fetch_parts(value, axis):
    return [value] + [fetch(value, axis, by) for by in OFFSETS[1:]]


def fetch_all(value, axis):
    return jnp.concatenate(fetch_parts(value, axis), axis=0)


def halves(core_zero, low, high):
    return jnp.where(core_zero, low, high), jnp.where(core_zero, high, low)


def in_core_order(core_zero, kept, got):
    return jnp.where(
        core_zero, jnp.concatenate([kept, got], 0), jnp.concatenate([got, kept], 0)
    )


def side_values(core_zero, after, token_ids, lookup_cot, teacher_ids, teacher_logits):
    here_tokens, thin = lookup_cot.shape
    share = teacher_ids.shape[0]
    pack = jnp.concatenate(
        [
            jnp.concatenate([teacher_logits, teacher_ids.astype(jnp.float32)], axis=1),
            token_ids.astype(jnp.float32).reshape(here_tokens // HALF, HALF),
            jnp.zeros((8 - here_tokens // HALF, HALF), jnp.float32),
        ],
        axis=0,
    )
    pack, turned, _ = lax.optimization_barrier((pack, lookup_cot.T, after))
    moved = lax.ppermute(
        turned,
        EVERY,
        route_by(lambda x, z, y, c: (z, x, y, c)),
    ).astype(jnp.float32)
    packs = [pack] + [
        lax.ppermute(pack, "dp", [((k + by) % SIDE, k) for k in range(SIDE)])
        for by in OFFSETS[1:]
    ]
    far_away = [packs[0], packs[1], packs[3], packs[2]]
    sides = [
        jnp.concatenate(
            [
                moved[:, half * HALF : (half + 1) * HALF],
                far_away[2 * half][:share],
                far_away[2 * half + 1][:share],
            ],
            axis=0,
        )
        for half in range(2)
    ]
    return *halves(core_zero, *sides), jnp.stack(packs)


def per_device(hidden, embed, token_ids, lookup_cot, teacher_ids, teacher_logits):
    rows, width = embed.shape
    here_tokens, thin = hidden.shape
    dp = SIDE
    vocab = 2 * SIDE * SIDE
    tokens = here_tokens * dp
    top = teacher_ids.shape[1]
    share = here_tokens // vocab
    columns = width // dp
    core_zero = lax.axis_index("core") == 0

    flat = hidden.T
    kept, given = halves(core_zero, flat[:, :HALF], flat[:, HALF:])
    pair = in_core_order(core_zero, kept, swap(given))
    row = fetch_all(pair, 0)
    own_near = fetch_all(row, 1)
    side = side_values(core_zero, row, token_ids, lookup_cot, teacher_ids, teacher_logits)
    own_near, kept, given, packs = lax.optimization_barrier((own_near, *side))
    first_near = fetch(own_near, 2, 1)
    second_near = fetch(own_near, 2, -1)
    own_far = swap(own_near)
    own_squashed, own_total, own_columns, table = logits_call(
        embed, [own_near], [own_far], columns, True
    )
    given = lax.optimization_barrier((given, own_total))[0]
    side = in_core_order(core_zero, kept, swap(given))
    first_near, second_near, side = lax.optimization_barrier((first_near, second_near, side))
    opposite_near = fetch(first_near, 2, 1)
    first_far = swap(second_near)
    second_far = swap(first_near)
    side_parts = fetch_parts(side, 0)
    side_squashed, side_total, side_columns = logits_call(
        table, [first_near, second_near], [first_far, second_far], columns, False
    )
    side_parts, opposite_near, side_total = lax.optimization_barrier(
        (side_parts, opposite_near, side_total)
    )
    opposite_far = swap(opposite_near)
    side_parts = fetch_parts(jnp.concatenate(side_parts, axis=0), 1)
    far_squashed, far_total, far_columns = logits_call(
        table, [opposite_near], [opposite_far], columns, False
    )
    side_parts, far_total = lax.optimization_barrier((side_parts, far_total))
    side_near = jnp.concatenate(side_parts, axis=0)
    side_far = swap(side_near)

    total = jnp.concatenate([own_total, side_total, far_total], axis=1)
    got = swap(total)
    total = total + jnp.concatenate(
        [
            got[:, :BLOCK],
            got[:, 2 * BLOCK : 3 * BLOCK],
            got[:, BLOCK : 2 * BLOCK],
            got[:, 3 * BLOCK :],
        ],
        axis=1,
    )
    for axis in (0, 1):
        for bit in (1, 2):
            total = total + exchange(total, axis, bit)

    cot, ids, prob, row_counts, column_counts = small_call(
        functools.partial(teacher_kernel, rows, thin),
        "teacher_prep",
        [
            ((width, BLOCK), jnp.float32, vmem),
            ((top, tokens), jnp.int32, vmem),
            ((top, tokens), jnp.float32, vmem),
            ((PADDED // GRAD_TILE,), jnp.int32, smem),
            ((PADDED // TABLE_TILE * (dp - 1),), jnp.int32, smem),
        ],
        side_near,
        side_far,
        scratch=[pltpu.VMEM((dp, BLOCK, 2 * top), jnp.float32)],
    )
    packed_cot, packed_ids, chunks = small_call(
        functools.partial(lookup_kernel, rows, share),
        "lookup_prep",
        [
            ((dp, columns, BLOCK), jnp.bfloat16, vmem),
            ((dp, 1, BLOCK), jnp.int32, vmem),
            ((1,), jnp.int32, smem),
        ],
        packs,
        cot,
        scratch=[pltpu.VMEM((1, tokens), jnp.float32)],
    )

    scattered = (SIDE, SIDE, thin + 8, BLOCK)
    own_grads, keep, give = pl.pallas_call(
        hidden_grad_kernel,
        in_specs=[smem()] + [vmem()] * 5,
        out_specs=[vmem()] * 3,
        out_shape=(
            pltpu.VMEM((PADDED, BLOCK), jnp.bfloat16),
            shape_of(scattered, jnp.float32),
            shape_of(scattered, jnp.float32),
        ),
        scratch_shapes=[
            pltpu.VMEM((BLOCK, width), jnp.float32),
            pltpu.VMEM((width, BLOCK), jnp.float32),
            pltpu.VMEM((8, BLOCK), jnp.float32),
            pltpu.VMEM((GRAD_TILE, BLOCK), jnp.bfloat16),
            pltpu.VMEM((GRAD_TILE, BLOCK), jnp.bfloat16),
        ],
        compiler_params=pltpu.CompilerParams(vmem_limit_bytes=10 << 20),
        cost_estimate=pl.CostEstimate(
            flops=2 * rows * width * BLOCK,
            bytes_accessed=rows * BLOCK * 6,
            transcendentals=rows * BLOCK,
        ),
        name="hidden_grads",
    )(row_counts, table, own_squashed, total, ids, prob)

    def table_grads(so_far):
        fresh = so_far is None
        started = [] if fresh else [so_far]
        operands = [
            column_counts,
            chunks,
            own_grads,
            side_squashed,
            far_squashed,
            total,
            ids,
            prob,
            packed_cot,
            packed_ids,
            own_columns,
            side_columns,
            far_columns,
        ]
        made = PADDED // 2
        half = (columns, PADDED // 2)
        return pl.pallas_call(
            functools.partial(table_grad_kernel, width, fresh),
            grid=(1 if fresh else 2,),
            in_specs=[smem()] * 2
            + [whole(operand.shape) for operand in operands[2:]]
            + [whole(half) for _ in started],
            out_specs=pl.BlockSpec(half, lambda n: (0, n)),
            out_shape=pltpu.VMEM(half, jnp.bfloat16)
            if fresh
            else shape_of((columns, rows), jnp.bfloat16),
            scratch_shapes=[
                pltpu.VMEM((columns, (dp + 1) * BLOCK), jnp.bfloat16),
                pltpu.VMEM((TABLE_TILE, (dp + 1) * BLOCK), jnp.bfloat16),
                pltpu.VMEM((TABLE_TILE, (dp + 1) * BLOCK), jnp.bfloat16),
            ],
            compiler_params=pltpu.CompilerParams(vmem_limit_bytes=12 << 20),
            cost_estimate=pl.CostEstimate(
                flops=2 * made * columns * (tokens + BLOCK),
                bytes_accessed=rows * columns * 2,
                transcendentals=made * tokens,
            ),
            name="table_grads_start" if fresh else "table_grads_rest",
        )(*operands, *started)

    quarter = (SIDE, thin + 8, BLOCK)
    got, packed_cot, packed_ids = lax.optimization_barrier((swap(give), packed_cot, packed_ids))
    parts = small_call(halve_kernel, "halve", [(quarter, jnp.float32, vmem)] * SIDE, keep, got)
    travelling = [hand_on(part, 1, by) for part, by in zip(parts[1:], OFFSETS[1:])]
    embed_grad = table_grads(None)
    travelling, embed_grad = lax.optimization_barrier((travelling, embed_grad))
    parts = small_call(
        quarter_kernel,
        "quarter",
        [(quarter[1:], jnp.float32, vmem)] * SIDE,
        parts[0],
        *travelling,
    )
    travelling = [hand_on(part, 0, by) for part, by in zip(parts[1:], OFFSETS[1:])]
    embed_grad = table_grads(embed_grad)
    parts = [parts[0]] + travelling

    hidden_grad, divergence = small_call(
        finish_kernel,
        "finish",
        [((thin, BLOCK), jnp.bfloat16, vmem), ((1, HALF), jnp.float32, vmem)],
        total,
        teacher_logits,
        *parts,
    )
    return (hidden_grad.T, embed_grad.T, divergence[0, :share])


def solution(mesh):
    dp, vocab = (mesh.shape[name] for name in ("dp", "vocab"))
    fine = Mesh(mesh.devices.reshape(dp, SIDE, SIDE, vocab // (SIDE * SIDE)), EVERY)
    return jax.shard_map(
        per_device,
        mesh=fine,
        in_specs=(
            P("dp", RING),
            P(RING, None),
            P("dp"),
            P("dp", RING),
            P(EVERY, None),
            P(EVERY, None),
        ),
        out_specs=(P("dp", RING), P(RING, "dp"), P(EVERY)),
        check_vma=False,
    )
```

```python
import functools
import math

import jax
import jax.numpy as jnp
from jax import lax
from jax.experimental import pallas as pl
from jax.experimental.pallas import tpu as pltpu
from jax.sharding import Mesh, PartitionSpec as P

SOFT_CAP = 30.0
LOSS_SCALE = 16.0
BLOCK = 256
HALF = 128
ROW_TILE = 400
ROW_STEP = 800
LONG_STEP = 2000
PADDED = 4096
STRIP = 16
WIDE_STRIP = 32
GRAD_TILE = 1024
TABLE_TILE = 512
FAST_SLOTS = 4
HIDDEN_SLOTS = 5
FAR = 1 << 30
LOG2_E = math.log2(math.e)
RING = ("z", "y", "core")
EVERY = ("dp",) + RING
SIDE = 4
OFFSETS = (0, 1, 3, 2)


def dot_nn(a, b):
    return lax.dot_general(a, b, (((1,), (0,)), ((), ())), preferred_element_type=jnp.float32)


def dot_nt(a, b):
    return lax.dot_general(a, b, (((1,), (1,)), ((), ())), preferred_element_type=jnp.float32)


def dot_tn(a, b):
    return lax.dot_general(a, b, (((0,), (0,)), ((), ())), preferred_element_type=jnp.float32)


def offset_of(index, core):
    return jnp.where(core == 0, OFFSETS[index], OFFSETS[(0, 2, 1, 3)[index]])


def chip_of(outer, inner, core, z, y):
    first, second = OFFSETS[inner], OFFSETS[outer]
    row = lax.rem(z + jnp.where(core == 0, second, first), SIDE)
    column = lax.rem(y + jnp.where(core == 0, first, second), SIDE)
    return row * SIDE + column


def here():
    return tuple(lax.axis_index(name) for name in EVERY)


def block_offset(rows, z, y, core):
    return ((z * SIDE + y) * 2 + core) * rows


def teacher_kernel(rows, thin, near, far, cot, ids, prob, row_counts, column_counts, joined):
    _, z, y, core = here()
    offset = block_offset(rows, z, y, core)
    top = ids.shape[0]
    share = 8
    group = thin + 2 * share
    for side, source in ((core, near), (1 - core, far)):
        lanes = pl.ds(pl.multiple_of(side * HALF, HALF), HALF)
        for outer in range(SIDE):
            for inner in range(SIDE):
                chip = chip_of(outer, inner, side, z, y)
                for other in range(2):
                    start = ((outer * SIDE + inner) * 2 + other) * group
                    rank = chip * 2 + other
                    into = pl.multiple_of(rank * thin, 8)
                    cot[pl.ds(into, thin), lanes] = source[start : start + thin]
                    for half in range(2):
                        held = source[start + thin + half * share : start + thin + (half + 1) * share]
                        joined[side * 2 + half, pl.ds(pl.multiple_of(rank * share, 8), share)] = held
    for block in range(SIDE):
        flipped = joined[offset_of(block, core)].T
        scores = flipped[:top]
        local = flipped[top:].astype(jnp.int32) - offset
        raised = jnp.exp(scores - jnp.max(scores, axis=0, keepdims=True))
        lanes = slice(block * BLOCK, (block + 1) * BLOCK)
        ids[:, lanes] = local
        prob[:, lanes] = raised / jnp.sum(raised, axis=0, keepdims=True)
        for tile in range(PADDED // TABLE_TILE):
            first = tile * TABLE_TILE
            inside = (local >= first) & (local < min(first + TABLE_TILE, rows))
            most = jnp.max(jnp.sum(inside.astype(jnp.int32), axis=0))
            if block == 0:
                row_counts[tile] = most
            else:
                column_counts[tile * (SIDE - 1) + block - 1] = most


def lookup_kernel(rows, share, packs, cot, packed_cot, packed_ids, chunks, tokens):
    mine, z, y, core = here()
    offset = block_offset(rows, z, y, core)
    count = tokens.shape[1]
    blocks = count // BLOCK
    for index in range(blocks):
        start = lax.rem(mine + OFFSETS[index], blocks) * BLOCK
        for half in range(BLOCK // HALF):
            lanes = pl.ds(pl.multiple_of(start + half * HALF, HALF), HALF)
            tokens[:, lanes] = packs[index, share + half : share + half + 1]
    local = tokens[...].astype(jnp.int32) - offset
    inside = (local >= 0) & (local < rows)
    hit = jnp.broadcast_to(jnp.where(inside, 1.0, 0.0), (8, count))
    before = lax.broadcasted_iota(jnp.int32, (count, count), 0)
    after = lax.broadcasted_iota(jnp.int32, (count, count), 1)
    upto = jnp.where(before <= after, 1.0, 0.0).astype(jnp.bfloat16)
    running = dot_nn(hit.astype(jnp.bfloat16), upto)[0:1].astype(jnp.int32)
    rank = jnp.where(inside, running - 1, -1)
    total = jnp.max(running)
    chunks[0] = (total + BLOCK - 1) // BLOCK
    safe = jnp.where(inside, local, 0)
    high = jnp.broadcast_to((safe >> 6).astype(jnp.float32), (8, count)).astype(jnp.bfloat16)
    low = jnp.broadcast_to((safe & 63).astype(jnp.float32), (8, count)).astype(jnp.bfloat16)
    for chunk in range(blocks):

        @pl.when(chunk * BLOCK < jnp.maximum(total, 1))
        def _():
            slot = lax.broadcasted_iota(jnp.int32, (BLOCK, count), 0) + chunk * BLOCK
            chosen = jnp.where(slot == rank, 1.0, 0.0).astype(jnp.bfloat16)
            columns = cot.shape[0] // blocks
            taken = jnp.zeros((columns, BLOCK), jnp.float32)
            for block in range(blocks):
                span = slice(block * BLOCK, (block + 1) * BLOCK)
                part = cot[block * columns : (block + 1) * columns].astype(jnp.bfloat16)
                taken = taken + dot_nt(part, chosen[:, span])
            packed_cot[chunk] = taken.astype(jnp.bfloat16)
            row = dot_nt(high, chosen)[0:1] * 64.0 + dot_nt(low, chosen)[0:1]
            used = dot_nt(hit.astype(jnp.bfloat16), chosen)[0:1] > 0.5
            packed_ids[chunk] = jnp.where(used, row.astype(jnp.int32), -1)


def next_slot(relative, prob, last):
    following = jnp.min(jnp.where(relative > last, relative, FAR), axis=0, keepdims=True)
    chance = jnp.sum(jnp.where(relative == following, prob, 0.0), axis=0, keepdims=True)
    return following, chance


def join_halves(near, far, joined):
    _, z, y, core = here()
    pair = near.shape[0] // (SIDE * SIDE)
    for side, source in ((core, near), (1 - core, far)):
        lanes = pl.ds(pl.multiple_of(side * HALF, HALF), HALF)
        for outer in range(SIDE):
            for inner in range(SIDE):
                start = (outer * SIDE + inner) * pair
                into = pl.multiple_of(chip_of(outer, inner, side, z, y) * pair, 16)
                joined[pl.ds(into, pair), lanes] = source[start : start + pair]


def table_copy(step, table, held, ready):
    rows = pl.ds(pl.multiple_of(step * ROW_STEP, STRIP), ROW_STEP)
    return pltpu.make_async_copy(table.at[rows], held.at[rows], ready.at[step])


def logit_kernel(blocks, fresh, embed, *refs):
    near, far = refs[:blocks], refs[blocks : 2 * blocks]
    squashed, total, columns = refs[2 * blocks : 2 * blocks + 3]
    rest = refs[2 * blocks + 3 :]
    step = pl.program_id(0)
    steps = pl.num_programs(0)
    length = ROW_STEP if fresh else LONG_STEP
    if fresh:
        held, hidden, sums, ready = rest

        @pl.when(step == 0)
        def _():
            for index in range(embed.shape[0] // ROW_STEP):
                table_copy(index, embed, held, ready).start()
            rows = embed.shape[0]
            held[rows:] = jnp.zeros((PADDED - rows, held.shape[1]), held.dtype)

    else:
        held, (hidden, sums) = embed, rest

    @pl.when(step == 0)
    def _():
        sums[...] = jnp.zeros_like(sums)
        used = ROW_STEP * (PADDED // ROW_STEP)
        squashed[used:] = jnp.zeros((PADDED - used, squashed.shape[1]), jnp.float32)
        size = columns.shape[1]
        start = pl.multiple_of(lax.axis_index("dp") * size, 16)
        for block in range(blocks):
            join_halves(near[block], far[block], hidden.at[block])
            columns[block] = hidden[block, pl.ds(start, size)]

    if fresh:
        table_copy(step, embed, held, ready).wait()

    for first in range(0, length, ROW_TILE):
        from_table = pl.ds(pl.multiple_of(step * length + first, STRIP), ROW_TILE)
        for block in range(blocks):
            span = slice(block * BLOCK, (block + 1) * BLOCK)
            raw = dot_nn(held[from_table], hidden[block])
            raised = jnp.zeros((8, BLOCK), jnp.float32)
            for chunk in range(0, ROW_TILE, STRIP):
                ratio = jnp.tanh(raw[chunk : chunk + STRIP] * (1.0 / SOFT_CAP))
                into = pl.multiple_of(step * length + first + chunk, STRIP)
                squashed[pl.ds(into, STRIP), span] = ratio
                power = jnp.exp2(ratio * (SOFT_CAP * LOG2_E))
                raised = raised + (power[:8] + power[8:])
            sums[:, span] += raised

    @pl.when(step == steps - 1)
    def _():
        total[...] = jnp.sum(sums[...], axis=0, keepdims=True)


def gradient(ratio, target, log_share):
    share = jnp.exp2(ratio * (SOFT_CAP * LOG2_E) + log_share)
    return (share - target) * (1.0 - ratio * ratio)


def first_slots(relative, chances, fast):
    last = jnp.full((1, relative.shape[1]), -1, jnp.int32)
    slots = []
    for _ in range(fast):
        last, chance = next_slot(relative, chances, last)
        slots.append((last, chance * LOSS_SCALE))
    return slots


def logit_grads(squashed, grads, log_share, slots, lanes, term=None):
    row = lax.broadcasted_iota(jnp.int32, (WIDE_STRIP, BLOCK), 0)
    added = jnp.zeros((8, BLOCK), jnp.float32)
    for start in range(0, grads.shape[0], WIDE_STRIP):
        strip = slice(start, start + WIDE_STRIP)
        ratio = squashed[strip]
        target = jnp.zeros((WIDE_STRIP, BLOCK), jnp.float32)
        for where, value in slots:
            target = jnp.where(row + start == where[:, lanes], value[:, lanes], target)
        grads[strip] = gradient(ratio, target, log_share).astype(jnp.bfloat16)
        if term is not None:
            product = target * ratio
            added = added + jnp.sum(product.reshape(WIDE_STRIP // 8, 8, BLOCK), axis=0)
    if term is not None:
        term[...] += added


def more_targets(
    squashed, grads, log_share, relative, chances, last, fast, count, term=None
):
    row = lax.broadcasted_iota(jnp.int32, (STRIP, BLOCK), 0)

    def slot(_, last):
        last, chance = next_slot(relative, chances, last)
        value = chance * LOSS_SCALE

        def strip(index, _):
            start = pl.multiple_of(index * STRIP, STRIP)
            rows = pl.ds(start, STRIP)
            ratio = squashed[rows]
            hit = row + start == last
            fresh = gradient(ratio, jnp.broadcast_to(value, ratio.shape), log_share)
            held = grads[rows].astype(jnp.float32)
            grads[rows] = jnp.where(hit, fresh, held).astype(jnp.bfloat16)
            if term is not None:
                product = jnp.where(hit, value * ratio, 0.0)
                term[...] += product[:8] + product[8:]
            return 0

        lax.fori_loop(0, grads.shape[0] // STRIP, strip, 0)
        return last

    lax.fori_loop(fast, count, slot, last)


def hidden_grad_kernel(
    counts,
    embed,
    squashed,
    total,
    ids,
    prob,
    grads,
    keep,
    give,
    rows_grad,
    flipped,
    term,
    ready,
    made,
):
    width = embed.shape[1]
    log_share = jnp.log2(LOSS_SCALE / total[:, 0:BLOCK])
    term[...] = jnp.zeros_like(term)
    ready[...] = jnp.zeros_like(ready)
    rows_grad[...] = jnp.zeros_like(rows_grad)
    tiles = PADDED // GRAD_TILE

    def rows_of(tile):
        return pl.ds(pl.multiple_of(tile * GRAD_TILE, GRAD_TILE), GRAD_TILE)

    def step(tile, _):
        rows = rows_of(tile)
        rows_grad[...] += dot_tn(ready[...], embed[rows_of(jnp.maximum(tile - 1, 0))])
        pieces = []
        for part in range(GRAD_TILE // TABLE_TILE):
            piece = tile * (GRAD_TILE // TABLE_TILE) + part
            start = pl.multiple_of(piece * TABLE_TILE, TABLE_TILE)
            held = squashed.at[pl.ds(start, TABLE_TILE)]
            into = made.at[pl.ds(part * TABLE_TILE, TABLE_TILE)]
            slots = first_slots(ids[:, 0:BLOCK] - start, prob[:, 0:BLOCK], HIDDEN_SLOTS)
            logit_grads(held, into, log_share, slots, slice(0, BLOCK), term)
            pieces.append((piece, start, held, into, slots[-1][0]))

        for piece, start, held, into, last in pieces:

            @pl.when(counts[piece] > HIDDEN_SLOTS)
            def _(piece=piece, start=start, held=held, into=into, last=last):
                more_targets(
                    held,
                    into,
                    log_share,
                    ids[:, 0:BLOCK] - start,
                    prob[:, 0:BLOCK],
                    last,
                    HIDDEN_SLOTS,
                    counts[piece],
                    term,
                )

        ready[...] = made[...]
        grads[rows] = made[...]
        return 0

    lax.fori_loop(0, tiles, step, 0)
    rows_grad[...] += dot_tn(ready[...], embed[rows_of(tiles - 1)])

    _, z, y, core = here()
    thin = keep.shape[2] - 8
    for part in range(width // BLOCK):
        span = slice(part * BLOCK, (part + 1) * BLOCK)
        flipped[span, :] = rows_grad[:, span].T
    summed = jnp.sum(term[...], axis=0, keepdims=True) * (SOFT_CAP / LOSS_SCALE)
    for outer in range(SIDE):
        for inner in range(SIDE):
            for ref, side in ((keep, core), (give, 1 - core)):
                rank = 2 * chip_of(outer, inner, side, z, y) + side
                start = pl.multiple_of(rank * thin, 8)
                ref[outer, inner, 0:thin] = flipped[pl.ds(start, thin)]
                ref[outer, inner, thin : thin + 8] = jnp.broadcast_to(summed, (8, BLOCK))


def halve_kernel(keep, got, *outs):
    for index, out in enumerate(outs):
        out[...] = keep[index] + got[index]


def quarter_kernel(*refs):
    parts, outs = refs[:SIDE], refs[SIDE:]
    for index, out in enumerate(outs):
        out[...] = (parts[0][index] + parts[1][index]) + (parts[2][index] + parts[3][index])


def finish_kernel(total, teacher_logits, *refs):
    parts, (hidden_grad, divergence) = refs[:SIDE], refs[SIDE:]
    _, z, y, core = here()
    summed = (parts[0][...] + parts[1][...]) + (parts[2][...] + parts[3][...])
    thin = hidden_grad.shape[0]
    hidden_grad[...] = summed[:thin].astype(jnp.bfloat16)
    scores = teacher_logits[...]
    share = scores.shape[0]
    shifted = scores - jnp.max(scores, axis=1, keepdims=True)
    raised = jnp.exp(shifted)
    prob = raised / jnp.sum(raised, axis=1, keepdims=True)
    entropy = jnp.sum(prob * jnp.log(prob), axis=1, keepdims=True)
    rest = jnp.log(total[:, 0:BLOCK]) - summed[thin : thin + 1]
    first = ((z * SIDE + y) * 2 + core) * share
    lane = lax.broadcasted_iota(jnp.int32, (share, BLOCK), 1)
    token = lax.broadcasted_iota(jnp.int32, (share, BLOCK), 0) + first
    value = entropy + jnp.sum(jnp.where(lane == token, rest, 0.0), axis=1, keepdims=True)
    line = lax.broadcasted_iota(jnp.int32, (share, HALF), 0)
    column = lax.broadcasted_iota(jnp.int32, (share, HALF), 1)
    divergence[...] = jnp.sum(jnp.where(line == column, value, 0.0), axis=0, keepdims=True)


def table_grad_kernel(
    width,
    fresh,
    counts,
    chunks,
    own_grads,
    side_squashed,
    far_squashed,
    total,
    ids,
    prob,
    packed_cot,
    packed_ids,
    own_columns,
    side_columns,
    far_columns,
    *refs,
):
    blocks = SIDE - 1
    tiles = PADDED // TABLE_TILE // 2
    first = 0 if fresh else tiles
    out, left, ready, made = refs[-4:]
    now = pl.program_id(0) == pl.num_programs(0) - 1

    if not fresh:

        @pl.when(jnp.logical_not(now))
        def _():
            out[...] = refs[0][...]

    def rows_of(tile):
        return pl.ds(pl.multiple_of(tile * TABLE_TILE, TABLE_TILE), TABLE_TILE)

    def onehot(tile, chunk):
        column = lax.broadcasted_iota(jnp.int32, (TABLE_TILE, BLOCK), 0) + tile * TABLE_TILE
        chosen = jnp.where(column == packed_ids[chunk], math.sqrt(width), 0.0)
        return chosen.astype(jnp.bfloat16)

    def product():
        return dot_nt(left[...], ready[...])

    def put(index, value):
        out[:, rows_of(index)] = value.astype(jnp.bfloat16)

    def more_lookups(index):
        spread = lax.fori_loop(
            1,
            chunks[0],
            lambda chunk, held: held + dot_nt(packed_cot[chunk], onehot(first + index, chunk)),
            product(),
        )
        put(index, spread)

    def step(index, _):
        tile = first + index
        rows = rows_of(tile)
        before = jnp.maximum(index - 1, 0)
        put(before, product())
        made[:, 0:BLOCK] = own_grads[rows]
        made[:, 4 * BLOCK :] = onehot(tile, 0)

        relative = ids[:, BLOCK:] - tile * TABLE_TILE
        chances = prob[:, BLOCK:]
        slots = first_slots(relative, chances, FAST_SLOTS)

        def of(block):
            lanes = pl.ds(block * BLOCK, BLOCK)
            held = far_squashed.at[rows] if block == 2 else side_squashed.at[rows, lanes]
            into = pl.ds((block + 1) * BLOCK, BLOCK)
            return held, made.at[:, into], jnp.log2(LOSS_SCALE / total[:, into])

        for block in range(blocks):
            logit_grads(*of(block), slots, slice(block * BLOCK, (block + 1) * BLOCK))
        for block in range(blocks):
            count = counts[tile * blocks + block]

            @pl.when(count > FAST_SLOTS)
            def _(block=block, count=count):
                own = pl.ds((block + 1) * BLOCK, BLOCK)
                more_targets(
                    *of(block),
                    ids[:, own] - tile * TABLE_TILE,
                    prob[:, own],
                    slots[-1][0][:, block * BLOCK : (block + 1) * BLOCK],
                    FAST_SLOTS,
                    count,
                )

        @pl.when((chunks[0] > 1) & (index > 0))
        def _():
            more_lookups(before)

        ready[...] = made[...]
        return 0

    @pl.when(now)
    def _():
        left[:, 0:BLOCK] = own_columns[0]
        left[:, BLOCK : 2 * BLOCK] = side_columns[0]
        left[:, 2 * BLOCK : 3 * BLOCK] = side_columns[1]
        left[:, 3 * BLOCK : 4 * BLOCK] = far_columns[0]
        left[:, 4 * BLOCK :] = packed_cot[0]
        ready[...] = jnp.zeros_like(ready)
        lax.fori_loop(0, tiles, step, 0)
        put(tiles - 1, product())

        @pl.when(chunks[0] > 1)
        def _():
            more_lookups(tiles - 1)


def smem():
    return pl.BlockSpec(memory_space=pltpu.SMEM)


def vmem():
    return pl.BlockSpec(memory_space=pltpu.VMEM)


def whole(shape):
    return pl.BlockSpec(shape, lambda *_: (0,) * len(shape))


def shape_of(shape, dtype):
    return jax.ShapeDtypeStruct(shape, dtype)


def small_call(kernel, name, outs, *args, scratch=(), limit=4 << 20):
    return pl.pallas_call(
        kernel,
        out_shape=tuple(shape_of(shape, dtype) for shape, dtype, _ in outs),
        in_specs=[vmem()] * len(args),
        out_specs=tuple(space() for _, _, space in outs),
        scratch_shapes=scratch,
        compiler_params=pltpu.CompilerParams(vmem_limit_bytes=limit),
        name=name,
    )(*args)


def logits_call(embed, near, far, columns, fresh):
    blocks = len(near)
    rows, width = embed.shape
    tokens = blocks * BLOCK
    length = ROW_STEP if fresh else LONG_STEP
    steps = ROW_STEP * (PADDED // ROW_STEP) // length
    table = whole((PADDED, width))
    out_specs = [
        whole((PADDED, tokens)),
        whole((1, tokens)),
        whole((blocks, columns, BLOCK)),
    ]
    out_shape = [
        pltpu.VMEM((PADDED, tokens), jnp.float32),
        shape_of((1, tokens), jnp.float32),
        shape_of((blocks, columns, BLOCK), jnp.bfloat16),
    ]
    scratch = [
        pltpu.VMEM((blocks, width, BLOCK), jnp.bfloat16),
        pltpu.VMEM((8, tokens), jnp.float32),
    ]
    if fresh:
        out_specs.append(table)
        out_shape.append(pltpu.VMEM((PADDED, width), embed.dtype))
        scratch.append(pltpu.SemaphoreType.DMA((steps,)))
    return pl.pallas_call(
        functools.partial(logit_kernel, blocks, fresh),
        grid=(steps,),
        in_specs=[pl.BlockSpec(memory_space=pltpu.HBM) if fresh else table]
        + [whole((width, HALF))] * (2 * blocks),
        out_specs=out_specs,
        out_shape=out_shape,
        scratch_shapes=scratch,
        compiler_params=pltpu.CompilerParams(vmem_limit_bytes=(3 + 2 * blocks) << 20),
        cost_estimate=pl.CostEstimate(
            flops=2 * rows * width * tokens,
            bytes_accessed=rows * tokens * 4 + (2 * rows * width if fresh else 0),
            transcendentals=2 * rows * tokens,
        ),
        name=f"logits_{blocks}",
    )(pltpu.with_memory_space_constraint(embed, pltpu.HBM) if fresh else embed, *near, *far)


def index_of(x, z, y, core):
    return ((x * SIDE + z) * SIDE + y) * 2 + core


def route_by(target):
    pairs = []
    for x in range(SIDE):
        for z in range(SIDE):
            for y in range(SIDE):
                for core in range(2):
                    pairs.append((index_of(x, z, y, core), index_of(*target(x, z, y, core))))
    return pairs


def along(axis, core, by, place):
    x, z, y = place
    if axis == 2:
        x = (x + (by if core == 0 else -by)) % SIDE
    elif axis == core:
        y = (y + by) % SIDE
    else:
        z = (z + by) % SIDE
    return x, z, y, core


def fetch(value, axis, by):
    return lax.ppermute(value, EVERY, route_by(lambda x, z, y, c: along(axis, c, -by, (x, z, y))))


def hand_on(value, axis, by):
    return lax.ppermute(value, EVERY, route_by(lambda x, z, y, c: along(axis, c, by, (x, z, y))))


def exchange(value, axis, bit):
    def other(x, z, y, core):
        return along(axis, core, ((y if axis == core else z) ^ bit) - (y if axis == core else z), (x, z, y))

    return lax.ppermute(value, EVERY, route_by(other))


def swap(value):
    return lax.ppermute(value, EVERY, route_by(lambda x, z, y, c: (x, z, y, 1 - c)))


def fetch_parts(value, axis):
    return [value] + [fetch(value, axis, by) for by in OFFSETS[1:]]


def fetch_all(value, axis):
    return jnp.concatenate(fetch_parts(value, axis), axis=0)


def halves(core_zero, low, high):
    return jnp.where(core_zero, low, high), jnp.where(core_zero, high, low)


def in_core_order(core_zero, kept, got):
    return jnp.where(
        core_zero, jnp.concatenate([kept, got], 0), jnp.concatenate([got, kept], 0)
    )


def side_values(core_zero, after, token_ids, lookup_cot, teacher_ids, teacher_logits):
    here_tokens, thin = lookup_cot.shape
    share = teacher_ids.shape[0]
    pack = jnp.concatenate(
        [
            jnp.concatenate([teacher_logits, teacher_ids.astype(jnp.float32)], axis=1),
            token_ids.astype(jnp.float32).reshape(here_tokens // HALF, HALF),
            jnp.zeros((8 - here_tokens // HALF, HALF), jnp.float32),
        ],
        axis=0,
    )
    pack, turned, _ = lax.optimization_barrier((pack, lookup_cot.T, after))
    moved = lax.ppermute(
        turned,
        EVERY,
        route_by(lambda x, z, y, c: (z, x, y, c)),
    ).astype(jnp.float32)
    packs = [pack] + [
        lax.ppermute(pack, "dp", [((k + by) % SIDE, k) for k in range(SIDE)])
        for by in OFFSETS[1:]
    ]
    far_away = [packs[0], packs[1], packs[3], packs[2]]
    sides = [
        jnp.concatenate(
            [
                moved[:, half * HALF : (half + 1) * HALF],
                far_away[2 * half][:share],
                far_away[2 * half + 1][:share],
            ],
            axis=0,
        )
        for half in range(2)
    ]
    return *halves(core_zero, *sides), jnp.stack(packs)


def per_device(hidden, embed, token_ids, lookup_cot, teacher_ids, teacher_logits):
    rows, width = embed.shape
    here_tokens, thin = hidden.shape
    dp = SIDE
    vocab = 2 * SIDE * SIDE
    tokens = here_tokens * dp
    top = teacher_ids.shape[1]
    share = here_tokens // vocab
    columns = width // dp
    core_zero = lax.axis_index("core") == 0

    flat = hidden.T
    kept, given = halves(core_zero, flat[:, :HALF], flat[:, HALF:])
    pair = in_core_order(core_zero, kept, swap(given))
    row = fetch_all(pair, 0)
    own_near = fetch_all(row, 1)
    side = side_values(core_zero, row, token_ids, lookup_cot, teacher_ids, teacher_logits)
    own_near, kept, given, packs = lax.optimization_barrier((own_near, *side))
    first_near = fetch(own_near, 2, 1)
    second_near = fetch(own_near, 2, -1)
    own_far = swap(own_near)
    own_squashed, own_total, own_columns, table = logits_call(
        embed, [own_near], [own_far], columns, True
    )
    given = lax.optimization_barrier((given, own_total))[0]
    side = in_core_order(core_zero, kept, swap(given))
    first_near, second_near, side = lax.optimization_barrier((first_near, second_near, side))
    opposite_near = fetch(first_near, 2, 1)
    first_far = swap(second_near)
    second_far = swap(first_near)
    side_parts = fetch_parts(side, 0)
    side_squashed, side_total, side_columns = logits_call(
        table, [first_near, second_near], [first_far, second_far], columns, False
    )
    side_parts, opposite_near, side_total = lax.optimization_barrier(
        (side_parts, opposite_near, side_total)
    )
    opposite_far = swap(opposite_near)
    side_parts = fetch_parts(jnp.concatenate(side_parts, axis=0), 1)
    far_squashed, far_total, far_columns = logits_call(
        table, [opposite_near], [opposite_far], columns, False
    )
    side_parts, far_total = lax.optimization_barrier((side_parts, far_total))
    side_near = jnp.concatenate(side_parts, axis=0)
    side_far = swap(side_near)

    total = jnp.concatenate([own_total, side_total, far_total], axis=1)
    got = swap(total)
    total = total + jnp.concatenate(
        [
            got[:, :BLOCK],
            got[:, 2 * BLOCK : 3 * BLOCK],
            got[:, BLOCK : 2 * BLOCK],
            got[:, 3 * BLOCK :],
        ],
        axis=1,
    )
    for axis in (0, 1):
        for bit in (1, 2):
            total = total + exchange(total, axis, bit)

    cot, ids, prob, row_counts, column_counts = small_call(
        functools.partial(teacher_kernel, rows, thin),
        "teacher_prep",
        [
            ((width, BLOCK), jnp.float32, vmem),
            ((top, tokens), jnp.int32, vmem),
            ((top, tokens), jnp.float32, vmem),
            ((PADDED // TABLE_TILE,), jnp.int32, smem),
            ((PADDED // TABLE_TILE * (dp - 1),), jnp.int32, smem),
        ],
        side_near,
        side_far,
        scratch=[pltpu.VMEM((dp, BLOCK, 2 * top), jnp.float32)],
    )
    packed_cot, packed_ids, chunks = small_call(
        functools.partial(lookup_kernel, rows, share),
        "lookup_prep",
        [
            ((dp, columns, BLOCK), jnp.bfloat16, vmem),
            ((dp, 1, BLOCK), jnp.int32, vmem),
            ((1,), jnp.int32, smem),
        ],
        packs,
        cot,
        scratch=[pltpu.VMEM((1, tokens), jnp.float32)],
    )

    scattered = (SIDE, SIDE, thin + 8, BLOCK)
    own_grads, keep, give = pl.pallas_call(
        hidden_grad_kernel,
        in_specs=[smem()] + [vmem()] * 5,
        out_specs=[vmem()] * 3,
        out_shape=(
            pltpu.VMEM((PADDED, BLOCK), jnp.bfloat16),
            shape_of(scattered, jnp.float32),
            shape_of(scattered, jnp.float32),
        ),
        scratch_shapes=[
            pltpu.VMEM((BLOCK, width), jnp.float32),
            pltpu.VMEM((width, BLOCK), jnp.float32),
            pltpu.VMEM((8, BLOCK), jnp.float32),
            pltpu.VMEM((GRAD_TILE, BLOCK), jnp.bfloat16),
            pltpu.VMEM((GRAD_TILE, BLOCK), jnp.bfloat16),
        ],
        compiler_params=pltpu.CompilerParams(vmem_limit_bytes=10 << 20),
        cost_estimate=pl.CostEstimate(
            flops=2 * rows * width * BLOCK,
            bytes_accessed=rows * BLOCK * 6,
            transcendentals=rows * BLOCK,
        ),
        name="hidden_grads",
    )(row_counts, table, own_squashed, total, ids, prob)

    def table_grads(so_far):
        fresh = so_far is None
        started = [] if fresh else [so_far]
        operands = [
            column_counts,
            chunks,
            own_grads,
            side_squashed,
            far_squashed,
            total,
            ids,
            prob,
            packed_cot,
            packed_ids,
            own_columns,
            side_columns,
            far_columns,
        ]
        made = PADDED // 2
        half = (columns, PADDED // 2)
        return pl.pallas_call(
            functools.partial(table_grad_kernel, width, fresh),
            grid=(1 if fresh else 2,),
            in_specs=[smem()] * 2
            + [whole(operand.shape) for operand in operands[2:]]
            + [whole(half) for _ in started],
            out_specs=pl.BlockSpec(half, lambda n: (0, n)),
            out_shape=pltpu.VMEM(half, jnp.bfloat16)
            if fresh
            else shape_of((columns, rows), jnp.bfloat16),
            scratch_shapes=[
                pltpu.VMEM((columns, (dp + 1) * BLOCK), jnp.bfloat16),
                pltpu.VMEM((TABLE_TILE, (dp + 1) * BLOCK), jnp.bfloat16),
                pltpu.VMEM((TABLE_TILE, (dp + 1) * BLOCK), jnp.bfloat16),
            ],
            compiler_params=pltpu.CompilerParams(vmem_limit_bytes=18 << 20),
            cost_estimate=pl.CostEstimate(
                flops=2 * made * columns * (tokens + BLOCK),
                bytes_accessed=rows * columns * 2,
                transcendentals=made * tokens,
            ),
            name="table_grads_start" if fresh else "table_grads_rest",
        )(*operands, *started)

    quarter = (SIDE, thin + 8, BLOCK)
    got, packed_cot, packed_ids = lax.optimization_barrier((swap(give), packed_cot, packed_ids))
    parts = small_call(halve_kernel, "halve", [(quarter, jnp.float32, vmem)] * SIDE, keep, got)
    travelling = [hand_on(part, 1, by) for part, by in zip(parts[1:], OFFSETS[1:])]
    embed_grad = table_grads(None)
    travelling, embed_grad = lax.optimization_barrier((travelling, embed_grad))
    parts = small_call(
        quarter_kernel,
        "quarter",
        [(quarter[1:], jnp.float32, vmem)] * SIDE,
        parts[0],
        *travelling,
    )
    travelling = [hand_on(part, 0, by) for part, by in zip(parts[1:], OFFSETS[1:])]
    embed_grad = table_grads(embed_grad)
    parts = [parts[0]] + travelling

    hidden_grad, divergence = small_call(
        finish_kernel,
        "finish",
        [((thin, BLOCK), jnp.bfloat16, vmem), ((1, HALF), jnp.float32, vmem)],
        total,
        teacher_logits,
        *parts,
    )
    return (hidden_grad.T, embed_grad.T, divergence[0, :share])


def solution(mesh):
    dp, vocab = (mesh.shape[name] for name in ("dp", "vocab"))
    fine = Mesh(mesh.devices.reshape(dp, SIDE, SIDE, vocab // (SIDE * SIDE)), EVERY)
    return jax.shard_map(
        per_device,
        mesh=fine,
        in_specs=(
            P("dp", RING),
            P(RING, None),
            P("dp"),
            P("dp", RING),
            P(EVERY, None),
            P(EVERY, None),
        ),
        out_specs=(P("dp", RING), P(RING, "dp"), P(EVERY)),
        check_vma=False,
    )
```
